128 devices in a mesh: dp: 128 (over y, z, x, core).
Axes of the slice: x: 4, y: 4, z: 4, core: 2. Of those that a mesh axis runs over, the one named last changes fastest.
Arguments:
- query_rows: bfloat16 [16384, 1152], P('dp'), may hold values from -30 to 30
- key_rows: bfloat16 [16384, 1152], P('dp'), may hold values from -30 to 30
- value_rows: bfloat16 [16384, 1152], P('dp'), may hold values from -6 to 6
- residual: bfloat16 [16384, 1152], P('dp'), may hold values from -4 to 4
- token_clip: int32 [16384], P('dp'), may hold values from 0 to 31, never falling along the last dimension, each value on 1 to 897 neighbouring positions
- clip_gate: float32 [32, 1152], replicated, may hold values from -4 to 4
- out_weight: bfloat16 [1152, 1152], replicated, may hold values from -0.1875 to 0.1875
- out_bias: float32 [1152], replicated, may hold values from -3 to 3
- out_grad: bfloat16 [16384, 1152], P('dp'), may hold values from -24 to 24
Outputs:
- block_out: bfloat16 [16384, 1152], P('dp')
- query_grad: bfloat16 [16384, 1152], P('dp')
- key_grad: bfloat16 [16384, 1152], P('dp')
- value_grad: bfloat16 [16384, 1152], P('dp')
- weight_grad: float32 [1152, 1152], P(None, 'dp')
The draws below stay inside these ranges and needn't reach their ends.
Inputs may be any that keep to these rules, and one draw needn't show every extreme that they name: `token_clip`: clip numbers never fall along the rows; each clip has 1 to 897 tokens, and one clip has exactly that many.
All inputs are finite; a program needn't handle non-finite values.
Results may differ from the reference program's by a relative error of at most 0.03.
Values may be sent and summed in bfloat16 or wider, within the bound.
No kernel may reach another device: no remote copies, remote signals or barrier semaphores. Data moves between devices by JAX's collectives and lax.ppermute only.
A program may use at most 128 MiB of HBM per device.

```python
import math
import jax
import jax.numpy as jnp
import numpy as np
from jax import lax

HEADS = 16
HEAD_DIM = 72
D = 1152
TOK_DEV = 128
REACH = 7
CLIPS = 32
TOKENS = 16384
N_DP = 128


def draw_query_rows(key, part):
    own_key = jax.random.fold_in(key, 1)
    return (2.0 * jax.random.truncated_normal(own_key, -4.0, 4.0, (TOKENS, HEADS * HEAD_DIM), jnp.float32)).astype(jnp.bfloat16)


def draw_key_rows(key, part):
    own_key = jax.random.fold_in(key, 2)
    return (2.0 * jax.random.truncated_normal(own_key, -4.0, 4.0, (TOKENS, HEADS * HEAD_DIM), jnp.float32)).astype(jnp.bfloat16)


def raised(result, stream_key, source, target, parts, factor):
    def block_of(position):
        return (jnp.arange(result.shape[position]) // (result.shape[position] // parts)).reshape((-1,) + (1,) * (result.ndim - 1 - position))

    first = jax.random.permutation(stream_key, parts)[block_of(target)]
    far = (block_of(target) + parts // 2) % parts
    return jnp.where((block_of(source) == first) | (block_of(source) == far), factor * result, result)


def block_scale(stream_key, extent, cuts, smallest, top_value):
    loudness = 1.0
    for position, blocks in cuts:
        draws = jax.random.uniform(jax.random.fold_in(jax.random.fold_in(stream_key, 6), position), (blocks,), jnp.float32, smallest / len(cuts), top_value / len(cuts))
        loudness = loudness * jnp.repeat(jnp.exp(draws), extent[position] // blocks).reshape((-1,) + (1,) * (len(extent) - 1 - position))
    return loudness


def length_profile(amount, total, bound, slope):
    portions = [(1 << 20) // math.isqrt(standing ** slope) + 1 for standing in range(2, amount + 1)]
    spare, given = total - bound - (amount - 1), [1] * (amount - 1)
    while spare > 0:
        free = [i for i in range(amount - 1) if given[i] < bound]
        mass, left = sum([portions[i] for i in free]), spare
        for i in free:
            addition = min(bound - given[i], max(1, left * portions[i] // mass), spare)
            given[i] = given[i] + addition
            spare = spare - addition
    return np.array([bound] + given)


def ragged_sizes(key, count, total, bound, slope):
    if count == 2:
        one = jax.random.randint(key, (), max(1, total - bound), min(bound, total - 1) + 1)
        return jnp.stack([one, total - one])
    sizes = jnp.asarray(length_profile(count, total, bound, slope), jnp.int32)
    couples = (count - 1) // 2
    donor, sink = sizes[1:1 + 2 * couples:2], sizes[2:2 + 2 * couples:2]
    room = jnp.minimum(donor - 1, bound - sink)
    moved = jax.random.randint(jax.random.fold_in(key, 1), (couples,), 0, 1 << 20) % (room + 1)
    sizes = sizes.at[1:1 + 2 * couples:2].set(donor - moved).at[2:2 + 2 * couples:2].set(sink + moved)
    return sizes[jax.random.permutation(jax.random.fold_in(key, 2), count)]


def scatter_about(key, dims, scale, limit, shards=(), held_as=jnp.bfloat16):
    values = jax.random.normal(key, dims, jnp.float32) * scale
    if len(shards) > 0:
        values = block_scale(key, dims, shards, -0.22, 0.18) * values
    return jnp.clip(values, min=-limit, max=limit).astype(held_as)


def bell_draw_with(rng, shape, deviation, bound, cuts, heavy, held_as=jnp.bfloat16):
    result = deviation * jax.random.normal(rng, shape, jnp.float32)
    if cuts:
        result = result * block_scale(rng, shape, cuts, -0.22, 0.18)
    return jnp.clip(raised(result, jax.random.fold_in(rng, 3), *heavy), -bound, bound).astype(held_as)


def setup_inputs(seed: int = 0) -> dict:
    streams_of = jax.random.split(jax.random.key(seed), 10)
    query_rows = draw_query_rows(jax.random.fold_in(streams_of[9], 71), 0)
    key_rows = draw_key_rows(jax.random.fold_in(streams_of[9], 71), 0)
    value_rows = scatter_about(streams_of[2], (TOKENS, D), 1.0, 6.0, ((0, 128),))
    residual = scatter_about(streams_of[3], (TOKENS, D), 0.5, 4.0, ((0, 128),))
    token_clip = jnp.searchsorted(jnp.cumsum(ragged_sizes(streams_of[4], CLIPS, TOKENS, REACH * TOK_DEV + 1, 2)), jnp.arange(TOKENS), side="right").astype(jnp.int32)
    clip_gate = scatter_about(streams_of[5], (CLIPS, D), 1.0, 4.0, (), jnp.float32)
    out_weight = scatter_about(streams_of[6], (D, D), D ** -0.5, 0.1875)
    out_bias = scatter_about(streams_of[7], (D,), 0.5, 3.0, (), jnp.float32)
    out_grad = bell_draw_with(streams_of[8], (TOKENS, D), 1.0, 24.0, ((0, 128),), (0, 1, 128, 5.5))
    return dict(query_rows=query_rows, key_rows=key_rows, value_rows=value_rows, residual=residual, token_clip=token_clip, clip_gate=clip_gate, out_weight=out_weight, out_bias=out_bias, out_grad=out_grad)


def head_split(values_in):
    return values_in.reshape(values_in.shape[0], HEADS, HEAD_DIM)

def masked_scores(query_part, key_part, query_tags, key_tags):
    raw_scores = jnp.einsum('qhd,khd->hqk', query_part.astype(jnp.float32), key_part.astype(jnp.float32)) * (1.0 / math.sqrt(HEAD_DIM))
    same_clip = query_tags[:, None] == key_tags[None, :]
    return jnp.where(same_clip[None], raw_scores, -1e+30)

def rounded(values_in):
    return lax.optimization_barrier(values_in.astype(jnp.bfloat16)).astype(jnp.float32)

def reference(query_rows, key_rows, value_rows, residual, token_clip, clip_gate, out_weight, out_bias, out_grad):
    margin = REACH * TOK_DEV
    span_rows = (2 * REACH + 1) * TOK_DEV
    scale_factor = 1.0 / math.sqrt(HEAD_DIM)
    own_tags = token_clip.astype(jnp.int32)
    query_heads = head_split(query_rows)
    key_heads = head_split(key_rows)
    value_heads = head_split(value_rows)

    def padded(values_in):
        return jnp.pad(values_in, ((margin, margin),) + ((0, 0),) * (values_in.ndim - 1))
    tag_pad = jnp.pad(own_tags, (margin, margin), constant_values=-1)
    key_pad = padded(key_heads)
    value_pad = padded(value_heads)
    starts = jnp.arange(N_DP, dtype=jnp.int32) * TOK_DEV

    def forward_block(first_row):
        query_part = lax.dynamic_slice_in_dim(query_heads, first_row, TOK_DEV, 0)
        query_tags = lax.dynamic_slice_in_dim(own_tags, first_row, TOK_DEV, 0)
        key_part = lax.dynamic_slice_in_dim(key_pad, first_row, span_rows, 0)
        value_part = lax.dynamic_slice_in_dim(value_pad, first_row, span_rows, 0)
        key_tags = lax.dynamic_slice_in_dim(tag_pad, first_row, span_rows, 0)
        scores = masked_scores(query_part, key_part, query_tags, key_tags)
        row_max = lax.optimization_barrier(jnp.max(scores, axis=2))
        weights = jnp.exp(scores - row_max[:, :, None])
        totals = lax.optimization_barrier(jnp.sum(weights, axis=2))
        accumulated = jnp.einsum('hqk,khd->qhd', rounded(weights), value_part.astype(jnp.float32))
        return (accumulated / totals.T[:, :, None], (row_max + jnp.log(totals)).T)
    attended, log_sum = lax.map(forward_block, starts)
    mixed = attended.reshape(TOKENS, D).astype(jnp.bfloat16)
    log_sum = log_sum.reshape(TOKENS, HEADS)
    gate_rows = clip_gate[own_tags]
    projected = jnp.dot(mixed, out_weight, preferred_element_type=jnp.float32) + out_bias
    block_out = (residual.astype(jnp.float32) + gate_rows * projected).astype(jnp.bfloat16)
    branch_grad = (out_grad.astype(jnp.float32) * gate_rows).astype(jnp.bfloat16)
    weight_grad = jnp.dot(mixed.T, branch_grad, preferred_element_type=jnp.float32)
    mixed_grad = jnp.dot(branch_grad, out_weight.T, preferred_element_type=jnp.float32).astype(jnp.bfloat16)
    grad_heads = head_split(mixed_grad)
    row_delta = lax.optimization_barrier(jnp.sum(grad_heads.astype(jnp.float32) * head_split(mixed).astype(jnp.float32), axis=2))

    def query_block(first_row):
        query_part = lax.dynamic_slice_in_dim(query_heads, first_row, TOK_DEV, 0)
        query_tags = lax.dynamic_slice_in_dim(own_tags, first_row, TOK_DEV, 0)
        grad_part = lax.dynamic_slice_in_dim(grad_heads, first_row, TOK_DEV, 0).astype(jnp.float32)
        lse_part = lax.dynamic_slice_in_dim(log_sum, first_row, TOK_DEV, 0)
        delta_part = lax.dynamic_slice_in_dim(row_delta, first_row, TOK_DEV, 0)
        key_part = lax.dynamic_slice_in_dim(key_pad, first_row, span_rows, 0)
        value_part = lax.dynamic_slice_in_dim(value_pad, first_row, span_rows, 0)
        key_tags = lax.dynamic_slice_in_dim(tag_pad, first_row, span_rows, 0)
        scores = masked_scores(query_part, key_part, query_tags, key_tags)
        prob_rows = jnp.exp(scores - lse_part.T[:, :, None])
        prob_grad = jnp.einsum('qhd,khd->hqk', grad_part, value_part.astype(jnp.float32))
        score_grad = rounded(prob_rows * (prob_grad - delta_part.T[:, :, None]))
        return jnp.einsum('hqk,khd->qhd', score_grad, key_part.astype(jnp.float32)) * scale_factor
    query_grad = lax.map(query_block, starts).reshape(TOKENS, D).astype(jnp.bfloat16)
    query_pad = padded(query_heads)
    grad_pad = padded(grad_heads)
    lse_pad = padded(log_sum)
    delta_pad = padded(row_delta)

    def key_block(first_row):
        key_part = lax.dynamic_slice_in_dim(key_heads, first_row, TOK_DEV, 0)
        value_part = lax.dynamic_slice_in_dim(value_heads, first_row, TOK_DEV, 0)
        key_tags = lax.dynamic_slice_in_dim(own_tags, first_row, TOK_DEV, 0)
        query_part = lax.dynamic_slice_in_dim(query_pad, first_row, span_rows, 0)
        grad_part = lax.dynamic_slice_in_dim(grad_pad, first_row, span_rows, 0).astype(jnp.float32)
        lse_part = lax.dynamic_slice_in_dim(lse_pad, first_row, span_rows, 0)
        delta_part = lax.dynamic_slice_in_dim(delta_pad, first_row, span_rows, 0)
        query_tags = lax.dynamic_slice_in_dim(tag_pad, first_row, span_rows, 0)
        scores = masked_scores(query_part, key_part, query_tags, key_tags)
        prob_rows = jnp.exp(scores - lse_part.T[:, :, None])
        value_acc = jnp.einsum('hqk,qhd->khd', rounded(prob_rows), grad_part)
        prob_grad = jnp.einsum('qhd,khd->hqk', grad_part, value_part.astype(jnp.float32))
        score_grad = rounded(prob_rows * (prob_grad - delta_part.T[:, :, None]))
        key_acc = jnp.einsum('hqk,qhd->khd', score_grad, query_part.astype(jnp.float32)) * scale_factor
        return (key_acc, value_acc)
    key_grad, value_grad = lax.map(key_block, starts)
    key_grad = key_grad.reshape(TOKENS, D).astype(jnp.bfloat16)
    value_grad = value_grad.reshape(TOKENS, D).astype(jnp.bfloat16)
    return (block_out, query_grad, key_grad, value_grad, weight_grad)
```

```python
import math

import jax
import jax.numpy as jnp
from jax import lax
from jax.experimental import pallas as pl
from jax.experimental.pallas import tpu as pltpu
from jax.sharding import Mesh, PartitionSpec as P

HEADS = 16
HEAD_DIM = 72
WIDTH = HEADS * HEAD_DIM
TOK = 128
GROUPS = 8
EDGE = 4
SPAN = HEADS + 2 * EDGE
TILE = 256
TILES = SPAN * TOK // TILE
CHUNK = 4 * HEAD_DIM + 16
CLIPS = 32
SCALE = 1.0 / math.sqrt(HEAD_DIM)
SCALE2 = SCALE / math.log(2.0)
FAR = -1e30
BF = jnp.bfloat16
F32 = jnp.float32
VMEM_BYTES = 56 * 1024 * 1024

WHOLE = pl.BlockSpec(memory_space=pltpu.VMEM)


def params():
    return pltpu.CompilerParams(vmem_limit_bytes=VMEM_BYTES)


def mm(left, right):
    return jnp.dot(left, right, preferred_element_type=F32)


def pack_body(query, key, value, out_grad, tags, gate, weight, bg_ref, chunk_ref):
    clip = tags[...]
    onehot = (lax.broadcasted_iota(jnp.int32, (CLIPS, TOK), 0) + 1 == clip).astype(F32)
    gate_rows = lax.dot_general(
        onehot, gate[...], (((0,), (0,)), ((), ())), precision=lax.Precision.HIGHEST, preferred_element_type=F32
    )
    branch = (out_grad[...].astype(F32) * gate_rows).astype(BF)
    bg_ref[...] = branch
    grad_t = lax.dot_general(weight[...], branch, (((1,), (1,)), ((), ())), preferred_element_type=F32)
    query_t = query[...].astype(F32).T
    key_t = key[...].astype(F32).T
    value_t = value[...].astype(F32).T
    tag_rows = jnp.broadcast_to(clip.astype(F32), (16, TOK))
    for head in range(HEADS):
        rows = slice(head * HEAD_DIM, (head + 1) * HEAD_DIM)
        whole = jnp.concatenate([query_t[rows], key_t[rows], value_t[rows], grad_t[rows], tag_rows], 0)
        chunk_ref[head] = whole.astype(BF)


def pack(query, key, value, out_grad, tags, gate, weight):
    return pl.pallas_call(
        pack_body,
        out_shape=(jax.ShapeDtypeStruct((TOK, WIDTH), BF), jax.ShapeDtypeStruct((HEADS, CHUNK, TOK), BF)),
        in_specs=[WHOLE] * 7,
        out_specs=(WHOLE, WHOLE),
        compiler_params=params(),
        name="pack",
    )(query, key, value, out_grad, tags, gate, weight)


def window_block(block, left, main, right):
    if block < EDGE:
        return left[block]
    if block < EDGE + HEADS:
        return main[block - EDGE]
    return right[block - EDGE - HEADS]


def clip_row(block, left, main, right):
    row = window_block(block, left, main, right)[4 * HEAD_DIM :].astype(F32)[0:1]
    if block >= EDGE + HEADS:
        row = jnp.where(row == 0.0, 100.0, row)
    return row


def owned_clips(clips):
    ids = lax.broadcasted_iota(jnp.int32, (CLIPS, TOK), 0).astype(F32) + 1.0
    middle = jnp.zeros((CLIPS, TOK), F32)
    for row in clips:
        middle += (row < ids).astype(F32) + (row <= ids).astype(F32)
    middle = jnp.sum(middle, axis=1, keepdims=True)
    inside = (middle >= 2.0 * EDGE * TOK) & (middle < 2.0 * (EDGE + HEADS) * TOK)
    held = jnp.where(inside, 1.0, 0.0)
    return [jnp.sum(jnp.where(ids == row, held, 0.0), axis=0, keepdims=True) for row in clips]


def tile_bounds(clips, owned, low_ref, high_ref):
    per = TILE // TOK
    for tile in range(TILES):
        low, high = None, None
        for block in range(tile * per, (tile + 1) * per):
            least = jnp.where(owned[block] > 0.0, clips[block], 1000.0)
            most = jnp.where(owned[block] > 0.0, clips[block], -1.0)
            low = least if low is None else jnp.minimum(low, least)
            high = most if high is None else jnp.maximum(high, most)
        low_ref[tile] = jnp.min(low).astype(jnp.int32)
        high_ref[tile] = jnp.max(high).astype(jnp.int32)


def key_range(tile, low_ref, high_ref):
    low, high = low_ref[tile], high_ref[tile]
    first, count = jnp.int32(0), jnp.int32(0)
    for other in range(TILES):
        meets = (high_ref[other] >= low) & (low_ref[other] <= high)
        before = high_ref[other] < low
        ahead = (high_ref[other] < 0) & (other < tile)
        first = first + jnp.where(before & (high_ref[other] >= 0), 1, 0) + jnp.where(ahead, 1, 0)
        count = count + jnp.where(meets, 1, 0)
    count = jnp.where(high < 0, 0, count)
    return first, first + count


def spread(piece, extra):
    rows = [piece] + extra
    have = sum(part.shape[0] for part in rows)
    if have < TOK:
        rows.append(jnp.zeros((TOK - have, TOK), F32))
    return jnp.concatenate(rows, 0)


def masks(row):
    ids = lax.broadcasted_iota(jnp.int32, (CLIPS, TOK), 0).astype(F32) + 1.0
    same = ids == row
    return jnp.where(same, 1.0, 0.0), jnp.where(same, 0.0, FAR)


def place(block):
    per = TILE // TOK
    return block // per, slice((block % per) * TOK, (block % per + 1) * TOK)


def forward_body(left, main, right, mixed_ref, stat_ref, query_t, key_n, value_t, out_t, low_ref, high_ref):
    clips = [clip_row(block, left, main, right) for block in range(SPAN)]
    owned = owned_clips(clips)
    tile_bounds(clips, owned, low_ref, high_ref)
    ones = jnp.ones((8, TOK), F32)
    for block in range(SPAN):
        whole = window_block(block, left, main, right).astype(F32)
        tile, part = place(block)
        near, far = masks(clips[block])
        query_t[tile, :, part] = spread(whole[0:72], [near]).astype(BF)
        key_n[tile, part, :] = spread(whole[72:144], [far]).T.astype(BF)
        value_t[tile, :, part] = spread(whole[144:216], [ones]).astype(BF)

    def query_step(tile, carry):
        first, last = key_range(tile, low_ref, high_ref)
        queries = query_t[tile]
        out_t[...] = jnp.zeros_like(out_t)

        def key_step(other, top):
            scores = mm(key_n[other], queries)
            new_top = jnp.maximum(top, jnp.max(scores, axis=0, keepdims=True))
            fade = jnp.exp2((top - new_top) * SCALE2)
            weights = jnp.exp2((scores - new_top) * SCALE2).astype(BF)
            out_t[...] = out_t[...] * fade + mm(value_t[other, 0:80, :], weights)
            return new_top

        top = lax.fori_loop(first, last, key_step, jnp.full((1, TILE), 2.0 * FAR, F32))
        sums = out_t[72:73, :]
        held = sums > 0.0
        sums = jnp.where(held, sums, 1.0)
        mixed = (out_t[0:72, :] / sums).astype(BF)
        log_sum = top * SCALE2 + jnp.log2(sums)
        for part in range(TILE // TOK):
            cols = slice(part * TOK, (part + 1) * TOK)
            block = tile * (TILE // TOK) + part
            mixed_ref[block] = mixed[:, cols]
            stat_ref[block] = jnp.broadcast_to(log_sum[:, cols], (8, TOK))
        return carry

    lax.fori_loop(0, TILES, query_step, 0)
    for block in range(SPAN):
        mixed_ref[block] = jnp.where(owned[block] > 0.0, mixed_ref[block].astype(F32), 0.0).astype(BF)


def forward(left, main, right):
    return pl.pallas_call(
        forward_body,
        out_shape=(
            jax.ShapeDtypeStruct((SPAN, HEAD_DIM, TOK), BF),
            jax.ShapeDtypeStruct((SPAN, 8, TOK), F32),
        ),
        in_specs=[WHOLE] * 3,
        out_specs=(WHOLE, WHOLE),
        scratch_shapes=[
            pltpu.VMEM((TILES, TOK, TILE), BF),
            pltpu.VMEM((TILES, TILE, TOK), BF),
            pltpu.VMEM((TILES, TOK, TILE), BF),
            pltpu.VMEM((80, TILE), F32),
            pltpu.SMEM((TILES,), jnp.int32),
            pltpu.SMEM((TILES,), jnp.int32),
        ],
        compiler_params=params(),
        name="forward",
    )(left, main, right)


def backward_body(
    left, main, right, mixed, stat, out_ref,
    query_t, query_n, key_t, key_n, value_n, grad_t, grad_n, stats, dq, dk, dv, low_ref, high_ref,
):
    clips = [clip_row(block, left, main, right) for block in range(SPAN)]
    owned = owned_clips(clips)
    tile_bounds(clips, owned, low_ref, high_ref)
    for block in range(SPAN):
        whole = window_block(block, left, main, right).astype(F32)
        tile, part = place(block)
        near, far = masks(clips[block])
        asked = spread(whole[0:72], [near])
        query_t[tile, :, part] = asked.astype(BF)
        query_n[tile, part, :] = asked.T.astype(BF)
        held = spread(whole[72:144], [far])
        key_t[tile, :, part] = held.astype(BF)
        key_n[tile, part, :] = held.T.astype(BF)
        value_n[tile, part, :] = spread(whole[144:216], []).T.astype(BF)
        grad = spread(whole[216:288], [])
        grad_t[tile, :, part] = grad.astype(BF)
        grad_n[tile, part, :] = grad.T.astype(BF)
        delta = jnp.sum(whole[216:288] * mixed[block].astype(F32), axis=0, keepdims=True)
        stats[tile, :, part] = jnp.concatenate([stat[block][0:1], delta, jnp.zeros((6, TOK), F32)], 0)
    dk[...] = jnp.zeros_like(dk)
    dv[...] = jnp.zeros_like(dv)

    def query_step(tile, carry):
        first, last = key_range(tile, low_ref, high_ref)
        log_sum = stats[tile, 0:1, :]
        delta = stats[tile, 1:2, :]
        dq[tile] = jnp.zeros((80, TILE), F32)

        def key_step(other, inner):
            scores = mm(key_n[other], query_t[tile])
            prob = jnp.exp2(scores * SCALE2 - log_sum)
            pull = mm(value_n[other], grad_t[tile])
            dv[other] += mm(prob.astype(BF), grad_n[tile])
            score_grad = (prob * (pull - delta)).astype(BF)
            dk[other] += mm(score_grad, query_n[tile])
            dq[tile] += mm(key_t[other, 0:80, :], score_grad)
            return inner

        return lax.fori_loop(first, last, key_step, carry)

    lax.fori_loop(0, TILES, query_step, 0)
    for block in range(SPAN):
        tile, part = place(block)
        held = owned[block] > 0.0
        pieces = [
            dq[tile, 0:72, part] * SCALE,
            dk[tile, part, :].T[0:72] * SCALE,
            dv[tile, part, :].T[0:72],
        ]
        out_ref[block] = jnp.where(held, jnp.concatenate(pieces, 0), 0.0).astype(BF)


def backward(left, main, right, mixed, stat):
    t_form = pltpu.VMEM((TILES, TOK, TILE), BF)
    n_form = pltpu.VMEM((TILES, TILE, TOK), BF)
    return pl.pallas_call(
        backward_body,
        out_shape=jax.ShapeDtypeStruct((SPAN, 3 * HEAD_DIM, TOK), BF),
        in_specs=[WHOLE] * 5,
        out_specs=WHOLE,
        scratch_shapes=[
            t_form, n_form, t_form, n_form, n_form, t_form, n_form,
            pltpu.VMEM((TILES, 8, TILE), F32),
            pltpu.VMEM((TILES, 80, TILE), F32),
            pltpu.VMEM((TILES, TILE, TOK), F32),
            pltpu.VMEM((TILES, TILE, TOK), F32),
            pltpu.SMEM((TILES,), jnp.int32),
            pltpu.SMEM((TILES,), jnp.int32),
        ],
        compiler_params=params(),
        name="backward",
    )(left, main, right, mixed, stat)


def unpack_body(packed, residual, tags, gate, weight, bias, out_ref, dq_ref, dk_ref, dv_ref):
    clip = tags[...]
    onehot = (lax.broadcasted_iota(jnp.int32, (CLIPS, TOK), 0) + 1 == clip).astype(F32)
    gate_rows = lax.dot_general(
        onehot, gate[...], (((0,), (0,)), ((), ())), precision=lax.Precision.HIGHEST, preferred_element_type=F32
    )
    whole = [packed[head].astype(F32) for head in range(HEADS)]
    mixed = jnp.concatenate([part[0:72] for part in whole], 0).T.astype(BF)
    projected = mm(mixed, weight[...]) + bias[...]
    out_ref[...] = (residual[...].astype(F32) + gate_rows * projected).astype(BF)
    for ref, start in ((dq_ref, 72), (dk_ref, 144), (dv_ref, 216)):
        ref[...] = jnp.concatenate([part[start : start + 72] for part in whole], 0).T.astype(BF)


def unpack(packed, residual, tags, gate, weight, bias):
    shape = jax.ShapeDtypeStruct((TOK, WIDTH), BF)
    return pl.pallas_call(
        unpack_body,
        out_shape=(shape,) * 4,
        in_specs=[WHOLE] * 6,
        out_specs=(WHOLE,) * 4,
        compiler_params=params(),
        name="unpack",
    )(packed, residual, tags, gate, weight, bias)


def from_neighbour(values, by):
    total = GROUPS * HEADS
    pairs = [(i, i + by * HEADS) for i in range(total) if 0 <= i + by * HEADS < total]
    return lax.ppermute(values, ("g", "r"), pairs)


def shards(query, key, value, residual, token_clip, gate, weight, bias, out_grad):
    tags = (token_clip + 1).reshape(1, TOK)
    branch, chunk = pack(query, key, value, out_grad, tags, gate, weight)
    gathered = lax.all_gather(branch, "r", axis=0, tiled=False)
    main = lax.all_to_all(chunk, "r", 0, 0, tiled=True)
    left = from_neighbour(main[HEADS - EDGE :], 1)
    right = from_neighbour(main[:EDGE], -1)
    mixed_window, stat = forward(left, main, right)
    mixed_from_left = from_neighbour(mixed_window[EDGE + HEADS :], 1)
    mixed_from_right = from_neighbour(mixed_window[:EDGE], -1)
    grads_window = backward(left, main, right, mixed_window, stat)
    grads_from_left = from_neighbour(grads_window[EDGE + HEADS :], 1)
    grads_from_right = from_neighbour(grads_window[:EDGE], -1)

    def joined(window, from_left, from_right):
        middle = jnp.zeros((HEADS - 2 * EDGE,) + from_left.shape[1:], BF)
        return window[EDGE : EDGE + HEADS] + jnp.concatenate([from_left, middle, from_right], 0)

    mixed = joined(mixed_window, mixed_from_left, mixed_from_right)
    grads = joined(grads_window, grads_from_left, grads_from_right)
    packed = lax.all_to_all(jnp.concatenate([mixed, grads], 1), "r", 0, 0, tiled=True)
    block_out, dq, dk, dv = unpack(packed, residual, tags, gate, weight, bias.reshape(1, WIDTH))

    term = jnp.einsum("bct,btd->cd", mixed, gathered, preferred_element_type=F32)
    share = WIDTH // GROUPS
    term = term.reshape(HEAD_DIM, GROUPS, share).transpose(1, 0, 2)
    term = jnp.sum(lax.all_to_all(term, "g", 0, 0, tiled=True), 0)
    final = share // HEADS
    term = term.reshape(HEAD_DIM, HEADS, final).transpose(1, 0, 2)
    weight_grad = lax.all_to_all(term, "r", 0, 0, tiled=True).reshape(WIDTH, final)
    return (block_out, dq, dk, dv, weight_grad)


def solution(mesh):
    split = Mesh(mesh.devices.reshape(GROUPS, HEADS), ("g", "r"))
    both = ("g", "r")
    in_specs = (
        P(both, None), P(both, None), P(both, None), P(both, None), P(both), P(), P(), P(), P(both, None),
    )
    out_specs = (P(both, None),) * 4 + (P(None, both),)
    return jax.shard_map(shards, mesh=split, in_specs=in_specs, out_specs=out_specs, check_vma=False)
```

```python
import math

import jax
import jax.numpy as jnp
from jax import lax
from jax.experimental import pallas as pl
from jax.experimental.pallas import tpu as pltpu
from jax.sharding import Mesh, PartitionSpec as P

HEADS = 16
HEAD_DIM = 72
WIDTH = HEADS * HEAD_DIM
TOK = 128
GROUPS = 8
EDGE = 7
SPAN = HEADS + 2 * EDGE
TILE = 256
TILES = HEADS * TOK // TILE
PART = TILE // TOK
STEP = 4
ROOM = SPAN + STEP - 1
CHUNKS = 5
SHARED = 2 * HEAD_DIM + 16
CHUNK = SHARED + 2 * HEAD_DIM
GRADS = 4 * HEAD_DIM
SHARE = WIDTH // GROUPS
FINAL = SHARE // HEADS
CLIPS = 32
SCALE = 1.0 / math.sqrt(HEAD_DIM)
SCALE2 = SCALE / math.log(2.0)
FAR = -1e30
BF = jnp.bfloat16
F32 = jnp.float32
VMEM_BYTES = 56 * 1024 * 1024

WHOLE = pl.BlockSpec(memory_space=pltpu.VMEM)


def params():
    return pltpu.CompilerParams(vmem_limit_bytes=VMEM_BYTES)


def mm(left, right):
    return jnp.dot(left, right, preferred_element_type=F32)


def pack_body(query, key, value, out_grad, tags, gate, weight, bg_ref, chunk_ref):
    clip = tags[...]
    onehot = (lax.broadcasted_iota(jnp.int32, (CLIPS, TOK), 0) + 1 == clip).astype(F32)
    gate_rows = lax.dot_general(
        onehot, gate[...], (((0,), (0,)), ((), ())), precision=lax.Precision.HIGHEST, preferred_element_type=F32
    )
    branch = (out_grad[...].astype(F32) * gate_rows).astype(BF)
    bg_ref[...] = branch
    grad_t = lax.dot_general(weight[...], branch, (((1,), (1,)), ((), ())), preferred_element_type=F32)
    query_t = query[...].astype(F32).T
    key_t = key[...].astype(F32).T
    value_t = value[...].astype(F32).T
    tag_rows = jnp.broadcast_to(clip.astype(F32), (16, TOK))
    for head in range(HEADS):
        rows = slice(head * HEAD_DIM, (head + 1) * HEAD_DIM)
        whole = jnp.concatenate([key_t[rows], value_t[rows], tag_rows, query_t[rows], grad_t[rows]], 0)
        chunk_ref[head] = whole.astype(BF)


def pack(query, key, value, out_grad, tags, gate, weight):
    return pl.pallas_call(
        pack_body,
        out_shape=(jax.ShapeDtypeStruct((TOK, WIDTH), BF), jax.ShapeDtypeStruct((HEADS, CHUNK, TOK), BF)),
        in_specs=[WHOLE] * 7,
        out_specs=(WHOLE, WHOLE),
        compiler_params=params(),
        name="pack",
    )(query, key, value, out_grad, tags, gate, weight)


def filled(piece, extra):
    rows = [piece] + extra
    have = sum(part.shape[0] for part in rows)
    if have < TOK:
        rows.append(jnp.zeros((TOK - have, TOK), F32))
    return jnp.concatenate(rows, 0)


def lay_out_keys(block, left, main, right, key_n, key_t, value_n, value_t):
    if block < EDGE:
        whole = left[block]
    elif block < EDGE + HEADS:
        whole = main[block - EDGE, 0:SHARED]
    else:
        whole = right[block - EDGE - HEADS]
    whole = whole.astype(F32)
    clip = whole[2 * HEAD_DIM : 2 * HEAD_DIM + 1]
    ids = lax.broadcasted_iota(jnp.int32, (CLIPS, TOK), 0).astype(F32) + 1.0
    rows = slice(block * TOK, (block + 1) * TOK)
    held = filled(whole[0:HEAD_DIM], [jnp.where(ids == clip, 0.0, FAR)])
    key_n[rows, :] = held.T.astype(BF)
    key_t[block] = held[0:80].astype(BF)
    held = filled(whole[HEAD_DIM : 2 * HEAD_DIM], [jnp.ones((8, TOK), F32)])
    value_n[rows, :] = held.T.astype(BF)
    value_t[block] = held[0:80].astype(BF)
    return clip


def lay_out_queries(block, main, clip, query_t, query_n, grad_t, grad_n):
    whole = main[block, SHARED:].astype(F32)
    ids = lax.broadcasted_iota(jnp.int32, (CLIPS, TOK), 0).astype(F32) + 1.0
    tile, cols = block // PART, slice((block % PART) * TOK, (block % PART + 1) * TOK)
    held = filled(whole[0:HEAD_DIM], [jnp.where(ids == clip, 1.0, 0.0)])
    query_t[tile, :, cols] = held.astype(BF)
    query_n[tile, cols, :] = held.T.astype(BF)
    held = filled(whole[HEAD_DIM:], [])
    grad_t[tile, :, cols] = held.astype(BF)
    grad_n[tile, cols, :] = held.T.astype(BF)


def key_ranges(clips, first_ref, count_ref):
    clips = [jnp.where(row == 0.0, 100.0, row) if at >= EDGE + HEADS else row for at, row in enumerate(clips)]
    clips = jnp.concatenate(clips + [jnp.full((32 - SPAN, TOK), 100.0, F32)], 0)
    least = jnp.min(clips, axis=1, keepdims=True)
    most = jnp.max(clips, axis=1, keepdims=True)
    for tile in range(TILES):
        start = EDGE + tile * PART
        low, high = least[start : start + 1], most[start + PART - 1 : start + PART]
        first = jnp.sum(jnp.where(most < low, 1.0, 0.0)).astype(jnp.int32)
        end = jnp.sum(jnp.where(least <= high, 1.0, 0.0)).astype(jnp.int32)
        first_ref[tile] = first
        count_ref[tile] = (end - first + STEP - 1) // STEP


def attend_body(
    left, main, right, own_ref, back_ref, ahead_ref,
    key_n, key_t, value_n, value_t, query_t, query_n, grad_t, grad_n, held, dk, dv, first_ref, count_ref,
):
    clips = [lay_out_keys(block, left, main, right, key_n, key_t, value_n, value_t) for block in range(SPAN)]
    for block in range(HEADS):
        lay_out_queries(block, main, clips[EDGE + block], query_t, query_n, grad_t, grad_n)
    rows = slice(SPAN * TOK, ROOM * TOK)
    lane = lax.broadcasted_iota(jnp.int32, ((ROOM - SPAN) * TOK, TOK), 1)
    key_n[rows, :] = jnp.where((lane >= HEAD_DIM) & (lane < HEAD_DIM + CLIPS), FAR, 0.0).astype(BF)
    value_n[rows, :] = jnp.zeros(((ROOM - SPAN) * TOK, TOK), BF)
    for block in range(SPAN, ROOM):
        key_t[block] = jnp.zeros((80, TOK), BF)
        value_t[block] = jnp.zeros((80, TOK), BF)
    key_ranges(clips, first_ref, count_ref)
    dk[...] = jnp.zeros_like(dk)
    dv[...] = jnp.zeros_like(dv)

    def side_by_side(ref, start):
        return jnp.concatenate([ref[start + at] for at in range(STEP)], 1)

    def query_step(tile, carry):
        first, count = first_ref[tile], count_ref[tile]

        def blocks(step):
            start = first + step * STEP
            return start, pl.ds(pl.multiple_of(start * TOK, TOK), STEP * TOK)

        def score_step(step, top):
            scores = mm(key_n[blocks(step)[1], :], query_t[tile])
            held[step] = scores
            return jnp.maximum(top, jnp.max(scores, axis=0, keepdims=True))

        top = lax.fori_loop(0, count, score_step, jnp.full((1, TILE), 2.0 * FAR, F32))

        def value_step(step, total):
            weights = jnp.exp2((held[step] - top) * SCALE2)
            held[step] = weights
            return total + mm(side_by_side(value_t, blocks(step)[0]), weights.astype(BF))

        total = lax.fori_loop(0, count, value_step, jnp.zeros((80, TILE), F32))
        inverse = 1.0 / total[HEAD_DIM : HEAD_DIM + 1]
        mixed = (total[0:HEAD_DIM] * inverse).astype(BF)
        grad = grad_t[tile]
        delta = jnp.sum(mixed.astype(F32) * grad[0:HEAD_DIM].astype(F32), axis=0, keepdims=True)

        def grad_step(step, total):
            start, rows = blocks(step)
            prob = held[step] * inverse
            pull = mm(value_n[rows, :], grad)
            dv[rows, :] += mm(prob.astype(BF), grad_n[tile])
            score_grad = (prob * (pull - delta)).astype(BF)
            dk[rows, :] += mm(score_grad, query_n[tile])
            return total + mm(side_by_side(key_t, start), score_grad)

        total = lax.fori_loop(0, count, grad_step, jnp.zeros((80, TILE), F32))
        pair = jnp.concatenate([mixed.astype(F32), total[0:HEAD_DIM] * SCALE], 0).astype(BF)
        for part in range(PART):
            own_ref[tile * PART + part, 0 : 2 * HEAD_DIM] = pair[:, part * TOK : (part + 1) * TOK]
        return carry

    lax.fori_loop(0, TILES, query_step, 0)
    for block in range(SPAN):
        rows = slice(block * TOK, (block + 1) * TOK)
        pair = jnp.concatenate([dk[rows, :].T[0:HEAD_DIM] * SCALE, dv[rows, :].T[0:HEAD_DIM]], 0).astype(BF)
        if block < EDGE:
            back_ref[block] = pair
        elif block < EDGE + HEADS:
            own_ref[block - EDGE, 2 * HEAD_DIM :] = pair
        else:
            ahead_ref[block - EDGE - HEADS] = pair


def attend(left, main, right):
    halo = jax.ShapeDtypeStruct((EDGE, 2 * HEAD_DIM, TOK), BF)
    row_form = pltpu.VMEM((ROOM * TOK, TOK), BF)
    column_form = pltpu.VMEM((ROOM, 80, TOK), BF)
    return pl.pallas_call(
        attend_body,
        out_shape=(jax.ShapeDtypeStruct((HEADS, GRADS, TOK), BF), halo, halo),
        in_specs=[WHOLE] * 3,
        out_specs=(WHOLE,) * 3,
        scratch_shapes=[
            row_form, column_form, row_form, column_form,
            pltpu.VMEM((TILES, TOK, TILE), BF), pltpu.VMEM((TILES, TILE, TOK), BF),
            pltpu.VMEM((TILES, TOK, TILE), BF), pltpu.VMEM((TILES, TILE, TOK), BF),
            pltpu.VMEM((CHUNKS, STEP * TOK, TILE), F32),
            pltpu.VMEM((ROOM * TOK, TOK), F32),
            pltpu.VMEM((ROOM * TOK, TOK), F32),
            pltpu.SMEM((TILES,), jnp.int32),
            pltpu.SMEM((TILES,), jnp.int32),
        ],
        compiler_params=params(),
        name="attend",
    )(left, main, right)


def weight_term_body(own, branch, out_ref, total):
    step = pl.program_id(0)
    mixed = jnp.concatenate([own[part, 0:80] for part in range(PART)], 1)

    @pl.when(step == 0)
    def _():
        total[...] = jnp.zeros_like(total)

    total[...] += mm(mixed, branch[...].reshape(TILE, WIDTH))

    @pl.when(step == TILES - 1)
    def _():
        whole = jnp.concatenate([total[0:HEAD_DIM], jnp.zeros((TOK - HEAD_DIM, WIDTH), F32)], 0)
        out_ref[...] = whole.T.astype(BF).reshape(GROUPS, SHARE, TOK)


def weight_term(own, branch):
    return pl.pallas_call(
        weight_term_body,
        grid=(TILES,),
        out_shape=jax.ShapeDtypeStruct((GROUPS, SHARE, TOK), BF),
        in_specs=[
            pl.BlockSpec((PART, GRADS, TOK), lambda i: (i, 0, 0)),
            pl.BlockSpec((PART, TOK, WIDTH), lambda i: (i, 0, 0)),
        ],
        out_specs=pl.BlockSpec((GROUPS, SHARE, TOK), lambda i: (0, 0, 0)),
        scratch_shapes=[pltpu.VMEM((80, WIDTH), F32)],
        compiler_params=params(),
        name="weight_term",
    )(own, branch)


def join_body(own, from_left, from_right, terms, out_ref, total):
    total[0:SHARE] = sum(terms[group].astype(F32) for group in range(GROUPS))
    total[SHARE:] = jnp.zeros((8, TOK), F32)
    for block in range(HEADS):
        whole = own[block].astype(F32)
        if block < EDGE or block >= HEADS - EDGE:
            other = from_left[block] if block < EDGE else from_right[block - HEADS + EDGE]
            pair = whole[2 * HEAD_DIM :] + other.astype(F32)
            whole = jnp.concatenate([whole[0 : 2 * HEAD_DIM], pair], 0)
        tail = total[block * FINAL : block * FINAL + 16, :]
        out_ref[block] = jnp.concatenate([whole, tail], 0).astype(BF)


def join(own, from_left, from_right, terms):
    return pl.pallas_call(
        join_body,
        out_shape=jax.ShapeDtypeStruct((HEADS, GRADS + 16, TOK), BF),
        in_specs=[WHOLE] * 4,
        out_specs=WHOLE,
        scratch_shapes=[pltpu.VMEM((SHARE + 8, TOK), F32)],
        compiler_params=params(),
        name="join",
    )(own, from_left, from_right, terms)


def unpack_body(packed, residual, tags, gate, weight, bias, out_ref, dq_ref, dk_ref, dv_ref, dw_ref):
    clip = tags[...]
    onehot = (lax.broadcasted_iota(jnp.int32, (CLIPS, TOK), 0) + 1 == clip).astype(F32)
    gate_rows = lax.dot_general(
        onehot, gate[...], (((0,), (0,)), ((), ())), precision=lax.Precision.HIGHEST, preferred_element_type=F32
    )
    whole = [packed[head].astype(F32) for head in range(HEADS)]
    mixed = jnp.concatenate([part[0:72] for part in whole], 0).T.astype(BF)
    projected = mm(mixed, weight[...]) + bias[...]
    out_ref[...] = (residual[...].astype(F32) + gate_rows * projected).astype(BF)
    for ref, start in ((dq_ref, 72), (dk_ref, 144), (dv_ref, 216)):
        ref[...] = jnp.concatenate([part[start : start + 72] for part in whole], 0).T.astype(BF)
    dw_ref[...] = jnp.concatenate([part[GRADS:].T[0:72] for part in whole], 0)[:, 0:FINAL]


def unpack(packed, residual, tags, gate, weight, bias):
    shape = jax.ShapeDtypeStruct((TOK, WIDTH), BF)
    return pl.pallas_call(
        unpack_body,
        out_shape=(shape,) * 4 + (jax.ShapeDtypeStruct((WIDTH, FINAL), F32),),
        in_specs=[WHOLE] * 6,
        out_specs=(WHOLE,) * 5,
        compiler_params=params(),
        name="unpack",
    )(packed, residual, tags, gate, weight, bias)


def from_neighbour(values, by):
    total = GROUPS * HEADS
    pairs = [(i, i + by * HEADS) for i in range(total) if 0 <= i + by * HEADS < total]
    return lax.ppermute(values, ("g", "r"), pairs)


def shards(query, key, value, residual, token_clip, gate, weight, bias, out_grad):
    tags = (token_clip + 1).reshape(1, TOK)
    branch, chunk = pack(query, key, value, out_grad, tags, gate, weight)
    main = lax.all_to_all(chunk, "r", 0, 0, tiled=True)
    left = from_neighbour(main[HEADS - EDGE :, 0:SHARED], 1)
    right = from_neighbour(main[:EDGE, 0:SHARED], -1)
    left, right, branch = lax.optimization_barrier((left, right, branch))
    gathered = lax.all_gather(branch, "r", axis=0, tiled=False)
    own, back, ahead = attend(left, main, right)
    from_left = from_neighbour(ahead, 1)
    from_right = from_neighbour(back, -1)
    terms = lax.all_to_all(weight_term(own, gathered), "g", 0, 0, tiled=True)
    packed = lax.all_to_all(join(own, from_left, from_right, terms), "r", 0, 0, tiled=True)
    return unpack(packed, residual, tags, gate, weight, bias.reshape(1, WIDTH))


def solution(mesh):
    split = Mesh(mesh.devices.reshape(GROUPS, HEADS), ("g", "r"))
    both = ("g", "r")
    in_specs = (
        P(both, None), P(both, None), P(both, None), P(both, None), P(both), P(), P(), P(), P(both, None),
    )
    out_specs = (P(both, None),) * 4 + (P(None, both),)
    return jax.shard_map(shards, mesh=split, in_specs=in_specs, out_specs=out_specs, check_vma=False)
```

```python
import math

import jax
import jax.numpy as jnp
from jax import lax
from jax.experimental import pallas as pl
from jax.experimental.pallas import tpu as pltpu
from jax.sharding import Mesh, PartitionSpec as P

HEADS = 16
HEAD_DIM = 72
WIDTH = HEADS * HEAD_DIM
TOK = 128
GROUPS = 8
EDGE = 7
SPAN = HEADS + 2 * EDGE
TILE = 256
TILES = HEADS * TOK // TILE
PART = TILE // TOK
STEP = 4
ROOM = SPAN + STEP - 1
CHUNKS = 5
SHARED = 2 * HEAD_DIM + 16
PAIR = 2 * HEAD_DIM
SHARE = WIDTH // GROUPS
FINAL = SHARE // HEADS
CLIPS = 32
SCALE = 1.0 / math.sqrt(HEAD_DIM)
SCALE2 = SCALE / math.log(2.0)
FAR = -1e30
BF = jnp.bfloat16
F32 = jnp.float32
VMEM_BYTES = 56 * 1024 * 1024

WHOLE = pl.BlockSpec(memory_space=pltpu.VMEM)


def params():
    return pltpu.CompilerParams(vmem_limit_bytes=VMEM_BYTES)


def cost(micros):
    return pl.CostEstimate(flops=int(micros * 4e8), bytes_accessed=int(micros * 2e6), transcendentals=0)


def mm(left, right):
    return jnp.dot(left, right, preferred_element_type=F32)


def clip_onehot(tags):
    ids = lax.broadcasted_iota(jnp.int32, (CLIPS, TOK), 0)
    return (ids == tags[...].reshape(1, TOK)).astype(F32)


def pack_keys_body(key, value, tags, out_ref):
    key_t = key[...].astype(F32).T
    value_t = value[...].astype(F32).T
    tag_rows = jnp.broadcast_to(tags[...].reshape(1, TOK).astype(F32) + 1.0, (16, TOK))
    for head in range(HEADS):
        rows = slice(head * HEAD_DIM, (head + 1) * HEAD_DIM)
        out_ref[head] = jnp.concatenate([key_t[rows], value_t[rows], tag_rows], 0).astype(BF)


def pack_keys(key, value, tags):
    return pl.pallas_call(
        pack_keys_body,
        out_shape=jax.ShapeDtypeStruct((HEADS, SHARED, TOK), BF),
        in_specs=[WHOLE] * 3,
        out_specs=WHOLE,
        compiler_params=params(),
        cost_estimate=cost(2),
        name="pack_keys",
    )(key, value, tags)


def pack_queries_body(query, out_grad, tags, gate, weight, bg_ref, out_ref):
    gate_rows = lax.dot_general(
        clip_onehot(tags), gate[...], (((0,), (0,)), ((), ())),
        precision=lax.Precision.HIGHEST, preferred_element_type=F32,
    )
    branch = (out_grad[...].astype(F32) * gate_rows).astype(BF)
    bg_ref[...] = branch
    grad_t = lax.dot_general(weight[...], branch, (((1,), (1,)), ((), ())), preferred_element_type=F32)
    query_t = query[...].astype(F32).T
    for head in range(HEADS):
        rows = slice(head * HEAD_DIM, (head + 1) * HEAD_DIM)
        out_ref[head] = jnp.concatenate([query_t[rows], grad_t[rows]], 0).astype(BF)


def pack_queries(query, out_grad, tags, gate, weight):
    return pl.pallas_call(
        pack_queries_body,
        out_shape=(jax.ShapeDtypeStruct((TOK, WIDTH), BF), jax.ShapeDtypeStruct((HEADS, PAIR, TOK), BF)),
        in_specs=[WHOLE] * 5,
        out_specs=(WHOLE, WHOLE),
        compiler_params=params(),
        cost_estimate=cost(4),
        name="pack_queries",
    )(query, out_grad, tags, gate, weight)


def filled(piece, extra):
    rows = [piece] + extra
    have = sum(part.shape[0] for part in rows)
    if have < TOK:
        rows.append(jnp.zeros((TOK - have, TOK), F32))
    return jnp.concatenate(rows, 0)


def lay_out_keys(block, left, keys, right, key_n, key_t, value_n, value_t):
    if block < EDGE:
        whole = left[block]
    elif block < EDGE + HEADS:
        whole = keys[block - EDGE]
    else:
        whole = right[block - EDGE - HEADS]
    whole = whole.astype(F32)
    clip = whole[2 * HEAD_DIM : 2 * HEAD_DIM + 1]
    ids = lax.broadcasted_iota(jnp.int32, (CLIPS, TOK), 0).astype(F32) + 1.0
    rows = slice(block * TOK, (block + 1) * TOK)
    held = filled(whole[0:HEAD_DIM], [jnp.where(ids == clip, 0.0, FAR)])
    key_n[rows, :] = held.T.astype(BF)
    key_t[block] = held[0:80].astype(BF)
    held = filled(whole[HEAD_DIM : 2 * HEAD_DIM], [jnp.ones((8, TOK), F32)])
    value_n[rows, :] = held.T.astype(BF)
    value_t[block] = held[0:80].astype(BF)
    return clip


def lay_out_queries(block, queries, clip, query_t, query_n, grad_t, grad_n):
    whole = queries[block].astype(F32)
    ids = lax.broadcasted_iota(jnp.int32, (CLIPS, TOK), 0).astype(F32) + 1.0
    tile, cols = block // PART, slice((block % PART) * TOK, (block % PART + 1) * TOK)
    held = filled(whole[0:HEAD_DIM], [jnp.where(ids == clip, 1.0, 0.0)])
    query_t[tile, :, cols] = held.astype(BF)
    query_n[tile, cols, :] = held.T.astype(BF)
    held = filled(whole[HEAD_DIM:], [])
    grad_t[tile, :, cols] = held.astype(BF)
    grad_n[tile, cols, :] = held.T.astype(BF)


def key_ranges(clips, first_ref, count_ref):
    clips = [jnp.where(row == 0.0, 100.0, row) if at >= EDGE + HEADS else row for at, row in enumerate(clips)]
    clips = jnp.concatenate(clips + [jnp.full((32 - SPAN, TOK), 100.0, F32)], 0)
    least = jnp.min(clips, axis=1, keepdims=True)
    most = jnp.max(clips, axis=1, keepdims=True)
    for tile in range(TILES):
        start = EDGE + tile * PART
        low, high = least[start : start + 1], most[start + PART - 1 : start + PART]
        first = jnp.sum(jnp.where(most < low, 1.0, 0.0)).astype(jnp.int32)
        end = jnp.sum(jnp.where(least <= high, 1.0, 0.0)).astype(jnp.int32)
        first_ref[tile] = first
        count_ref[tile] = (end - first + STEP - 1) // STEP


def attend_body(
    left, keys, right, queries, asked_ref, given_ref, back_ref, ahead_ref,
    key_n, key_t, value_n, value_t, query_t, query_n, grad_t, grad_n, held, dk, dv, first_ref, count_ref,
):
    clips = [lay_out_keys(block, left, keys, right, key_n, key_t, value_n, value_t) for block in range(SPAN)]
    for block in range(HEADS):
        lay_out_queries(block, queries, clips[EDGE + block], query_t, query_n, grad_t, grad_n)
    rows = slice(SPAN * TOK, ROOM * TOK)
    lane = lax.broadcasted_iota(jnp.int32, ((ROOM - SPAN) * TOK, TOK), 1)
    key_n[rows, :] = jnp.where((lane >= HEAD_DIM) & (lane < HEAD_DIM + CLIPS), FAR, 0.0).astype(BF)
    value_n[rows, :] = jnp.zeros(((ROOM - SPAN) * TOK, TOK), BF)
    for block in range(SPAN, ROOM):
        key_t[block] = jnp.zeros((80, TOK), BF)
        value_t[block] = jnp.zeros((80, TOK), BF)
    key_ranges(clips, first_ref, count_ref)
    dk[...] = jnp.zeros_like(dk)
    dv[...] = jnp.zeros_like(dv)

    def side_by_side(ref, start):
        return jnp.concatenate([ref[start + at] for at in range(STEP)], 1)

    def query_step(tile, carry):
        first, count = first_ref[tile], count_ref[tile]

        def blocks(step):
            start = first + step * STEP
            return start, pl.ds(pl.multiple_of(start * TOK, TOK), STEP * TOK)

        def score_step(step, top):
            scores = mm(key_n[blocks(step)[1], :], query_t[tile])
            held[step] = scores
            return jnp.maximum(top, jnp.max(scores, axis=0, keepdims=True))

        top = lax.fori_loop(0, count, score_step, jnp.full((1, TILE), 2.0 * FAR, F32))

        def value_step(step, total):
            weights = jnp.exp2((held[step] - top) * SCALE2)
            held[step] = weights
            return total + mm(side_by_side(value_t, blocks(step)[0]), weights.astype(BF))

        total = lax.fori_loop(0, count, value_step, jnp.zeros((80, TILE), F32))
        inverse = 1.0 / total[HEAD_DIM : HEAD_DIM + 1]
        mixed = (total[0:HEAD_DIM] * inverse).astype(BF)
        grad = grad_t[tile]
        delta = jnp.sum(mixed.astype(F32) * grad[0:HEAD_DIM].astype(F32), axis=0, keepdims=True)

        def grad_step(step, total):
            start, rows = blocks(step)
            prob = held[step] * inverse
            pull = mm(value_n[rows, :], grad)
            dv[rows, :] += mm(prob.astype(BF), grad_n[tile])
            score_grad = (prob * (pull - delta)).astype(BF)
            dk[rows, :] += mm(score_grad, query_n[tile])
            return total + mm(side_by_side(key_t, start), score_grad)

        total = lax.fori_loop(0, count, grad_step, jnp.zeros((80, TILE), F32))
        pair = jnp.concatenate([mixed.astype(F32), total[0:HEAD_DIM] * SCALE], 0).astype(BF)
        for part in range(PART):
            asked_ref[tile * PART + part] = pair[:, part * TOK : (part + 1) * TOK]
        return carry

    lax.fori_loop(0, TILES, query_step, 0)
    for block in range(SPAN):
        rows = slice(block * TOK, (block + 1) * TOK)
        pair = jnp.concatenate([dk[rows, :].T[0:HEAD_DIM] * SCALE, dv[rows, :].T[0:HEAD_DIM]], 0).astype(BF)
        if block < EDGE:
            back_ref[block] = pair
        elif block < EDGE + HEADS:
            given_ref[block - EDGE] = pair
        else:
            ahead_ref[block - EDGE - HEADS] = pair


def attend(left, keys, right, queries):
    own = jax.ShapeDtypeStruct((HEADS, PAIR, TOK), BF)
    halo = jax.ShapeDtypeStruct((EDGE, PAIR, TOK), BF)
    row_form = pltpu.VMEM((ROOM * TOK, TOK), BF)
    column_form = pltpu.VMEM((ROOM, 80, TOK), BF)
    return pl.pallas_call(
        attend_body,
        out_shape=(own, own, halo, halo),
        in_specs=[WHOLE] * 4,
        out_specs=(WHOLE,) * 4,
        cost_estimate=cost(20),
        scratch_shapes=[
            row_form, column_form, row_form, column_form,
            pltpu.VMEM((TILES, TOK, TILE), BF), pltpu.VMEM((TILES, TILE, TOK), BF),
            pltpu.VMEM((TILES, TOK, TILE), BF), pltpu.VMEM((TILES, TILE, TOK), BF),
            pltpu.VMEM((CHUNKS, STEP * TOK, TILE), F32),
            pltpu.VMEM((ROOM * TOK, TOK), F32),
            pltpu.VMEM((ROOM * TOK, TOK), F32),
            pltpu.SMEM((TILES,), jnp.int32),
            pltpu.SMEM((TILES,), jnp.int32),
        ],
        compiler_params=params(),
        name="attend",
    )(left, keys, right, queries)


def weight_term_body(asked, branch, out_ref, total):
    step = pl.program_id(0)
    mixed = jnp.concatenate([asked[part, 0:80] for part in range(PART)], 1)

    @pl.when(step == 0)
    def _():
        total[...] = jnp.zeros_like(total)

    total[...] += mm(mixed, branch[...].reshape(TILE, WIDTH))

    @pl.when(step == TILES - 1)
    def _():
        whole = jnp.concatenate([total[0:HEAD_DIM], jnp.zeros((TOK - HEAD_DIM, WIDTH), F32)], 0)
        out_ref[...] = whole.T.astype(BF).reshape(GROUPS, SHARE, TOK)


def weight_term(asked, branch):
    return pl.pallas_call(
        weight_term_body,
        grid=(TILES,),
        out_shape=jax.ShapeDtypeStruct((GROUPS, SHARE, TOK), BF),
        in_specs=[
            pl.BlockSpec((PART, PAIR, TOK), lambda i: (i, 0, 0)),
            pl.BlockSpec((PART, TOK, WIDTH), lambda i: (i, 0, 0)),
        ],
        out_specs=pl.BlockSpec((GROUPS, SHARE, TOK), lambda i: (0, 0, 0)),
        scratch_shapes=[pltpu.VMEM((80, WIDTH), F32)],
        compiler_params=params(),
        cost_estimate=cost(6),
        name="weight_term",
    )(asked, branch)


def join_body(given, from_left, from_right, terms, out_ref, total):
    total[0:SHARE] = sum(terms[group].astype(F32) for group in range(GROUPS))
    total[SHARE:] = jnp.zeros((8, TOK), F32)
    for block in range(HEADS):
        whole = given[block].astype(F32)
        if block < EDGE:
            whole += from_left[block].astype(F32)
        if block >= HEADS - EDGE:
            whole += from_right[block - HEADS + EDGE].astype(F32)
        tail = total[block * FINAL : block * FINAL + 16, :]
        out_ref[block] = jnp.concatenate([whole, tail], 0).astype(BF)


def join(given, from_left, from_right, terms):
    return pl.pallas_call(
        join_body,
        out_shape=jax.ShapeDtypeStruct((HEADS, PAIR + 16, TOK), BF),
        in_specs=[WHOLE] * 4,
        out_specs=WHOLE,
        scratch_shapes=[pltpu.VMEM((SHARE + 8, TOK), F32)],
        compiler_params=params(),
        cost_estimate=cost(2),
        name="join",
    )(given, from_left, from_right, terms)


def gathered_heads(packed, start):
    rows = slice(start, start + HEAD_DIM)
    return jnp.concatenate([packed[head].astype(F32)[rows] for head in range(HEADS)], 0).T.astype(BF)


def finish_queries_body(packed, residual, tags, gate, weight, bias, out_ref, dq_ref):
    gate_rows = lax.dot_general(
        clip_onehot(tags), gate[...], (((0,), (0,)), ((), ())),
        precision=lax.Precision.HIGHEST, preferred_element_type=F32,
    )
    projected = mm(gathered_heads(packed, 0), weight[...]) + bias[...].reshape(1, WIDTH)
    out_ref[...] = (residual[...].astype(F32) + gate_rows * projected).astype(BF)
    dq_ref[...] = gathered_heads(packed, HEAD_DIM)


def finish_queries(packed, residual, tags, gate, weight, bias):
    return pl.pallas_call(
        finish_queries_body,
        out_shape=(jax.ShapeDtypeStruct((TOK, WIDTH), BF),) * 2,
        in_specs=[WHOLE] * 6,
        out_specs=(WHOLE,) * 2,
        compiler_params=params(),
        cost_estimate=cost(4),
        name="finish_queries",
    )(packed, residual, tags, gate, weight, bias)


def finish_keys_body(packed, dk_ref, dv_ref, dw_ref):
    dk_ref[...] = gathered_heads(packed, 0)
    dv_ref[...] = gathered_heads(packed, HEAD_DIM)
    tails = [packed[head].astype(F32)[PAIR:, 0:HEAD_DIM] for head in range(HEADS)]
    dw_ref[...] = jnp.concatenate(tails, 1)[0:FINAL]


def finish_keys(packed):
    return pl.pallas_call(
        finish_keys_body,
        out_shape=(jax.ShapeDtypeStruct((TOK, WIDTH), BF),) * 2 + (jax.ShapeDtypeStruct((FINAL, WIDTH), F32),),
        in_specs=[WHOLE],
        out_specs=(WHOLE,) * 3,
        compiler_params=params(),
        cost_estimate=cost(2),
        name="finish_keys",
    )(packed)


def from_neighbour(values, by):
    total = GROUPS * HEADS
    pairs = [(i, i + by * HEADS) for i in range(total) if 0 <= i + by * HEADS < total]
    return lax.ppermute(values, ("g", "r"), pairs)


def traded(values, axis):
    return lax.all_to_all(values, axis, 0, 0, tiled=True)


def shards(query, key, value, residual, tags, gate, weight, bias, out_grad):
    keys = pack_keys(key, value, tags)
    keys, query = lax.optimization_barrier((keys, query))
    keys = traded(keys, "r")
    branch, asking = pack_queries(query, out_grad, tags, gate, weight)
    gathered = lax.all_gather(branch, "r", axis=0, tiled=False)
    left = from_neighbour(keys[HEADS - EDGE :], 1)
    right = from_neighbour(keys[:EDGE], -1)
    queries = traded(asking, "r")
    asked, given, back, ahead = attend(left, keys, right, queries)
    from_left = from_neighbour(ahead, 1)
    from_right = from_neighbour(back, -1)
    asked_back = traded(asked, "r")
    terms = traded(weight_term(asked, gathered), "g")
    given_back = traded(join(given, from_left, from_right, terms), "r")
    block_out, dq = finish_queries(asked_back, residual, tags, gate, weight, bias)
    dk, dv, dw = finish_keys(given_back)
    return block_out, dq, dk, dv, dw.T


def solution(mesh):
    split = Mesh(mesh.devices.reshape(GROUPS, HEADS), ("g", "r"))
    both = ("g", "r")
    in_specs = (
        P(both, None), P(both, None), P(both, None), P(both, None), P(both), P(), P(), P(), P(both, None),
    )
    out_specs = (P(both, None),) * 4 + (P(None, both),)
    return jax.shard_map(shards, mesh=split, in_specs=in_specs, out_specs=out_specs, check_vma=False)
```

```python
import math

import jax
import jax.numpy as jnp
from jax import lax
from jax.experimental import pallas as pl
from jax.experimental.pallas import tpu as pltpu
from jax.sharding import Mesh, PartitionSpec as P

HEADS = 16
HEAD_DIM = 72
WIDTH = HEADS * HEAD_DIM
TOK = 128
GROUPS = 8
EDGE = 7
SPAN = HEADS + 2 * EDGE
TILE = 256
TILES = HEADS * TOK // TILE
PART = TILE // TOK
STEP = 4
ROOM = SPAN + STEP - 1
CHUNKS = 5
SHARED = 2 * HEAD_DIM + 16
PAIR = 2 * HEAD_DIM
SHARE = WIDTH // GROUPS
FINAL = SHARE // HEADS
CLIPS = 32
SCALE = 1.0 / math.sqrt(HEAD_DIM)
SCALE2 = SCALE / math.log(2.0)
FAR = -1e30
BF = jnp.bfloat16
F32 = jnp.float32
VMEM_BYTES = 56 * 1024 * 1024

WHOLE = pl.BlockSpec(memory_space=pltpu.VMEM)


def params():
    return pltpu.CompilerParams(vmem_limit_bytes=VMEM_BYTES)


def cost(micros):
    return pl.CostEstimate(flops=int(micros * 4e8), bytes_accessed=int(micros * 2e6), transcendentals=0)


def mm(left, right):
    return jnp.dot(left, right, preferred_element_type=F32)


def clip_onehot(tags):
    ids = lax.broadcasted_iota(jnp.int32, (CLIPS, TOK), 0)
    return (ids == tags[...].reshape(1, TOK)).astype(F32)


def pack_keys_body(key, value, tags, out_ref):
    key_t = key[...].astype(F32).T
    value_t = value[...].astype(F32).T
    tag_rows = jnp.broadcast_to(tags[...].reshape(1, TOK).astype(F32) + 1.0, (16, TOK))
    for head in range(HEADS):
        rows = slice(head * HEAD_DIM, (head + 1) * HEAD_DIM)
        out_ref[head] = jnp.concatenate([key_t[rows], value_t[rows], tag_rows], 0).astype(BF)


def pack_keys(key, value, tags):
    return pl.pallas_call(
        pack_keys_body,
        out_shape=jax.ShapeDtypeStruct((HEADS, SHARED, TOK), BF),
        in_specs=[WHOLE] * 3,
        out_specs=WHOLE,
        compiler_params=params(),
        cost_estimate=cost(2),
        name="pack_keys",
    )(key, value, tags)


def pack_queries_body(query, out_grad, tags, gate, weight, bg_ref, out_ref):
    gate_rows = lax.dot_general(
        clip_onehot(tags), gate[...], (((0,), (0,)), ((), ())),
        precision=lax.Precision.HIGHEST, preferred_element_type=F32,
    )
    branch = (out_grad[...].astype(F32) * gate_rows).astype(BF)
    bg_ref[...] = branch
    grad_t = lax.dot_general(weight[...], branch, (((1,), (1,)), ((), ())), preferred_element_type=F32)
    query_t = query[...].astype(F32).T
    for head in range(HEADS):
        rows = slice(head * HEAD_DIM, (head + 1) * HEAD_DIM)
        out_ref[head] = jnp.concatenate([query_t[rows], grad_t[rows]], 0).astype(BF)


def pack_queries(query, out_grad, tags, gate, weight):
    return pl.pallas_call(
        pack_queries_body,
        out_shape=(jax.ShapeDtypeStruct((TOK, WIDTH), BF), jax.ShapeDtypeStruct((HEADS, PAIR, TOK), BF)),
        in_specs=[WHOLE] * 5,
        out_specs=(WHOLE, WHOLE),
        compiler_params=params(),
        cost_estimate=cost(4),
        name="pack_queries",
    )(query, out_grad, tags, gate, weight)


def filled(piece, extra):
    rows = [piece] + extra
    have = sum(part.shape[0] for part in rows)
    if have < TOK:
        rows.append(jnp.zeros((TOK - have, TOK), F32))
    return jnp.concatenate(rows, 0)


def window_block(block, left, keys, right):
    if block < EDGE:
        return left[block].astype(F32)
    if block < EDGE + HEADS:
        return keys[block - EDGE].astype(F32)
    return right[block - EDGE - HEADS].astype(F32)


def same_clip(clip, same, other):
    ids = lax.broadcasted_iota(jnp.int32, (CLIPS, TOK), 0).astype(F32) + 1.0
    return jnp.where(ids == clip, same, other)


def lay_out_keys(block, whole, key_n, key_t):
    held = filled(whole[0:HEAD_DIM], [same_clip(whole[PAIR : PAIR + 1], 0.0, FAR)])
    key_n[block * TOK : (block + 1) * TOK, :] = held.T.astype(BF)
    if key_t is not None:
        key_t[block] = held[0:80].astype(BF)


def key_padding(key_n, key_t):
    rows = slice(SPAN * TOK, ROOM * TOK)
    lane = lax.broadcasted_iota(jnp.int32, ((ROOM - SPAN) * TOK, TOK), 1)
    key_n[rows, :] = jnp.where((lane >= HEAD_DIM) & (lane < HEAD_DIM + CLIPS), FAR, 0.0).astype(BF)
    if key_t is not None:
        for block in range(SPAN, ROOM):
            key_t[block] = jnp.zeros((80, TOK), BF)


def key_ranges(clips, first_ref, count_ref):
    clips = [jnp.where(row == 0.0, 100.0, row) if at >= EDGE + HEADS else row for at, row in enumerate(clips)]
    clips = jnp.concatenate(clips + [jnp.full((32 - SPAN, TOK), 100.0, F32)], 0)
    least = jnp.min(clips, axis=1, keepdims=True)
    most = jnp.max(clips, axis=1, keepdims=True)
    for tile in range(TILES):
        start = EDGE + tile * PART
        low, high = least[start : start + 1], most[start + PART - 1 : start + PART]
        first = jnp.sum(jnp.where(most < low, 1.0, 0.0)).astype(jnp.int32)
        end = jnp.sum(jnp.where(least <= high, 1.0, 0.0)).astype(jnp.int32)
        first_ref[tile] = first
        count_ref[tile] = (end - first + STEP - 1) // STEP


def side_by_side(ref, start):
    return jnp.concatenate([ref[start + at] for at in range(STEP)], 1)


def blocks(first, step):
    start = first + step * STEP
    return start, pl.ds(pl.multiple_of(start * TOK, TOK), STEP * TOK)


def forward_body(
    left, keys, right, queries, mixed_ref, stat_ref, key_n, value_t, query_t, held, first_ref, count_ref
):
    clips = []
    for block in range(SPAN):
        whole = window_block(block, left, keys, right)
        clips.append(whole[PAIR : PAIR + 1])
        lay_out_keys(block, whole, key_n, None)
        value_t[block] = filled(whole[HEAD_DIM:PAIR], [jnp.ones((8, TOK), F32)])[0:80].astype(BF)
    for block in range(SPAN, ROOM):
        value_t[block] = jnp.zeros((80, TOK), BF)
    key_padding(key_n, None)
    for block in range(HEADS):
        cols = slice((block % PART) * TOK, (block % PART + 1) * TOK)
        asked = filled(queries[block].astype(F32)[0:HEAD_DIM], [same_clip(clips[EDGE + block], 1.0, 0.0)])
        query_t[block // PART, :, cols] = asked.astype(BF)
    key_ranges(clips, first_ref, count_ref)

    def query_step(tile, carry):
        first, count = first_ref[tile], count_ref[tile]

        def score_step(step, top):
            scores = mm(key_n[blocks(first, step)[1], :], query_t[tile])
            held[step] = scores
            return jnp.maximum(top, jnp.max(scores, axis=0, keepdims=True))

        top = lax.fori_loop(0, count, score_step, jnp.full((1, TILE), 2.0 * FAR, F32))

        def value_step(step, total):
            weights = jnp.exp2((held[step] - top) * SCALE2).astype(BF)
            return total + mm(side_by_side(value_t, blocks(first, step)[0]), weights)

        total = lax.fori_loop(0, count, value_step, jnp.zeros((80, TILE), F32))
        sums = total[HEAD_DIM : HEAD_DIM + 1]
        mixed = (total[0:HEAD_DIM] / sums).astype(BF)
        stat_ref[tile] = jnp.broadcast_to(top * SCALE2 + jnp.log2(sums), (8, TILE))
        for part in range(PART):
            mixed_ref[tile * PART + part] = mixed[:, part * TOK : (part + 1) * TOK]
        return carry

    lax.fori_loop(0, TILES, query_step, 0)


def forward(left, keys, right, queries):
    return pl.pallas_call(
        forward_body,
        out_shape=(
            jax.ShapeDtypeStruct((HEADS, HEAD_DIM, TOK), BF),
            jax.ShapeDtypeStruct((TILES, 8, TILE), F32),
        ),
        in_specs=[WHOLE] * 4,
        out_specs=(WHOLE,) * 2,
        cost_estimate=cost(10),
        scratch_shapes=[
            pltpu.VMEM((ROOM * TOK, TOK), BF),
            pltpu.VMEM((ROOM, 80, TOK), BF),
            pltpu.VMEM((TILES, TOK, TILE), BF),
            pltpu.VMEM((CHUNKS, STEP * TOK, TILE), F32),
            pltpu.SMEM((TILES,), jnp.int32),
            pltpu.SMEM((TILES,), jnp.int32),
        ],
        compiler_params=params(),
        name="forward",
    )(left, keys, right, queries)


def backward_body(
    left, keys, right, queries, mixed, stat, dq_ref, given_ref, back_ref, ahead_ref,
    key_n, key_t, value_n, query_t, query_n, grad_t, grad_n, deltas, dk, dv, first_ref, count_ref,
):
    clips = []
    for block in range(SPAN):
        whole = window_block(block, left, keys, right)
        clips.append(whole[PAIR : PAIR + 1])
        lay_out_keys(block, whole, key_n, key_t)
        value_n[block * TOK : (block + 1) * TOK, :] = filled(whole[HEAD_DIM:PAIR], []).T.astype(BF)
    value_n[SPAN * TOK :, :] = jnp.zeros(((ROOM - SPAN) * TOK, TOK), BF)
    key_padding(key_n, key_t)
    for block in range(HEADS):
        tile, cols = block // PART, slice((block % PART) * TOK, (block % PART + 1) * TOK)
        whole = queries[block].astype(F32)
        asked = filled(whole[0:HEAD_DIM], [same_clip(clips[EDGE + block], 1.0, 0.0)])
        query_t[tile, :, cols] = asked.astype(BF)
        query_n[tile, cols, :] = asked.T.astype(BF)
        grad = filled(whole[HEAD_DIM:], [])
        grad_t[tile, :, cols] = grad.astype(BF)
        grad_n[tile, cols, :] = grad.T.astype(BF)
        delta = jnp.sum(whole[HEAD_DIM:] * mixed[block].astype(F32), axis=0, keepdims=True)
        deltas[tile, :, cols] = jnp.broadcast_to(delta, (8, TOK))
    key_ranges(clips, first_ref, count_ref)
    dk[...] = jnp.zeros_like(dk)
    dv[...] = jnp.zeros_like(dv)

    def query_step(tile, carry):
        first, count = first_ref[tile], count_ref[tile]
        log_sum = stat[tile, 0:1]
        delta = deltas[tile, 0:1]

        def grad_step(step, total):
            start, rows = blocks(first, step)
            scores = mm(key_n[rows, :], query_t[tile])
            prob = jnp.exp2(scores * SCALE2 - log_sum)
            pull = mm(value_n[rows, :], grad_t[tile])
            dv[rows, :] += mm(prob.astype(BF), grad_n[tile])
            score_grad = (prob * (pull - delta)).astype(BF)
            dk[rows, :] += mm(score_grad, query_n[tile])
            return total + mm(side_by_side(key_t, start), score_grad)

        total = lax.fori_loop(0, count, grad_step, jnp.zeros((80, TILE), F32))
        grad = (total[0:HEAD_DIM] * SCALE).astype(BF)
        for part in range(PART):
            dq_ref[tile * PART + part] = grad[:, part * TOK : (part + 1) * TOK]
        return carry

    lax.fori_loop(0, TILES, query_step, 0)
    for block in range(SPAN):
        rows = slice(block * TOK, (block + 1) * TOK)
        pair = jnp.concatenate([dk[rows, :].T[0:HEAD_DIM] * SCALE, dv[rows, :].T[0:HEAD_DIM]], 0).astype(BF)
        if block < EDGE:
            back_ref[block] = pair
        elif block < EDGE + HEADS:
            given_ref[block - EDGE] = pair
        else:
            ahead_ref[block - EDGE - HEADS] = pair


def backward(left, keys, right, queries, mixed, stat):
    halo = jax.ShapeDtypeStruct((EDGE, PAIR, TOK), BF)
    row_form = pltpu.VMEM((ROOM * TOK, TOK), BF)
    return pl.pallas_call(
        backward_body,
        out_shape=(
            jax.ShapeDtypeStruct((HEADS, HEAD_DIM, TOK), BF),
            jax.ShapeDtypeStruct((HEADS, PAIR, TOK), BF),
            halo,
            halo,
        ),
        in_specs=[WHOLE] * 6,
        out_specs=(WHOLE,) * 4,
        cost_estimate=cost(14),
        scratch_shapes=[
            row_form, pltpu.VMEM((ROOM, 80, TOK), BF), row_form,
            pltpu.VMEM((TILES, TOK, TILE), BF), pltpu.VMEM((TILES, TILE, TOK), BF),
            pltpu.VMEM((TILES, TOK, TILE), BF), pltpu.VMEM((TILES, TILE, TOK), BF),
            pltpu.VMEM((TILES, 8, TILE), F32),
            pltpu.VMEM((ROOM * TOK, TOK), F32),
            pltpu.VMEM((ROOM * TOK, TOK), F32),
            pltpu.SMEM((TILES,), jnp.int32),
            pltpu.SMEM((TILES,), jnp.int32),
        ],
        compiler_params=params(),
        name="backward",
    )(left, keys, right, queries, mixed, stat)


def weight_term_body(mixed_ref, branch, out_ref, total):
    step = pl.program_id(0)
    mixed = jnp.concatenate([mixed_ref[part].astype(F32) for part in range(PART)], 1).astype(BF)

    @pl.when(step == 0)
    def _():
        total[...] = jnp.zeros_like(total)

    total[...] += mm(mixed, branch[...].reshape(TILE, WIDTH))

    @pl.when(step == TILES - 1)
    def _():
        whole = jnp.concatenate([total[...], jnp.zeros((TOK - HEAD_DIM, WIDTH), F32)], 0)
        out_ref[...] = whole.T.astype(BF).reshape(GROUPS, SHARE, TOK)


def weight_term(mixed, branch):
    return pl.pallas_call(
        weight_term_body,
        grid=(TILES,),
        out_shape=jax.ShapeDtypeStruct((GROUPS, SHARE, TOK), BF),
        in_specs=[
            pl.BlockSpec((PART, HEAD_DIM, TOK), lambda i: (i, 0, 0)),
            pl.BlockSpec((PART, TOK, WIDTH), lambda i: (i, 0, 0)),
        ],
        out_specs=pl.BlockSpec((GROUPS, SHARE, TOK), lambda i: (0, 0, 0)),
        scratch_shapes=[pltpu.VMEM((HEAD_DIM, WIDTH), F32)],
        compiler_params=params(),
        cost_estimate=cost(6),
        name="weight_term",
    )(mixed, branch)


def join_body(mixed, dq, given, from_left, from_right, terms, out_ref, total):
    total[0:SHARE] = sum(terms[group].astype(F32) for group in range(GROUPS))
    total[SHARE:] = jnp.zeros((8, TOK), F32)
    for block in range(HEADS):
        pair = given[block].astype(F32)
        if block < EDGE:
            pair += from_left[block].astype(F32)
        if block >= HEADS - EDGE:
            pair += from_right[block - HEADS + EDGE].astype(F32)
        tail = total[block * FINAL : block * FINAL + 16, :]
        whole = [mixed[block].astype(F32), dq[block].astype(F32), pair, tail]
        out_ref[block] = jnp.concatenate(whole, 0).astype(BF)


def join(mixed, dq, given, from_left, from_right, terms):
    return pl.pallas_call(
        join_body,
        out_shape=jax.ShapeDtypeStruct((HEADS, 2 * PAIR + 16, TOK), BF),
        in_specs=[WHOLE] * 6,
        out_specs=WHOLE,
        scratch_shapes=[pltpu.VMEM((SHARE + 8, TOK), F32)],
        compiler_params=params(),
        cost_estimate=cost(2),
        name="join",
    )(mixed, dq, given, from_left, from_right, terms)


def finish_body(packed, residual, tags, gate, weight, bias, out_ref, dq_ref, dk_ref, dv_ref, dw_ref):
    whole = [packed[head].astype(F32) for head in range(HEADS)]

    def rows(at):
        part = slice(at * HEAD_DIM, (at + 1) * HEAD_DIM)
        return jnp.concatenate([one[part] for one in whole], 0).T.astype(BF)

    gate_rows = lax.dot_general(
        clip_onehot(tags), gate[...], (((0,), (0,)), ((), ())),
        precision=lax.Precision.HIGHEST, preferred_element_type=F32,
    )
    projected = mm(rows(0), weight[...]) + bias[...].reshape(1, WIDTH)
    out_ref[...] = (residual[...].astype(F32) + gate_rows * projected).astype(BF)
    dq_ref[...] = rows(1)
    dk_ref[...] = rows(2)
    dv_ref[...] = rows(3)
    dw_ref[...] = jnp.concatenate([one[2 * PAIR :, 0:HEAD_DIM] for one in whole], 1)[0:FINAL]


def finish(packed, residual, tags, gate, weight, bias):
    return pl.pallas_call(
        finish_body,
        out_shape=(jax.ShapeDtypeStruct((TOK, WIDTH), BF),) * 4 + (jax.ShapeDtypeStruct((FINAL, WIDTH), F32),),
        in_specs=[WHOLE] * 6,
        out_specs=(WHOLE,) * 5,
        compiler_params=params(),
        cost_estimate=cost(4),
        name="finish",
    )(packed, residual, tags, gate, weight, bias)


def from_neighbour(values, by):
    total = GROUPS * HEADS
    pairs = [(i, i + by * HEADS) for i in range(total) if 0 <= i + by * HEADS < total]
    return lax.ppermute(values, ("g", "r"), pairs)


def traded(values, axis):
    return lax.all_to_all(values, axis, 0, 0, tiled=True)


def shards(query, key, value, residual, tags, gate, weight, bias, out_grad):
    keys = pack_keys(key, value, tags)
    keys, query = lax.optimization_barrier((keys, query))
    keys = traded(keys, "r")
    branch, asking = pack_queries(query, out_grad, tags, gate, weight)
    gathered = lax.all_gather(branch, "r", axis=0, tiled=False)
    left = from_neighbour(keys[HEADS - EDGE :], 1)
    right = from_neighbour(keys[:EDGE], -1)
    queries = traded(asking, "r")
    mixed, stat = forward(left, keys, right, queries)
    term = weight_term(mixed, gathered)
    term, stat = lax.optimization_barrier((term, stat))
    terms = traded(term, "g")
    dq, given, back, ahead = backward(left, keys, right, queries, mixed, stat)
    from_left = from_neighbour(ahead, 1)
    from_right = from_neighbour(back, -1)
    packed = traded(join(mixed, dq, given, from_left, from_right, terms), "r")
    block_out, dq, dk, dv, dw = finish(packed, residual, tags, gate, weight, bias)
    return block_out, dq, dk, dv, dw.T


def solution(mesh):
    split = Mesh(mesh.devices.reshape(GROUPS, HEADS), ("g", "r"))
    both = ("g", "r")
    in_specs = (
        P(both, None), P(both, None), P(both, None), P(both, None), P(both), P(), P(), P(), P(both, None),
    )
    out_specs = (P(both, None),) * 4 + (P(None, both),)
    return jax.shard_map(shards, mesh=split, in_specs=in_specs, out_specs=out_specs, check_vma=False)
```

```python
import math

import jax
import jax.numpy as jnp
from jax import lax
from jax.experimental import pallas as pl
from jax.experimental.pallas import tpu as pltpu
from jax.sharding import PartitionSpec as P

HEADS = 16
HEAD_DIM = 72
WIDTH = HEADS * HEAD_DIM
TOK = 128
DEVICES = 128
PLANES = 4
PLANE = 32
SIDE = 16
EDGE = 7
SPAN = SIDE + 2 * EDGE
NEAR = SIDE + EDGE
TILE = 256
TILES = SIDE * TOK // TILE
PART = TILE // TOK
STEP = 4
ROOM = SPAN + STEP - 1
CHUNKS = 5
HALF = 40
FULL = 2 * HALF
FINAL = WIDTH // DEVICES
SHARE = WIDTH // PLANES // 2
CLIPS = 32
SCALE = 1.0 / math.sqrt(HEAD_DIM)
SCALE2 = SCALE / math.log(2.0)
FAR = -1e30
BF = jnp.bfloat16
F32 = jnp.float32
VMEM_BYTES = 56 * 1024 * 1024

WHOLE = pl.BlockSpec(memory_space=pltpu.VMEM)


def params():
    return pltpu.CompilerParams(vmem_limit_bytes=VMEM_BYTES)


def cost(micros):
    return pl.CostEstimate(flops=int(micros * 4e8), bytes_accessed=int(micros * 2e6), transcendentals=0)


def mm(left, right):
    return jnp.dot(left, right, preferred_element_type=F32)


def clip_onehot(tags):
    ids = lax.broadcasted_iota(jnp.int32, (CLIPS, TOK), 0)
    return (ids == tags[...].reshape(1, TOK)).astype(F32)


def core():
    return lax.axis_index("dp") % 2


def pick(flag, first, second):
    return jnp.where(jnp.full(first.shape, flag, jnp.int32) == 0, first, second)


def pack_body(query, key, value, out_grad, tags, gate, weight, chunk_ref, mine_ref, theirs_ref):
    gate_t = lax.dot_general(
        gate[...], clip_onehot(tags), (((0,), (0,)), ((), ())),
        precision=lax.Precision.HIGHEST, preferred_element_type=F32,
    )
    branch_t = (out_grad[...].astype(F32).T * gate_t).astype(BF)
    grad_t = mm(weight[...], branch_t)
    wide = branch_t.astype(F32)
    halves = []
    for side in range(2):
        starts = [(2 * plane + side) * SHARE for plane in range(PLANES)]
        halves.append(jnp.concatenate([wide[start : start + SHARE] for start in starts], 0))
    side = core()
    mine_ref[...] = pick(side, halves[0], halves[1]).astype(BF)
    theirs_ref[...] = pick(side, halves[1], halves[0]).astype(BF)
    key_t = key[...].astype(F32).T
    value_t = value[...].astype(F32).T
    query_t = query[...].astype(F32).T
    tag_rows = jnp.broadcast_to(tags[...].reshape(1, TOK).astype(F32) + 1.0, (8, TOK))
    blank = jnp.zeros((8, TOK), F32)
    for head in range(HEADS):
        start = head * HEAD_DIM
        low, high = slice(start, start + HALF), slice(start + HALF, start + HEAD_DIM)
        whole = [key_t[low], value_t[low], query_t[low], grad_t[low]]
        chunk_ref[2 * head] = jnp.concatenate(whole, 0).astype(BF)
        whole = [key_t[high], tag_rows, value_t[high], blank, query_t[high], blank, grad_t[high], blank]
        chunk_ref[2 * head + 1] = jnp.concatenate(whole, 0).astype(BF)


def pack(query, key, value, out_grad, tags, gate, weight):
    half = jax.ShapeDtypeStruct((WIDTH // 2, TOK), BF)
    return pl.pallas_call(
        pack_body,
        out_shape=(jax.ShapeDtypeStruct((PLANE, 2 * FULL, TOK), BF), half, half),
        in_specs=[WHOLE] * 7,
        out_specs=(WHOLE,) * 3,
        compiler_params=params(),
        cost_estimate=cost(5),
        name="pack",
    )(query, key, value, out_grad, tags, gate, weight)


def filled(piece, extra):
    rows = [piece] + extra
    have = sum(part.shape[0] for part in rows)
    if have < TOK:
        rows.append(jnp.zeros((TOK - have, TOK), F32))
    return jnp.concatenate(rows, 0)


def natural(side, own, other):
    own, other = own.astype(F32), other.astype(F32)
    low, high = pick(side, own, other), pick(side, other, own)
    return [jnp.concatenate([low[rows], high[rows]], 0) for rows in (slice(0, HALF), slice(HALF, FULL))]


def window(side, own, near, far_own, far_other):
    for block in range(NEAR):
        at = block + EDGE * (1 - side)
        yield (at,) + tuple(natural(side, own[block + (SIDE - EDGE) * side, 0:FULL], near[block]))
    for block in range(EDGE):
        yield (block + NEAR * side,) + tuple(natural(side, far_own[block], far_other[block]))


def token_rows(block):
    return pl.ds(pl.multiple_of(block * TOK, TOK), TOK)


def same_clip(clip, same, other):
    ids = lax.broadcasted_iota(jnp.int32, (CLIPS, TOK), 0).astype(F32) + 1.0
    return jnp.where(ids == clip, same, other)


def lay_out_keys(block, key, key_n, key_t, clips):
    clip = key[HEAD_DIM : HEAD_DIM + 1]
    clips[block] = key[HEAD_DIM:]
    held = filled(key[0:HEAD_DIM], [same_clip(clip, 0.0, FAR)])
    key_n[token_rows(block), :] = held.T.astype(BF)
    if key_t is not None:
        key_t[block] = jnp.concatenate([key[0:HEAD_DIM], jnp.zeros((8, TOK), F32)], 0).astype(BF)


def key_padding(key_n, key_t):
    rows = slice(SPAN * TOK, ROOM * TOK)
    lane = lax.broadcasted_iota(jnp.int32, ((ROOM - SPAN) * TOK, TOK), 1)
    key_n[rows, :] = jnp.where((lane >= HEAD_DIM) & (lane < HEAD_DIM + CLIPS), FAR, 0.0).astype(BF)
    if key_t is not None:
        for block in range(SPAN, ROOM):
            key_t[block] = jnp.zeros((80, TOK), BF)


def key_ranges(clips, first_ref, count_ref):
    rows = [clips[block][0:1] for block in range(SPAN)]
    rows = [jnp.where(row == 0.0, 100.0, row) if at >= NEAR else row for at, row in enumerate(rows)]
    rows = jnp.concatenate(rows + [jnp.full((32 - SPAN, TOK), 100.0, F32)], 0)
    least = jnp.min(rows, axis=1, keepdims=True)
    most = jnp.max(rows, axis=1, keepdims=True)
    for tile in range(TILES):
        start = EDGE + tile * PART
        low, high = least[start : start + 1], most[start + PART - 1 : start + PART]
        first = jnp.sum(jnp.where(most < low, 1.0, 0.0)).astype(jnp.int32)
        end = jnp.sum(jnp.where(least <= high, 1.0, 0.0)).astype(jnp.int32)
        first_ref[tile] = first
        count_ref[tile] = (end - first + STEP - 1) // STEP


def side_by_side(ref, start):
    return jnp.concatenate([ref[start + at] for at in range(STEP)], 1)


def blocks(first, step):
    start = first + step * STEP
    return start, pl.ds(pl.multiple_of(start * TOK, TOK), STEP * TOK)


def forward_body(
    own, near, asked, far_own, far_other, mixed_ref, stat_ref,
    key_n, value_t, query_t, held, clips, first_ref, count_ref,
):
    side = core()
    for at, key, value in window(side, own, near, far_own, far_other):
        lay_out_keys(at, key, key_n, None, clips)
        value_t[at] = jnp.concatenate([value[0:HEAD_DIM], jnp.ones((8, TOK), F32)], 0).astype(BF)
    for block in range(SPAN, ROOM):
        value_t[block] = jnp.zeros((80, TOK), BF)
    key_padding(key_n, None)
    for block in range(SIDE):
        cols = slice((block % PART) * TOK, (block % PART + 1) * TOK)
        query = natural(side, own[SIDE * side + block, FULL:], asked[block])[0][0:HEAD_DIM]
        query = filled(query, [same_clip(clips[EDGE + block][0:1], 1.0, 0.0)])
        query_t[block // PART, :, cols] = query.astype(BF)
    key_ranges(clips, first_ref, count_ref)

    def query_step(tile, carry):
        first, count = first_ref[tile], count_ref[tile]

        def score_step(step, top):
            scores = mm(key_n[blocks(first, step)[1], :], query_t[tile])
            held[step] = scores
            return jnp.maximum(top, jnp.max(scores, axis=0, keepdims=True))

        top = lax.fori_loop(0, count, score_step, jnp.full((1, TILE), 2.0 * FAR, F32))

        def value_step(step, total):
            weights = jnp.exp2((held[step] - top) * SCALE2).astype(BF)
            return total + mm(side_by_side(value_t, blocks(first, step)[0]), weights)

        total = lax.fori_loop(0, count, value_step, jnp.zeros((80, TILE), F32))
        sums = total[HEAD_DIM : HEAD_DIM + 1]
        mixed = jnp.concatenate([total[0:HEAD_DIM] / sums, jnp.zeros((8, TILE), F32)], 0).astype(BF)
        stat_ref[tile] = jnp.broadcast_to(top * SCALE2 + jnp.log2(sums), (8, TILE))
        for part in range(PART):
            mixed_ref[tile * PART + part] = mixed[:, part * TOK : (part + 1) * TOK]
        return carry

    lax.fori_loop(0, TILES, query_step, 0)


def forward(own, near, asked, far_own, far_other):
    return pl.pallas_call(
        forward_body,
        out_shape=(
            jax.ShapeDtypeStruct((SIDE, FULL, TOK), BF),
            jax.ShapeDtypeStruct((TILES, 8, TILE), F32),
        ),
        in_specs=[WHOLE] * 5,
        out_specs=(WHOLE,) * 2,
        cost_estimate=cost(10),
        scratch_shapes=[
            pltpu.VMEM((ROOM * TOK, TOK), BF),
            pltpu.VMEM((ROOM, 80, TOK), BF),
            pltpu.VMEM((TILES, TOK, TILE), BF),
            pltpu.VMEM((CHUNKS, STEP * TOK, TILE), F32),
            pltpu.VMEM((SPAN, 8, TOK), F32),
            pltpu.SMEM((TILES,), jnp.int32),
            pltpu.SMEM((TILES,), jnp.int32),
        ],
        compiler_params=params(),
        name="forward",
    )(own, near, asked, far_own, far_other)


def backward_body(
    own, near, asked, far_own, far_other, mixed, stat,
    keep_ref, give_ref, keep_near_ref, give_near_ref, keep_far_ref, give_far_ref,
    key_n, key_t, value_n, query_t, query_n, grad_t, grad_n, deltas, dq, dk, dv, clips, first_ref, count_ref,
):
    side = core()
    for at, key, value in window(side, own, near, far_own, far_other):
        lay_out_keys(at, key, key_n, key_t, clips)
        value_n[token_rows(at), :] = filled(value[0:HEAD_DIM], []).T.astype(BF)
    value_n[SPAN * TOK :, :] = jnp.zeros(((ROOM - SPAN) * TOK, TOK), BF)
    key_padding(key_n, key_t)
    for block in range(SIDE):
        tile, cols = block // PART, slice((block % PART) * TOK, (block % PART + 1) * TOK)
        query, grad = natural(side, own[SIDE * side + block, FULL:], asked[block])
        query = filled(query[0:HEAD_DIM], [same_clip(clips[EDGE + block][0:1], 1.0, 0.0)])
        query_t[tile, :, cols] = query.astype(BF)
        query_n[tile, cols, :] = query.T.astype(BF)
        delta = jnp.sum(grad * mixed[block].astype(F32), axis=0, keepdims=True)
        deltas[tile, :, cols] = jnp.broadcast_to(delta, (8, TOK))
        grad = filled(grad, [])
        grad_t[tile, :, cols] = grad.astype(BF)
        grad_n[tile, cols, :] = grad.T.astype(BF)
    key_ranges(clips, first_ref, count_ref)
    dk[...] = jnp.zeros_like(dk)
    dv[...] = jnp.zeros_like(dv)

    def query_step(tile, carry):
        first, count = first_ref[tile], count_ref[tile]
        log_sum = stat[tile, 0:1]
        delta = deltas[tile, 0:1]

        def grad_step(step, total):
            start, rows = blocks(first, step)
            scores = mm(key_n[rows, :], query_t[tile])
            prob = jnp.exp2(scores * SCALE2 - log_sum)
            pull = mm(value_n[rows, :], grad_t[tile])
            dv[rows, :] += mm(prob.astype(BF), grad_n[tile])
            score_grad = (prob * (pull - delta)).astype(BF)
            dk[rows, :] += mm(score_grad, query_n[tile])
            return total + mm(side_by_side(key_t, start), score_grad)

        total = lax.fori_loop(0, count, grad_step, jnp.zeros((80, TILE), F32))
        for part in range(PART):
            dq[tile * PART + part] = total[:, part * TOK : (part + 1) * TOK] * SCALE
        return carry

    lax.fori_loop(0, TILES, query_step, 0)

    def halves(wholes):
        low = jnp.concatenate([whole[0:HALF] for whole in wholes], 0)
        high = jnp.concatenate([whole[HALF:] for whole in wholes], 0)
        return pick(side, low, high).astype(BF), pick(side, high, low).astype(BF)

    def key_grads(at):
        rows = token_rows(at)
        return [dk[rows, :].T[0:FULL] * SCALE, dv[rows, :].T[0:FULL]]

    for block in range(SIDE):
        wholes = [mixed[block].astype(F32), dq[block]] + key_grads(EDGE + block)
        keep_ref[block], give_ref[block] = halves(wholes)
    for block in range(EDGE):
        keep_near_ref[block], give_near_ref[block] = halves(key_grads(block + NEAR * (1 - side)))
        keep_far_ref[block], give_far_ref[block] = halves(key_grads(block + NEAR * side))


def backward(own, near, asked, far_own, far_other, mixed, stat):
    whole = jax.ShapeDtypeStruct((SIDE, 2 * FULL, TOK), BF)
    edge = jax.ShapeDtypeStruct((EDGE, FULL, TOK), BF)
    row_form = pltpu.VMEM((ROOM * TOK, TOK), BF)
    return pl.pallas_call(
        backward_body,
        out_shape=(whole, whole, edge, edge, edge, edge),
        in_specs=[WHOLE] * 7,
        out_specs=(WHOLE,) * 6,
        cost_estimate=cost(14),
        scratch_shapes=[
            row_form, pltpu.VMEM((ROOM, 80, TOK), BF), row_form,
            pltpu.VMEM((TILES, TOK, TILE), BF), pltpu.VMEM((TILES, TILE, TOK), BF),
            pltpu.VMEM((TILES, TOK, TILE), BF), pltpu.VMEM((TILES, TILE, TOK), BF),
            pltpu.VMEM((TILES, 8, TILE), F32),
            pltpu.VMEM((SIDE, FULL, TOK), F32),
            pltpu.VMEM((ROOM * TOK, TOK), F32),
            pltpu.VMEM((ROOM * TOK, TOK), F32),
            pltpu.VMEM((SPAN, 8, TOK), F32),
            pltpu.SMEM((TILES,), jnp.int32),
            pltpu.SMEM((TILES,), jnp.int32),
        ],
        compiler_params=params(),
        name="backward",
    )(own, near, asked, far_own, far_other, mixed, stat)


def weight_term_body(mixed, other, branch, out_ref, total):
    step = pl.program_id(0)
    side = core()
    blocks_here = []
    for at in range(2):
        block = 2 * step + (side if at == 0 else 1 - side)
        place = lax.rem(block, SIDE)
        foreign = jnp.where(block // SIDE == side, 0, 1)
        blocks_here.append(pick(foreign, mixed[place].astype(F32), other[place].astype(F32)))
    right = jnp.concatenate(blocks_here, 1).astype(BF)
    left = jnp.concatenate([branch[0, 0], branch[0, 1]], 1)
    term = lax.dot_general(left, right, (((1,), (1,)), ((), ())), preferred_element_type=F32)

    @pl.when(step == 0)
    def _():
        total[...] = term

    @pl.when(step > 0)
    def _():
        total[...] += term

    @pl.when(step == HEADS - 1)
    def _():
        whole = jnp.concatenate([total[...], jnp.zeros((WIDTH // 2, TOK - FULL), F32)], 1)
        out_ref[...] = whole.astype(BF).reshape(PLANES, SHARE, TOK)


def weight_term(mixed, other, branch):
    return pl.pallas_call(
        weight_term_body,
        grid=(HEADS,),
        out_shape=jax.ShapeDtypeStruct((PLANES, SHARE, TOK), BF),
        in_specs=[
            pl.BlockSpec((SIDE, FULL, TOK), lambda i: (0, 0, 0)),
            pl.BlockSpec((SIDE, FULL, TOK), lambda i: (0, 0, 0)),
            pl.BlockSpec((1, 2, WIDTH // 2, TOK), lambda i: (i, 0, 0, 0)),
        ],
        out_specs=pl.BlockSpec((PLANES, SHARE, TOK), lambda i: (0, 0, 0)),
        scratch_shapes=[pltpu.VMEM((WIDTH // 2, FULL), F32)],
        compiler_params=params(),
        cost_estimate=cost(6),
        name="weight_term",
    )(mixed, other, branch)


def join_body(
    keep, got, keep_near, got_near, got_same, got_cross, term, term1, term2, term3, out_ref, total, pairs
):
    side = core()
    plane = lax.axis_index("dp") // PLANE
    total[0:SHARE] = sum(one.astype(F32) for one in (term[plane], term1[...], term2[...], term3[...]))
    total[SHARE:] = jnp.zeros((8, TOK), F32)
    mine, others = SIDE * side, SIDE * (1 - side)
    for block in range(SIDE):
        pairs[mine + block] = keep[block, FULL:].astype(F32)
        pairs[others + block] = got[block, FULL:].astype(F32)
    late, early = (SIDE - EDGE) * side, (SIDE - EDGE) * (1 - side)
    for block in range(EDGE):
        pairs[others + late + block] += keep_near[block].astype(F32)
        pairs[mine + early + block] += got_near[block].astype(F32)
    for block in range(EDGE):
        pairs[others + early + block] += got_same[block].astype(F32)
        pairs[mine + late + block] += got_cross[block].astype(F32)
    for block in range(SIDE):
        tail = total[block * FINAL : block * FINAL + 16, :]
        for start, asked in ((mine, keep), (others, got)):
            whole = [asked[block, 0:FULL].astype(F32), pairs[start + block], tail]
            out_ref[start + block] = jnp.concatenate(whole, 0).astype(BF)


def join(*values):
    return pl.pallas_call(
        join_body,
        out_shape=jax.ShapeDtypeStruct((PLANE, 2 * FULL + 16, TOK), BF),
        in_specs=[WHOLE] * 10,
        out_specs=WHOLE,
        scratch_shapes=[pltpu.VMEM((SHARE + 8, TOK), F32), pltpu.VMEM((PLANE, FULL, TOK), F32)],
        compiler_params=params(),
        cost_estimate=cost(3),
        name="join",
    )(*values)


def finish_body(packed, residual, tags, gate, weight, bias, out_ref, dq_ref, dk_ref, dv_ref, dw_ref):
    def rows(at):
        low = slice(at * HALF, (at + 1) * HALF)
        high = slice(at * HALF, at * HALF + HEAD_DIM - HALF)
        parts = []
        for head in range(HEADS):
            parts += [packed[2 * head].astype(F32)[low], packed[2 * head + 1].astype(F32)[high]]
        return jnp.concatenate(parts, 0).T.astype(BF)

    gate_rows = lax.dot_general(
        clip_onehot(tags), gate[...], (((0,), (0,)), ((), ())),
        precision=lax.Precision.HIGHEST, preferred_element_type=F32,
    )
    projected = mm(rows(0), weight[...]) + bias[...].reshape(1, WIDTH)
    out_ref[...] = (residual[...].astype(F32) + gate_rows * projected).astype(BF)
    dq_ref[...] = rows(1)
    dk_ref[...] = rows(2)
    dv_ref[...] = rows(3)
    source = lax.rem(lax.axis_index("dp"), PLANE) // SIDE
    tails = [packed[2 * head + source, 2 * FULL :].astype(F32)[:, 0:HEAD_DIM] for head in range(HEADS)]
    dw_ref[...] = jnp.concatenate(tails, 1)[0:FINAL]


def finish(packed, residual, tags, gate, weight, bias):
    return pl.pallas_call(
        finish_body,
        out_shape=(jax.ShapeDtypeStruct((TOK, WIDTH), BF),) * 4 + (jax.ShapeDtypeStruct((FINAL, WIDTH), F32),),
        in_specs=[WHOLE] * 6,
        out_specs=(WHOLE,) * 5,
        compiler_params=params(),
        cost_estimate=cost(4),
        name="finish",
    )(packed, residual, tags, gate, weight, bias)


def sent(values, target):
    pairs = [(i, target(i)) for i in range(DEVICES)]
    return lax.ppermute(values, "dp", [(i, j) for i, j in pairs if 0 <= j < DEVICES])


def other_core(device):
    return device ^ 1


def same_out(device):
    return device + PLANE if device % 2 == 0 else device - PLANE


def same_back(device):
    return device - PLANE if device % 2 == 0 else device + PLANE


def cross(device):
    return device - PLANE + 1 if device % 2 == 0 else device + PLANE - 1


def planes_on(count):
    return lambda device: (device + count * PLANE) % DEVICES


def traded(values):
    groups = [[plane * PLANE + i for i in range(PLANE)] for plane in range(PLANES)]
    return lax.all_to_all(values, "dp", 0, 0, axis_index_groups=groups, tiled=True)


def some_blocks(values, start, rows, count):
    return lax.dynamic_slice(values, (start, rows, 0), (count, FULL, TOK))


def shards(query, key, value, residual, tags, gate, weight, bias, out_grad):
    me = lax.axis_index("dp")
    side, plane = me % 2, me // PLANE
    chunk, branch, branch_away = pack(query, key, value, out_grad, tags, gate, weight)
    branch = jnp.stack([branch, sent(branch_away, other_core)])
    cores = [[plane * PLANE + 2 * chip + at for chip in range(HEADS)] for plane in range(PLANES) for at in range(2)]
    gathered = lax.all_gather(branch, "dp", axis=0, axis_index_groups=cores, tiled=False)
    own = traded(chunk)
    near = sent(some_blocks(own, (SIDE - EDGE) * (1 - side), 0, NEAR), other_core)
    asked = sent(some_blocks(own, SIDE * (1 - side), FULL, SIDE), other_core)
    last = PLANE - EDGE
    far_own = sent(some_blocks(own, last * (1 - side), 0, EDGE), same_out)
    far_other = sent(some_blocks(own, last * side, 0, EDGE), cross)
    mixed, stat = forward(own, near, asked, far_own, far_other)
    mixed_other = sent(mixed, other_core)
    keep, give, keep_near, give_near, keep_far, give_far = backward(
        own, near, asked, far_own, far_other, mixed, stat
    )
    got = sent(give, other_core)
    got_near = sent(give_near, other_core)
    got_same = sent(keep_far, same_back)
    got_cross = sent(give_far, cross)
    term = weight_term(mixed, mixed_other, gathered)
    terms = [sent(lax.dynamic_index_in_dim(term, (plane + k) % PLANES, 0, False), planes_on(k)) for k in (1, 2, 3)]
    packed = traded(join(keep, got, keep_near, got_near, got_same, got_cross, term, *terms))
    block_out, dq, dk, dv, dw = finish(packed, residual, tags, gate, weight, bias)
    return block_out, dq, dk, dv, dw.T


def solution(mesh):
    rows = P("dp", None)
    in_specs = (rows, rows, rows, rows, P("dp"), P(), P(), P(), rows)
    out_specs = (rows,) * 4 + (P(None, "dp"),)
    return jax.shard_map(shards, mesh=mesh, in_specs=in_specs, out_specs=out_specs, check_vma=False)
```

```python
import math

import jax
import jax.numpy as jnp
from jax import lax
from jax.experimental import pallas as pl
from jax.experimental.pallas import tpu as pltpu
from jax.sharding import PartitionSpec as P

HEADS = 16
HEAD_DIM = 72
WIDTH = HEADS * HEAD_DIM
TOK = 128
DEVICES = 128
PLANES = 4
PLANE = 32
SIDE = 16
EDGE = 7
SPAN = SIDE + 2 * EDGE
NEAR = SIDE + EDGE
TILE = 256
TILES = SIDE * TOK // TILE
PART = TILE // TOK
STEP = 4
ROOM = SPAN + STEP - 1
CHUNKS = 5
HALF = 40
FULL = 2 * HALF
FINAL = WIDTH // DEVICES
CHIPS = 4
SHARE = WIDTH // PLANES // 2
CLIPS = 32
SCALE = 1.0 / math.sqrt(HEAD_DIM)
SCALE2 = SCALE / math.log(2.0)
FAR = -1e30
BF = jnp.bfloat16
F32 = jnp.float32

WHOLE = pl.BlockSpec(memory_space=pltpu.VMEM)


def params(mebibytes):
    return pltpu.CompilerParams(vmem_limit_bytes=mebibytes * 1024 * 1024)


def cost(micros):
    return pl.CostEstimate(flops=int(micros * 4e8), bytes_accessed=int(micros * 2e6), transcendentals=0)


def mm(left, right):
    return jnp.dot(left, right, preferred_element_type=F32)


def clip_onehot(tags):
    ids = lax.broadcasted_iota(jnp.int32, (CLIPS, TOK), 0)
    return (ids == tags[...].reshape(1, TOK)).astype(F32)


def core():
    return lax.axis_index("dp") % 2


def pick(flag, first, second):
    return jnp.where(jnp.full(first.shape, flag, jnp.int32) == 0, first, second)


def pack_body(query, key, value, out_grad, tags, gate, weight, chunk_ref, mine_ref, theirs_ref):
    gate_t = lax.dot_general(
        gate[...], clip_onehot(tags), (((0,), (0,)), ((), ())),
        precision=lax.Precision.HIGHEST, preferred_element_type=F32,
    )
    branch_t = (out_grad[...].astype(F32).T * gate_t).astype(BF)
    grad_t = mm(weight[...], branch_t)
    wide = branch_t.astype(F32)
    halves = []
    for side in range(2):
        starts = [(2 * plane + side) * SHARE for plane in range(PLANES)]
        halves.append(jnp.concatenate([wide[start : start + SHARE] for start in starts], 0))
    side = core()
    mine_ref[0] = pick(side, halves[0], halves[1]).astype(BF)
    mine_ref[1] = jnp.zeros((WIDTH // 2, TOK), BF)
    theirs_ref[...] = pick(side, halves[1], halves[0]).astype(BF)
    key_t = key[...].astype(F32).T
    value_t = value[...].astype(F32).T
    query_t = query[...].astype(F32).T
    tag_rows = jnp.broadcast_to(tags[...].reshape(1, TOK).astype(F32) + 1.0, (8, TOK))
    blank = jnp.zeros((8, TOK), F32)
    for head in range(HEADS):
        start = head * HEAD_DIM
        low, high = slice(start, start + HALF), slice(start + HALF, start + HEAD_DIM)
        whole = [key_t[low], value_t[low], query_t[low], grad_t[low]]
        chunk_ref[2 * head] = jnp.concatenate(whole, 0).astype(BF)
        whole = [key_t[high], tag_rows, value_t[high], blank, query_t[high], blank, grad_t[high], blank]
        chunk_ref[2 * head + 1] = jnp.concatenate(whole, 0).astype(BF)


def pack(query, key, value, out_grad, tags, gate, weight):
    half = jax.ShapeDtypeStruct((WIDTH // 2, TOK), BF)
    room = jax.ShapeDtypeStruct((2, WIDTH // 2, TOK), BF)
    return pl.pallas_call(
        pack_body,
        out_shape=(jax.ShapeDtypeStruct((PLANE, 2 * FULL, TOK), BF), room, half),
        in_specs=[WHOLE] * 7,
        out_specs=(WHOLE,) * 3,
        compiler_params=params(24),
        cost_estimate=cost(5),
        name="pack",
    )(query, key, value, out_grad, tags, gate, weight)


def filled(piece, extra):
    rows = [piece] + extra
    have = sum(part.shape[0] for part in rows)
    if have < TOK:
        rows.append(jnp.zeros((TOK - have, TOK), F32))
    return jnp.concatenate(rows, 0)


def natural(side, own, other):
    own, other = own.astype(F32), other.astype(F32)
    low, high = pick(side, own, other), pick(side, other, own)
    return [jnp.concatenate([low[rows], high[rows]], 0) for rows in (slice(0, HALF), slice(HALF, FULL))]


def window(side, own, near, far_own, far_other):
    for block in range(NEAR):
        at = block + EDGE * (1 - side)
        yield (at,) + tuple(natural(side, own[block + (SIDE - EDGE) * side, 0:FULL], near[block]))
    for block in range(EDGE):
        yield (block + NEAR * side,) + tuple(natural(side, far_own[block], far_other[block]))


def token_rows(block):
    return pl.ds(pl.multiple_of(block * TOK, TOK), TOK)


def same_clip(clip, same, other):
    ids = lax.broadcasted_iota(jnp.int32, (CLIPS, TOK), 0).astype(F32) + 1.0
    return jnp.where(ids == clip, same, other)


def lay_out_keys(block, key, key_n, key_t, clips):
    clip = key[HEAD_DIM : HEAD_DIM + 1]
    clips[block] = key[HEAD_DIM:]
    held = filled(key[0:HEAD_DIM], [same_clip(clip, 0.0, FAR)])
    key_n[token_rows(block), :] = held.T.astype(BF)
    if key_t is not None:
        key_t[block] = jnp.concatenate([key[0:HEAD_DIM], jnp.zeros((8, TOK), F32)], 0).astype(BF)


def key_padding(key_n, key_t):
    rows = slice(SPAN * TOK, ROOM * TOK)
    lane = lax.broadcasted_iota(jnp.int32, ((ROOM - SPAN) * TOK, TOK), 1)
    key_n[rows, :] = jnp.where((lane >= HEAD_DIM) & (lane < HEAD_DIM + CLIPS), FAR, 0.0).astype(BF)
    if key_t is not None:
        for block in range(SPAN, ROOM):
            key_t[block] = jnp.zeros((80, TOK), BF)


def key_ranges(clips, first_ref, count_ref):
    rows = [clips[block][0:1] for block in range(SPAN)]
    rows = [jnp.where(row == 0.0, 100.0, row) if at >= NEAR else row for at, row in enumerate(rows)]
    rows = jnp.concatenate(rows + [jnp.full((32 - SPAN, TOK), 100.0, F32)], 0)
    least = jnp.min(rows, axis=1, keepdims=True)
    most = jnp.max(rows, axis=1, keepdims=True)
    for tile in range(TILES):
        start = EDGE + tile * PART
        low, high = least[start : start + 1], most[start + PART - 1 : start + PART]
        first = jnp.sum(jnp.where(most < low, 1.0, 0.0)).astype(jnp.int32)
        end = jnp.sum(jnp.where(least <= high, 1.0, 0.0)).astype(jnp.int32)
        first_ref[tile] = first
        count_ref[tile] = (end - first + STEP - 1) // STEP


def side_by_side(ref, start):
    return jnp.concatenate([ref[start + at] for at in range(STEP)], 1)


def blocks(first, step):
    start = first + step * STEP
    return start, pl.ds(pl.multiple_of(start * TOK, TOK), STEP * TOK)


def attend_body(
    own, near, asked, far_own, far_other,
    mixed_ref, keep_ref, give_ref, keep_near_ref, give_near_ref, keep_far_ref, give_far_ref,
    key_n, key_t, value_n, value_t, query_t, query_n, grad_t, grad_n, held, mixed_t, dq, dk, dv,
    clips, first_ref, count_ref,
):
    side = core()
    for at, key, value in window(side, own, near, far_own, far_other):
        lay_out_keys(at, key, key_n, key_t, clips)
        value = filled(value[0:HEAD_DIM], [jnp.ones((8, TOK), F32)])
        value_n[token_rows(at), :] = value.T.astype(BF)
        value_t[at] = value[0:80].astype(BF)
    value_n[SPAN * TOK :, :] = jnp.zeros(((ROOM - SPAN) * TOK, TOK), BF)
    for block in range(SPAN, ROOM):
        value_t[block] = jnp.zeros((80, TOK), BF)
    key_padding(key_n, key_t)
    for block in range(SIDE):
        tile, cols = block // PART, slice((block % PART) * TOK, (block % PART + 1) * TOK)
        query, grad = natural(side, own[SIDE * side + block, FULL:], asked[block])
        query = filled(query[0:HEAD_DIM], [same_clip(clips[EDGE + block][0:1], 1.0, 0.0)])
        query_t[tile, :, cols] = query.astype(BF)
        query_n[tile, cols, :] = query.T.astype(BF)
        grad = filled(grad, [])
        grad_t[tile, :, cols] = grad.astype(BF)
        grad_n[tile, cols, :] = grad.T.astype(BF)
    key_ranges(clips, first_ref, count_ref)
    dk[...] = jnp.zeros_like(dk)
    dv[...] = jnp.zeros_like(dv)

    def query_step(tile, carry):
        first, count = first_ref[tile], count_ref[tile]

        def score_step(step, top):
            scores = mm(key_n[blocks(first, step)[1], :], query_t[tile])
            held[step] = scores
            return jnp.maximum(top, jnp.max(scores, axis=0, keepdims=True))

        top = lax.fori_loop(0, count, score_step, jnp.full((1, TILE), 2.0 * FAR, F32))

        def value_step(step, total):
            weights = jnp.exp2((held[step] - top) * SCALE2)
            held[step] = weights
            return total + mm(side_by_side(value_t, blocks(first, step)[0]), weights.astype(BF))

        total = lax.fori_loop(0, count, value_step, jnp.zeros((80, TILE), F32))
        inverse = 1.0 / total[HEAD_DIM : HEAD_DIM + 1]
        mixed = jnp.concatenate([total[0:HEAD_DIM] * inverse, jnp.zeros((8, TILE), F32)], 0).astype(BF)
        grad = grad_t[tile]
        delta = jnp.sum(mixed.astype(F32) * grad[0:FULL].astype(F32), axis=0, keepdims=True)
        mixed_t[tile] = mixed

        def grad_step(step, total):
            start, rows = blocks(first, step)
            prob = held[step] * inverse
            pull = mm(value_n[rows, :], grad)
            dv[rows, :] += mm(prob.astype(BF), grad_n[tile])
            score_grad = (prob * (pull - delta)).astype(BF)
            dk[rows, :] += mm(score_grad, query_n[tile])
            return total + mm(side_by_side(key_t, start), score_grad)

        dq[tile] = lax.fori_loop(0, count, grad_step, jnp.zeros((80, TILE), F32)) * SCALE
        return carry

    lax.fori_loop(0, TILES, query_step, 0)

    def halves(wholes):
        low = jnp.concatenate([whole[0:HALF] for whole in wholes], 0)
        high = jnp.concatenate([whole[HALF:] for whole in wholes], 0)
        return pick(side, low, high).astype(BF), pick(side, high, low).astype(BF)

    def key_grads(at):
        rows = token_rows(at)
        return [dk[rows, :].T[0:FULL] * SCALE, dv[rows, :].T[0:FULL]]

    for block in range(SIDE):
        tile, cols = block // PART, slice((block % PART) * TOK, (block % PART + 1) * TOK)
        mixed = mixed_t[tile, :, cols]
        mixed_ref[block] = mixed
        wholes = [mixed.astype(F32), dq[tile, :, cols]] + key_grads(EDGE + block)
        keep_ref[block], give_ref[block] = halves(wholes)
    for block in range(EDGE):
        keep_near_ref[block], give_near_ref[block] = halves(key_grads(block + NEAR * (1 - side)))
        keep_far_ref[block], give_far_ref[block] = halves(key_grads(block + NEAR * side))


def attend(own, near, asked, far_own, far_other):
    whole = jax.ShapeDtypeStruct((SIDE, 2 * FULL, TOK), BF)
    edge = jax.ShapeDtypeStruct((EDGE, FULL, TOK), BF)
    row_form = pltpu.VMEM((ROOM * TOK, TOK), BF)
    column_form = pltpu.VMEM((ROOM, 80, TOK), BF)
    return pl.pallas_call(
        attend_body,
        out_shape=(jax.ShapeDtypeStruct((SIDE, FULL, TOK), BF), whole, whole, edge, edge, edge, edge),
        in_specs=[WHOLE] * 5,
        out_specs=(WHOLE,) * 7,
        cost_estimate=cost(20),
        scratch_shapes=[
            row_form, column_form, row_form, column_form,
            pltpu.VMEM((TILES, TOK, TILE), BF), pltpu.VMEM((TILES, TILE, TOK), BF),
            pltpu.VMEM((TILES, TOK, TILE), BF), pltpu.VMEM((TILES, TILE, TOK), BF),
            pltpu.VMEM((CHUNKS, STEP * TOK, TILE), F32),
            pltpu.VMEM((TILES, FULL, TILE), BF),
            pltpu.VMEM((TILES, FULL, TILE), F32),
            pltpu.VMEM((ROOM * TOK, TOK), F32),
            pltpu.VMEM((ROOM * TOK, TOK), F32),
            pltpu.VMEM((SPAN, 8, TOK), F32),
            pltpu.SMEM((TILES,), jnp.int32),
            pltpu.SMEM((TILES,), jnp.int32),
        ],
        compiler_params=params(32),
        name="attend",
    )(own, near, asked, far_own, far_other)


def weight_term_body(mixed, other, branch, *refs):
    out_refs, total = refs[:PLANES], refs[PLANES]
    step = pl.program_id(0)
    side = core()
    left, right = [], []
    for chip in range(CHIPS):
        for at in range(2):
            block = 2 * (CHIPS * step + chip) + (side if at == 0 else 1 - side)
            place = lax.rem(block, SIDE)
            foreign = jnp.where(block // SIDE == side, 0, 1)
            right.append(pick(foreign, mixed[place].astype(F32), other[place].astype(F32)))
            left.append(branch[chip, at])
    term = lax.dot_general(
        jnp.concatenate(left, 1), jnp.concatenate(right, 1).astype(BF), (((1,), (1,)), ((), ())),
        preferred_element_type=F32,
    )

    @pl.when(step == 0)
    def _():
        total[:, 0:FULL] = term
        total[:, FULL:] = jnp.zeros((WIDTH // 2, TOK - FULL), F32)

    @pl.when(step > 0)
    def _():
        total[:, 0:FULL] += term

    @pl.when(step == HEADS // CHIPS - 1)
    def _():
        plane = lax.axis_index("dp") // PLANE
        for away in range(PLANES):
            start = pl.multiple_of(lax.rem(plane + away, PLANES) * SHARE, 8)
            out_refs[away][...] = total[pl.ds(start, SHARE), :].astype(BF)


def weight_term(mixed, other, branch):
    share = pl.BlockSpec((SHARE, TOK), lambda i: (0, 0))
    held = pl.BlockSpec((SIDE, FULL, TOK), lambda i: (0, 0, 0))
    return pl.pallas_call(
        weight_term_body,
        grid=(HEADS // CHIPS,),
        out_shape=(jax.ShapeDtypeStruct((SHARE, TOK), BF),) * PLANES,
        in_specs=[held, held, pl.BlockSpec((CHIPS, 2, WIDTH // 2, TOK), lambda i: (i, 0, 0, 0))],
        out_specs=(share,) * PLANES,
        scratch_shapes=[pltpu.VMEM((WIDTH // 2, TOK), F32)],
        compiler_params=params(24),
        cost_estimate=cost(5),
        name="weight_term",
    )(mixed, other, branch)


def join_body(
    keep, got, keep_near, got_near, got_same, got_cross, term, term1, term2, term3, out_ref, total, pairs
):
    side = core()
    total[0:SHARE] = sum(one[...].astype(F32) for one in (term, term1, term2, term3))
    total[SHARE:] = jnp.zeros((8, TOK), F32)
    mine, others = SIDE * side, SIDE * (1 - side)
    for block in range(SIDE):
        pairs[mine + block] = keep[block, FULL:].astype(F32)
        pairs[others + block] = got[block, FULL:].astype(F32)
    late, early = (SIDE - EDGE) * side, (SIDE - EDGE) * (1 - side)
    for block in range(EDGE):
        pairs[others + late + block] += keep_near[block].astype(F32)
        pairs[mine + early + block] += got_near[block].astype(F32)
    for block in range(EDGE):
        pairs[others + early + block] += got_same[block].astype(F32)
        pairs[mine + late + block] += got_cross[block].astype(F32)
    for block in range(SIDE):
        tail = total[block * FINAL : block * FINAL + 16, :]
        for start, asked in ((mine, keep), (others, got)):
            whole = [asked[block, 0:FULL].astype(F32), pairs[start + block], tail]
            out_ref[start + block] = jnp.concatenate(whole, 0).astype(BF)


def join(*values):
    return pl.pallas_call(
        join_body,
        out_shape=jax.ShapeDtypeStruct((PLANE, 2 * FULL + 16, TOK), BF),
        in_specs=[WHOLE] * 10,
        out_specs=WHOLE,
        scratch_shapes=[pltpu.VMEM((SHARE + 8, TOK), F32), pltpu.VMEM((PLANE, FULL, TOK), F32)],
        compiler_params=params(24),
        cost_estimate=cost(3),
        name="join",
    )(*values)


def finish_body(packed, residual, tags, gate, weight, bias, out_ref, dq_ref, dk_ref, dv_ref, dw_ref):
    def rows(at):
        low = slice(at * HALF, (at + 1) * HALF)
        high = slice(at * HALF, at * HALF + HEAD_DIM - HALF)
        parts = []
        for head in range(HEADS):
            parts += [packed[2 * head].astype(F32)[low], packed[2 * head + 1].astype(F32)[high]]
        return jnp.concatenate(parts, 0).T.astype(BF)

    gate_rows = lax.dot_general(
        clip_onehot(tags), gate[...], (((0,), (0,)), ((), ())),
        precision=lax.Precision.HIGHEST, preferred_element_type=F32,
    )
    projected = mm(rows(0), weight[...]) + bias[...].reshape(1, WIDTH)
    out_ref[...] = (residual[...].astype(F32) + gate_rows * projected).astype(BF)
    dq_ref[...] = rows(1)
    dk_ref[...] = rows(2)
    dv_ref[...] = rows(3)
    source = lax.rem(lax.axis_index("dp"), PLANE) // SIDE
    tails = [packed[2 * head + source, 2 * FULL :].astype(F32)[:, 0:HEAD_DIM] for head in range(HEADS)]
    dw_ref[...] = jnp.concatenate(tails, 1)[0:FINAL]


def finish(packed, residual, tags, gate, weight, bias):
    return pl.pallas_call(
        finish_body,
        out_shape=(jax.ShapeDtypeStruct((TOK, WIDTH), BF),) * 4 + (jax.ShapeDtypeStruct((FINAL, WIDTH), F32),),
        in_specs=[WHOLE] * 6,
        out_specs=(WHOLE,) * 5,
        compiler_params=params(24),
        cost_estimate=cost(4),
        name="finish",
    )(packed, residual, tags, gate, weight, bias)


def sent(values, target):
    pairs = [(i, target(i)) for i in range(DEVICES)]
    return lax.ppermute(values, "dp", [(i, j) for i, j in pairs if 0 <= j < DEVICES])


def other_core(device):
    return device ^ 1


def same_out(device):
    return device + PLANE if device % 2 == 0 else device - PLANE


def same_back(device):
    return device - PLANE if device % 2 == 0 else device + PLANE


def cross(device):
    return device - PLANE + 1 if device % 2 == 0 else device + PLANE - 1


def planes_on(count):
    return lambda device: (device + count * PLANE) % DEVICES


def traded(values):
    groups = [[plane * PLANE + i for i in range(PLANE)] for plane in range(PLANES)]
    return lax.all_to_all(values, "dp", 0, 0, axis_index_groups=groups, tiled=True)


def some_blocks(values, start, rows, count):
    return lax.dynamic_slice(values, (start, rows, 0), (count, FULL, TOK))


def shards(query, key, value, residual, tags, gate, weight, bias, out_grad):
    me = lax.axis_index("dp")
    side = me % 2
    chunk, branch, branch_away = pack(query, key, value, out_grad, tags, gate, weight)
    branch = lax.dynamic_update_slice(branch, sent(branch_away, other_core)[None], (1, 0, 0))
    cores = [[plane * PLANE + 2 * chip + at for chip in range(HEADS)] for plane in range(PLANES) for at in range(2)]
    gathered = lax.all_gather(branch, "dp", axis=0, axis_index_groups=cores, tiled=False)
    own = traded(chunk)
    near = sent(some_blocks(own, (SIDE - EDGE) * (1 - side), 0, NEAR), other_core)
    asked = sent(some_blocks(own, SIDE * (1 - side), FULL, SIDE), other_core)
    last = PLANE - EDGE
    far_own = sent(some_blocks(own, last * (1 - side), 0, EDGE), same_out)
    far_other = sent(some_blocks(own, last * side, 0, EDGE), cross)
    mixed, keep, give, keep_near, give_near, keep_far, give_far = attend(own, near, asked, far_own, far_other)
    mixed_other = sent(mixed, other_core)
    got = sent(give, other_core)
    got_near = sent(give_near, other_core)
    got_same = sent(keep_far, same_back)
    got_cross = sent(give_far, cross)
    term, *terms = weight_term(mixed, mixed_other, gathered)
    terms = [sent(one, planes_on(away + 1)) for away, one in enumerate(terms)]
    packed = traded(join(keep, got, keep_near, got_near, got_same, got_cross, term, *terms))
    block_out, dq, dk, dv, dw = finish(packed, residual, tags, gate, weight, bias)
    return block_out, dq, dk, dv, dw.T


def solution(mesh):
    rows = P("dp", None)
    in_specs = (rows, rows, rows, rows, P("dp"), P(), P(), P(), rows)
    out_specs = (rows,) * 4 + (P(None, "dp"),)
    return jax.shard_map(shards, mesh=mesh, in_specs=in_specs, out_specs=out_specs, check_vma=False)
```

```python
import math

import jax
import jax.numpy as jnp
from jax import lax
from jax.experimental import pallas as pl
from jax.experimental.pallas import tpu as pltpu
from jax.sharding import PartitionSpec as P

HEADS = 16
HEAD_DIM = 72
WIDTH = HEADS * HEAD_DIM
TOK = 128
DEVICES = 128
PLANES = 4
PLANE = 32
SIDE = 16
EDGE = 7
SPAN = SIDE + 2 * EDGE
NEAR = SIDE + EDGE
TILE = 256
TILES = SIDE * TOK // TILE
PART = TILE // TOK
STEP = 4
ROOM = SPAN + STEP - 1
CHUNKS = 5
HALF = 40
FULL = 2 * HALF
FINAL = WIDTH // DEVICES
CHIPS = 4
SHARE = WIDTH // PLANES // 2
CLIPS = 32
SCALE = 1.0 / math.sqrt(HEAD_DIM)
SCALE2 = SCALE / math.log(2.0)
FAR = -1e30
BF = jnp.bfloat16
F32 = jnp.float32

WHOLE = pl.BlockSpec(memory_space=pltpu.VMEM)
FAR_AWAY = pl.BlockSpec(memory_space=pltpu.HBM)


def params(mebibytes):
    return pltpu.CompilerParams(vmem_limit_bytes=mebibytes * 1024 * 1024)


def cost(micros):
    return pl.CostEstimate(flops=int(micros * 4e8), bytes_accessed=int(micros * 2e6), transcendentals=0)


def mm(left, right):
    return jnp.dot(left, right, preferred_element_type=F32)


def clip_onehot(tags):
    ids = lax.broadcasted_iota(jnp.int32, (CLIPS, TOK), 0)
    return (ids == tags[...].reshape(1, TOK)).astype(F32)


def core():
    return lax.axis_index("dp") % 2


def pick(flag, first, second):
    return jnp.where(jnp.full(first.shape, flag, jnp.int32) == 0, first, second)


def branch_body(out_grad, tags, gate, branch_ref, mine_ref, theirs_ref):
    gate_t = lax.dot_general(
        gate[...], clip_onehot(tags), (((0,), (0,)), ((), ())),
        precision=lax.Precision.HIGHEST, preferred_element_type=F32,
    )
    branch_t = (out_grad[...].astype(F32).T * gate_t).astype(BF)
    branch_ref[...] = branch_t
    wide = branch_t.astype(F32)
    halves = []
    for side in range(2):
        starts = [(2 * plane + side) * SHARE for plane in range(PLANES)]
        halves.append(jnp.concatenate([wide[start : start + SHARE] for start in starts], 0))
    side = core()
    mine_ref[0] = pick(side, halves[0], halves[1]).astype(BF)
    mine_ref[1] = jnp.zeros((WIDTH // 2, TOK), BF)
    theirs_ref[...] = pick(side, halves[1], halves[0]).astype(BF)


def branch_columns(out_grad, tags, gate):
    return pl.pallas_call(
        branch_body,
        out_shape=(
            jax.ShapeDtypeStruct((WIDTH, TOK), BF),
            jax.ShapeDtypeStruct((2, WIDTH // 2, TOK), BF),
            jax.ShapeDtypeStruct((WIDTH // 2, TOK), BF),
        ),
        in_specs=[WHOLE] * 3,
        out_specs=(WHOLE,) * 3,
        compiler_params=params(56),
        cost_estimate=cost(2),
        name="branch_columns",
    )(out_grad, tags, gate)


def pack_body(query, key, value, tags, branch, weight, chunk_ref, weight_here, weight_sem):
    load = pltpu.make_async_copy(weight, weight_here, weight_sem)
    load.start()
    key_t = key[...].astype(F32).T
    value_t = value[...].astype(F32).T
    query_t = query[...].astype(F32).T
    tag_rows = jnp.broadcast_to(tags[...].reshape(1, TOK).astype(F32) + 1.0, (8, TOK))
    blank = jnp.zeros((8, TOK), F32)
    load.wait()
    grad_t = mm(weight_here[...], branch[...])
    for head in range(HEADS):
        start = head * HEAD_DIM
        low, high = slice(start, start + HALF), slice(start + HALF, start + HEAD_DIM)
        whole = [key_t[low], value_t[low], query_t[low], grad_t[low]]
        chunk_ref[2 * head] = jnp.concatenate(whole, 0).astype(BF)
        whole = [key_t[high], tag_rows, value_t[high], blank, query_t[high], blank, grad_t[high], blank]
        chunk_ref[2 * head + 1] = jnp.concatenate(whole, 0).astype(BF)


def pack(query, key, value, tags, branch, weight):
    return pl.pallas_call(
        pack_body,
        out_shape=jax.ShapeDtypeStruct((PLANE, 2 * FULL, TOK), BF),
        in_specs=[WHOLE] * 5 + [FAR_AWAY],
        out_specs=WHOLE,
        scratch_shapes=[pltpu.VMEM((WIDTH, WIDTH), BF), pltpu.SemaphoreType.DMA],
        compiler_params=params(52),
        cost_estimate=cost(4),
        name="pack",
    )(query, key, value, tags, branch, weight)


def filled(piece, extra):
    rows = [piece] + extra
    have = sum(part.shape[0] for part in rows)
    if have < TOK:
        rows.append(jnp.zeros((TOK - have, TOK), F32))
    return jnp.concatenate(rows, 0)


def natural(side, own, other):
    own, other = own.astype(F32), other.astype(F32)
    low, high = pick(side, own, other), pick(side, other, own)
    return [jnp.concatenate([low[rows], high[rows]], 0) for rows in (slice(0, HALF), slice(HALF, FULL))]


def window(side, own, near, far_own, far_other):
    for block in range(NEAR):
        at = block + EDGE * (1 - side)
        yield (at,) + tuple(natural(side, own[block + (SIDE - EDGE) * side, 0:FULL], near[block]))
    for block in range(EDGE):
        yield (block + NEAR * side,) + tuple(natural(side, far_own[block], far_other[block]))


def token_rows(block):
    return pl.ds(pl.multiple_of(block * TOK, TOK), TOK)


def same_clip(clip, same, other):
    ids = lax.broadcasted_iota(jnp.int32, (CLIPS, TOK), 0).astype(F32) + 1.0
    return jnp.where(ids == clip, same, other)


def lay_out_keys(block, key, key_n, key_t, clips):
    clip = key[HEAD_DIM : HEAD_DIM + 1]
    clips[block] = key[HEAD_DIM:]
    held = filled(key[0:HEAD_DIM], [same_clip(clip, 0.0, FAR)])
    key_n[token_rows(block), :] = held.T.astype(BF)
    if key_t is not None:
        key_t[block] = jnp.concatenate([key[0:HEAD_DIM], jnp.zeros((8, TOK), F32)], 0).astype(BF)


def key_padding(key_n, key_t):
    rows = slice(SPAN * TOK, ROOM * TOK)
    lane = lax.broadcasted_iota(jnp.int32, ((ROOM - SPAN) * TOK, TOK), 1)
    key_n[rows, :] = jnp.where((lane >= HEAD_DIM) & (lane < HEAD_DIM + CLIPS), FAR, 0.0).astype(BF)
    if key_t is not None:
        for block in range(SPAN, ROOM):
            key_t[block] = jnp.zeros((80, TOK), BF)


def key_ranges(clips, first_ref, count_ref):
    rows = [clips[block][0:1] for block in range(SPAN)]
    rows = [jnp.where(row == 0.0, 100.0, row) if at >= NEAR else row for at, row in enumerate(rows)]
    rows = jnp.concatenate(rows + [jnp.full((32 - SPAN, TOK), 100.0, F32)], 0)
    least = jnp.min(rows, axis=1, keepdims=True)
    most = jnp.max(rows, axis=1, keepdims=True)
    for tile in range(TILES):
        start = EDGE + tile * PART
        low, high = least[start : start + 1], most[start + PART - 1 : start + PART]
        first = jnp.sum(jnp.where(most < low, 1.0, 0.0)).astype(jnp.int32)
        end = jnp.sum(jnp.where(least <= high, 1.0, 0.0)).astype(jnp.int32)
        first_ref[tile] = first
        count_ref[tile] = (end - first + STEP - 1) // STEP


def side_by_side(ref, start):
    return jnp.concatenate([ref[start + at] for at in range(STEP)], 1)


def blocks(first, step):
    start = first + step * STEP
    return start, pl.ds(pl.multiple_of(start * TOK, TOK), STEP * TOK)


def attend_body(
    own, near, asked, far_own, far_other,
    mixed_ref, keep_ref, give_ref, keep_near_ref, give_near_ref, keep_far_ref, give_far_ref,
    key_n, key_t, value_n, value_t, query_t, query_n, grad_t, grad_n, held, mixed_t, dq, dk, dv,
    clips, first_ref, count_ref,
):
    side = core()
    for at, key, value in window(side, own, near, far_own, far_other):
        lay_out_keys(at, key, key_n, key_t, clips)
        value = filled(value[0:HEAD_DIM], [jnp.ones((8, TOK), F32)])
        value_n[token_rows(at), :] = value.T.astype(BF)
        value_t[at] = value[0:80].astype(BF)
    value_n[SPAN * TOK :, :] = jnp.zeros(((ROOM - SPAN) * TOK, TOK), BF)
    for block in range(SPAN, ROOM):
        value_t[block] = jnp.zeros((80, TOK), BF)
    key_padding(key_n, key_t)
    for block in range(SIDE):
        tile, cols = block // PART, slice((block % PART) * TOK, (block % PART + 1) * TOK)
        query, grad = natural(side, own[SIDE * side + block, FULL:], asked[block])
        query = filled(query[0:HEAD_DIM], [same_clip(clips[EDGE + block][0:1], 1.0, 0.0)])
        query_t[tile, :, cols] = query.astype(BF)
        query_n[tile, cols, :] = query.T.astype(BF)
        grad = filled(grad, [])
        grad_t[tile, :, cols] = grad.astype(BF)
        grad_n[tile, cols, :] = grad.T.astype(BF)
    key_ranges(clips, first_ref, count_ref)
    dk[...] = jnp.zeros_like(dk)
    dv[...] = jnp.zeros_like(dv)

    def query_step(tile, carry):
        first, count = first_ref[tile], count_ref[tile]

        def score_step(step, top):
            scores = mm(key_n[blocks(first, step)[1], :], query_t[tile])
            held[step] = scores
            return jnp.maximum(top, jnp.max(scores, axis=0, keepdims=True))

        top = lax.fori_loop(0, count, score_step, jnp.full((1, TILE), 2.0 * FAR, F32))

        def value_step(step, total):
            weights = jnp.exp2((held[step] - top) * SCALE2)
            held[step] = weights
            return total + mm(side_by_side(value_t, blocks(first, step)[0]), weights.astype(BF))

        total = lax.fori_loop(0, count, value_step, jnp.zeros((80, TILE), F32))
        inverse = 1.0 / total[HEAD_DIM : HEAD_DIM + 1]
        mixed = jnp.concatenate([total[0:HEAD_DIM] * inverse, jnp.zeros((8, TILE), F32)], 0).astype(BF)
        grad = grad_t[tile]
        delta = jnp.sum(mixed.astype(F32) * grad[0:FULL].astype(F32), axis=0, keepdims=True)
        mixed_t[tile] = mixed

        def grad_step(step, total):
            start, rows = blocks(first, step)
            prob = held[step] * inverse
            pull = mm(value_n[rows, :], grad)
            dv[rows, :] += mm(prob.astype(BF), grad_n[tile])
            score_grad = (prob * (pull - delta)).astype(BF)
            dk[rows, :] += mm(score_grad, query_n[tile])
            return total + mm(side_by_side(key_t, start), score_grad)

        dq[tile] = lax.fori_loop(0, count, grad_step, jnp.zeros((80, TILE), F32)) * SCALE
        return carry

    lax.fori_loop(0, TILES, query_step, 0)

    def halves(wholes):
        low = jnp.concatenate([whole[0:HALF] for whole in wholes], 0)
        high = jnp.concatenate([whole[HALF:] for whole in wholes], 0)
        return pick(side, low, high).astype(BF), pick(side, high, low).astype(BF)

    def key_grads(at):
        rows = token_rows(at)
        return [dk[rows, :].T[0:FULL] * SCALE, dv[rows, :].T[0:FULL]]

    for block in range(SIDE):
        tile, cols = block // PART, slice((block % PART) * TOK, (block % PART + 1) * TOK)
        mixed = mixed_t[tile, :, cols]
        mixed_ref[block] = mixed
        wholes = [mixed.astype(F32), dq[tile, :, cols]] + key_grads(EDGE + block)
        keep_ref[block], give_ref[block] = halves(wholes)
    for block in range(EDGE):
        keep_near_ref[block], give_near_ref[block] = halves(key_grads(block + NEAR * (1 - side)))
        keep_far_ref[block], give_far_ref[block] = halves(key_grads(block + NEAR * side))


def attend(own, near, asked, far_own, far_other):
    whole = jax.ShapeDtypeStruct((SIDE, 2 * FULL, TOK), BF)
    edge = jax.ShapeDtypeStruct((EDGE, FULL, TOK), BF)
    row_form = pltpu.VMEM((ROOM * TOK, TOK), BF)
    column_form = pltpu.VMEM((ROOM, 80, TOK), BF)
    return pl.pallas_call(
        attend_body,
        out_shape=(jax.ShapeDtypeStruct((SIDE, FULL, TOK), BF), whole, whole, edge, edge, edge, edge),
        in_specs=[WHOLE] * 5,
        out_specs=(WHOLE,) * 7,
        cost_estimate=cost(20),
        scratch_shapes=[
            row_form, column_form, row_form, column_form,
            pltpu.VMEM((TILES, TOK, TILE), BF), pltpu.VMEM((TILES, TILE, TOK), BF),
            pltpu.VMEM((TILES, TOK, TILE), BF), pltpu.VMEM((TILES, TILE, TOK), BF),
            pltpu.VMEM((CHUNKS, STEP * TOK, TILE), F32),
            pltpu.VMEM((TILES, FULL, TILE), BF),
            pltpu.VMEM((TILES, FULL, TILE), F32),
            pltpu.VMEM((ROOM * TOK, TOK), F32),
            pltpu.VMEM((ROOM * TOK, TOK), F32),
            pltpu.VMEM((SPAN, 8, TOK), F32),
            pltpu.SMEM((TILES,), jnp.int32),
            pltpu.SMEM((TILES,), jnp.int32),
        ],
        compiler_params=params(24),
        name="attend",
    )(own, near, asked, far_own, far_other)


def weight_term_body(mixed, other, branch, *refs):
    out_refs, (columns, sems) = refs[:PLANES], refs[PLANES:]
    loads = []
    for step in range(HEADS // CHIPS):
        chips = pl.ds(step * CHIPS, CHIPS)
        loads.append(pltpu.make_async_copy(branch.at[chips], columns.at[chips], sems.at[step]))
        loads[-1].start()
    side = core()
    right = []
    for block in range(2 * HEADS):
        place = lax.rem(2 * (block // 2) + (side if block % 2 == 0 else 1 - side), SIDE)
        foreign = jnp.where(side == block // SIDE, 0, 1)
        right.append(pick(foreign, mixed[place].astype(F32), other[place].astype(F32)).astype(BF))
    total = jnp.zeros((WIDTH // 2, FULL), F32)
    for step, load in enumerate(loads):
        load.wait()
        left = [columns[chip, at] for chip in range(step * CHIPS, (step + 1) * CHIPS) for at in range(2)]
        total += lax.dot_general(
            jnp.concatenate(left, 1), jnp.concatenate(right[2 * step * CHIPS : 2 * (step + 1) * CHIPS], 1),
            (((1,), (1,)), ((), ())), preferred_element_type=F32,
        )
    plane = lax.axis_index("dp") // PLANE
    for away in range(PLANES):
        share = total[0:SHARE]
        for at in range(1, PLANES):
            here = jnp.where(lax.rem(plane + away, PLANES) == at, 1, 0)
            share = pick(here, share, total[at * SHARE : (at + 1) * SHARE])
        out_refs[away][:, 0:FULL] = share.astype(BF)
        out_refs[away][:, FULL:] = jnp.zeros((SHARE, TOK - FULL), BF)


def weight_term(mixed, other, branch):
    return pl.pallas_call(
        weight_term_body,
        out_shape=(jax.ShapeDtypeStruct((SHARE, TOK), BF),) * PLANES,
        in_specs=[WHOLE, WHOLE, FAR_AWAY],
        out_specs=(WHOLE,) * PLANES,
        scratch_shapes=[
            pltpu.VMEM((HEADS, 2, WIDTH // 2, TOK), BF),
            pltpu.SemaphoreType.DMA((HEADS // CHIPS,)),
        ],
        compiler_params=params(60),
        cost_estimate=cost(4),
        name="weight_term",
    )(mixed, other, branch)


def join_body(
    keep, got, keep_near, got_near, got_same, got_cross, term, term1, term2, term3, out_ref, total, pairs
):
    side = core()
    total[0:SHARE] = sum(one[...].astype(F32) for one in (term, term1, term2, term3))
    total[SHARE:] = jnp.zeros((8, TOK), F32)
    mine, others = SIDE * side, SIDE * (1 - side)
    for block in range(SIDE):
        pairs[mine + block] = keep[block, FULL:].astype(F32)
        pairs[others + block] = got[block, FULL:].astype(F32)
    late, early = (SIDE - EDGE) * side, (SIDE - EDGE) * (1 - side)
    for block in range(EDGE):
        pairs[others + late + block] += keep_near[block].astype(F32)
        pairs[mine + early + block] += got_near[block].astype(F32)
    for block in range(EDGE):
        pairs[others + early + block] += got_same[block].astype(F32)
        pairs[mine + late + block] += got_cross[block].astype(F32)
    for block in range(SIDE):
        tail = total[block * FINAL : block * FINAL + 16, :]
        for start, asked in ((mine, keep), (others, got)):
            whole = [asked[block, 0:FULL].astype(F32), pairs[start + block], tail]
            out_ref[start + block] = jnp.concatenate(whole, 0).astype(BF)


def join(*values):
    return pl.pallas_call(
        join_body,
        out_shape=jax.ShapeDtypeStruct((PLANE, 2 * FULL + 16, TOK), BF),
        in_specs=[WHOLE] * 10,
        out_specs=WHOLE,
        scratch_shapes=[pltpu.VMEM((SHARE + 8, TOK), F32), pltpu.VMEM((PLANE, FULL, TOK), F32)],
        compiler_params=params(12),
        cost_estimate=cost(3),
        name="join",
    )(*values)


def finish_body(packed, residual, tags, gate, weight, bias, out_ref, dq_ref, dk_ref, dv_ref, dw_ref):
    def rows(at):
        low = slice(at * HALF, (at + 1) * HALF)
        high = slice(at * HALF, at * HALF + HEAD_DIM - HALF)
        parts = []
        for head in range(HEADS):
            parts += [packed[2 * head].astype(F32)[low], packed[2 * head + 1].astype(F32)[high]]
        return jnp.concatenate(parts, 0).T.astype(BF)

    gate_rows = lax.dot_general(
        clip_onehot(tags), gate[...], (((0,), (0,)), ((), ())),
        precision=lax.Precision.HIGHEST, preferred_element_type=F32,
    )
    projected = mm(rows(0), weight[...]) + bias[...].reshape(1, WIDTH)
    out_ref[...] = (residual[...].astype(F32) + gate_rows * projected).astype(BF)
    dq_ref[...] = rows(1)
    dk_ref[...] = rows(2)
    dv_ref[...] = rows(3)
    source = lax.rem(lax.axis_index("dp"), PLANE) // SIDE
    tails = [packed[2 * head + source, 2 * FULL :].astype(F32)[:, 0:HEAD_DIM] for head in range(HEADS)]
    dw_ref[...] = jnp.concatenate(tails, 1)[0:FINAL]


def finish(packed, residual, tags, gate, weight, bias):
    return pl.pallas_call(
        finish_body,
        out_shape=(jax.ShapeDtypeStruct((TOK, WIDTH), BF),) * 4 + (jax.ShapeDtypeStruct((FINAL, WIDTH), F32),),
        in_specs=[WHOLE] * 6,
        out_specs=(WHOLE,) * 5,
        compiler_params=params(16),
        cost_estimate=cost(4),
        name="finish",
    )(packed, residual, tags, gate, weight, bias)


def sent(values, target):
    pairs = [(i, target(i)) for i in range(DEVICES)]
    return lax.ppermute(values, "dp", [(i, j) for i, j in pairs if 0 <= j < DEVICES])


def other_core(device):
    return device ^ 1


def same_out(device):
    return device + PLANE if device % 2 == 0 else device - PLANE


def same_back(device):
    return device - PLANE if device % 2 == 0 else device + PLANE


def cross(device):
    return device - PLANE + 1 if device % 2 == 0 else device + PLANE - 1


def planes_on(count):
    return lambda device: (device + count * PLANE) % DEVICES


def traded(values):
    groups = [[plane * PLANE + i for i in range(PLANE)] for plane in range(PLANES)]
    return lax.all_to_all(values, "dp", 0, 0, axis_index_groups=groups, tiled=True)


def some_blocks(values, start, rows, count):
    return lax.dynamic_slice(values, (start, rows, 0), (count, FULL, TOK))


def shards(query, key, value, residual, tags, gate, weight, bias, out_grad):
    me = lax.axis_index("dp")
    side = me % 2
    whole_branch, branch, branch_away = branch_columns(out_grad, tags, gate)
    branch = lax.dynamic_update_slice(branch, sent(branch_away, other_core)[None], (1, 0, 0))
    cores = [[plane * PLANE + 2 * chip + at for chip in range(HEADS)] for plane in range(PLANES) for at in range(2)]
    gathered = lax.all_gather(branch, "dp", axis=0, axis_index_groups=cores, tiled=False)
    own = traded(pack(query, key, value, tags, whole_branch, weight))
    near = sent(some_blocks(own, (SIDE - EDGE) * (1 - side), 0, NEAR), other_core)
    asked = sent(some_blocks(own, SIDE * (1 - side), FULL, SIDE), other_core)
    last = PLANE - EDGE
    far_own = sent(some_blocks(own, last * (1 - side), 0, EDGE), same_out)
    far_other = sent(some_blocks(own, last * side, 0, EDGE), cross)
    mixed, keep, give, keep_near, give_near, keep_far, give_far = attend(own, near, asked, far_own, far_other)
    mixed_other = sent(mixed, other_core)
    got = sent(give, other_core)
    got_near = sent(give_near, other_core)
    got_same = sent(keep_far, same_back)
    got_cross = sent(give_far, cross)
    term, *terms = weight_term(mixed, mixed_other, gathered)
    terms = [sent(one, planes_on(away + 1)) for away, one in enumerate(terms)]
    packed = traded(join(keep, got, keep_near, got_near, got_same, got_cross, term, *terms))
    block_out, dq, dk, dv, dw = finish(packed, residual, tags, gate, weight, bias)
    return block_out, dq, dk, dv, dw.T


def solution(mesh):
    rows = P("dp", None)
    in_specs = (rows, rows, rows, rows, P("dp"), P(), P(), P(), rows)
    out_specs = (rows,) * 4 + (P(None, "dp"),)
    return jax.shard_map(shards, mesh=mesh, in_specs=in_specs, out_specs=out_specs, check_vma=False)
```

```python
import math

import jax
import jax.numpy as jnp
from jax import lax
from jax.experimental import pallas as pl
from jax.experimental.pallas import tpu as pltpu
from jax.sharding import PartitionSpec as P

HEADS = 16
HEAD_DIM = 72
WIDTH = HEADS * HEAD_DIM
TOK = 128
DEVICES = 128
PLANES = 4
PLANE = 32
SIDE = 16
EDGE = 7
SPAN = SIDE + 2 * EDGE
NEAR = SIDE + EDGE
TILE = 256
TILES = SIDE * TOK // TILE
PART = TILE // TOK
STEP = 4
ROOM = SPAN + STEP - 1
CHUNKS = 5
HALF = 40
FULL = 2 * HALF
FINAL = WIDTH // DEVICES
CHIPS = 4
SHARE = WIDTH // PLANES // 2
CLIPS = 32
SCALE = 1.0 / math.sqrt(HEAD_DIM)
SCALE2 = SCALE / math.log(2.0)
FAR = -1e30
BF = jnp.bfloat16
F32 = jnp.float32

WHOLE = pl.BlockSpec(memory_space=pltpu.VMEM)
FAR_AWAY = pl.BlockSpec(memory_space=pltpu.HBM)


def params(mebibytes):
    return pltpu.CompilerParams(vmem_limit_bytes=mebibytes * 1024 * 1024)


def cost(micros):
    return pl.CostEstimate(flops=int(micros * 4e8), bytes_accessed=int(micros * 2e6), transcendentals=0)


def mm(left, right):
    return jnp.dot(left, right, preferred_element_type=F32)


def clip_onehot(tags):
    ids = lax.broadcasted_iota(jnp.int32, (CLIPS, TOK), 0)
    return (ids == tags[...].reshape(1, TOK)).astype(F32)


def core():
    return lax.axis_index("dp") % 2


def pick(flag, first, second):
    return jnp.where(jnp.full(first.shape, flag, jnp.int32) == 0, first, second)


def branch_body(out_grad, tags, gate, branch_ref, mine_ref, theirs_ref):
    gate_t = lax.dot_general(
        gate[...], clip_onehot(tags), (((0,), (0,)), ((), ())),
        precision=lax.Precision.HIGHEST, preferred_element_type=F32,
    )
    branch_t = (out_grad[...].astype(F32).T * gate_t).astype(BF)
    branch_ref[...] = branch_t
    wide = branch_t.astype(F32)
    halves = []
    for side in range(2):
        starts = [(2 * plane + side) * SHARE for plane in range(PLANES)]
        halves.append(jnp.concatenate([wide[start : start + SHARE] for start in starts], 0))
    side = core()
    mine_ref[0] = pick(side, halves[0], halves[1]).astype(BF)
    mine_ref[1] = jnp.zeros((WIDTH // 2, TOK), BF)
    theirs_ref[...] = pick(side, halves[1], halves[0]).astype(BF)


def branch_columns(out_grad, tags, gate):
    return pl.pallas_call(
        branch_body,
        out_shape=(
            jax.ShapeDtypeStruct((WIDTH, TOK), BF),
            jax.ShapeDtypeStruct((2, WIDTH // 2, TOK), BF),
            jax.ShapeDtypeStruct((WIDTH // 2, TOK), BF),
        ),
        in_specs=[WHOLE] * 3,
        out_specs=(WHOLE,) * 3,
        compiler_params=params(56),
        cost_estimate=cost(2),
        name="branch_columns",
    )(out_grad, tags, gate)


def fill_body(_, got, out_ref, sem):
    load = pltpu.make_async_copy(got, out_ref.at[1], sem)
    load.start()
    load.wait()


def fill(branch, got):
    return pl.pallas_call(
        fill_body,
        out_shape=jax.ShapeDtypeStruct(branch.shape, BF),
        in_specs=[FAR_AWAY] * 2,
        out_specs=FAR_AWAY,
        input_output_aliases={0: 0},
        scratch_shapes=[pltpu.SemaphoreType.DMA],
        compiler_params=params(16),
        cost_estimate=cost(1),
        name="fill",
    )(branch, got)


def pack_body(query, key, value, tags, branch, weight, chunk_ref, weight_here, weight_sem):
    load = pltpu.make_async_copy(weight, weight_here, weight_sem)
    load.start()
    key_t = key[...].astype(F32).T
    value_t = value[...].astype(F32).T
    query_t = query[...].astype(F32).T
    tag_rows = jnp.broadcast_to(tags[...].reshape(1, TOK).astype(F32) + 1.0, (8, TOK))
    blank = jnp.zeros((8, TOK), F32)
    load.wait()
    grad_t = mm(weight_here[...], branch[...])
    for head in range(HEADS):
        start = head * HEAD_DIM
        low, high = slice(start, start + HALF), slice(start + HALF, start + HEAD_DIM)
        whole = [key_t[low], value_t[low], query_t[low], grad_t[low]]
        chunk_ref[2 * head] = jnp.concatenate(whole, 0).astype(BF)
        whole = [key_t[high], tag_rows, value_t[high], blank, query_t[high], blank, grad_t[high], blank]
        chunk_ref[2 * head + 1] = jnp.concatenate(whole, 0).astype(BF)


def pack(query, key, value, tags, branch, weight):
    return pl.pallas_call(
        pack_body,
        out_shape=jax.ShapeDtypeStruct((PLANE, 2 * FULL, TOK), BF),
        in_specs=[WHOLE] * 5 + [FAR_AWAY],
        out_specs=WHOLE,
        scratch_shapes=[pltpu.VMEM((WIDTH, WIDTH), BF), pltpu.SemaphoreType.DMA],
        compiler_params=params(61),
        cost_estimate=cost(4),
        name="pack",
    )(query, key, value, tags, branch, weight)


def filled(piece, extra):
    rows = [piece] + extra
    have = sum(part.shape[0] for part in rows)
    if have < TOK:
        rows.append(jnp.zeros((TOK - have, TOK), F32))
    return jnp.concatenate(rows, 0)


def natural(side, own, other):
    own, other = own.astype(F32), other.astype(F32)
    low, high = pick(side, own, other), pick(side, other, own)
    return [jnp.concatenate([low[rows], high[rows]], 0) for rows in (slice(0, HALF), slice(HALF, FULL))]


def window(side, own, near, far_own, far_other):
    for block in range(NEAR):
        at = block + EDGE * (1 - side)
        yield (at,) + tuple(natural(side, own[block + (SIDE - EDGE) * side, 0:FULL], near[block]))
    for block in range(EDGE):
        yield (block + NEAR * side,) + tuple(natural(side, far_own[block], far_other[block]))


def token_rows(block):
    return pl.ds(pl.multiple_of(block * TOK, TOK), TOK)


def same_clip(clip, same, other):
    ids = lax.broadcasted_iota(jnp.int32, (CLIPS, TOK), 0).astype(F32) + 1.0
    return jnp.where(ids == clip, same, other)


def lay_out_keys(block, key, key_n, key_t, clips):
    clip = key[HEAD_DIM : HEAD_DIM + 1]
    clips[block] = key[HEAD_DIM:]
    held = filled(key[0:HEAD_DIM], [same_clip(clip, 0.0, FAR)])
    key_n[token_rows(block), :] = held.T.astype(BF)
    if key_t is not None:
        key_t[block] = jnp.concatenate([key[0:HEAD_DIM], jnp.zeros((8, TOK), F32)], 0).astype(BF)


def key_padding(key_n, key_t):
    rows = slice(SPAN * TOK, ROOM * TOK)
    lane = lax.broadcasted_iota(jnp.int32, ((ROOM - SPAN) * TOK, TOK), 1)
    key_n[rows, :] = jnp.where((lane >= HEAD_DIM) & (lane < HEAD_DIM + CLIPS), FAR, 0.0).astype(BF)
    if key_t is not None:
        for block in range(SPAN, ROOM):
            key_t[block] = jnp.zeros((80, TOK), BF)


def key_ranges(clips, first_ref, count_ref):
    rows = [clips[block][0:1] for block in range(SPAN)]
    rows = [jnp.where(row == 0.0, 100.0, row) if at >= NEAR else row for at, row in enumerate(rows)]
    rows = jnp.concatenate(rows + [jnp.full((32 - SPAN, TOK), 100.0, F32)], 0)
    least = jnp.min(rows, axis=1, keepdims=True)
    most = jnp.max(rows, axis=1, keepdims=True)
    for tile in range(TILES):
        start = EDGE + tile * PART
        low, high = least[start : start + 1], most[start + PART - 1 : start + PART]
        first = jnp.sum(jnp.where(most < low, 1.0, 0.0)).astype(jnp.int32)
        end = jnp.sum(jnp.where(least <= high, 1.0, 0.0)).astype(jnp.int32)
        first_ref[tile] = first
        count_ref[tile] = (end - first + STEP - 1) // STEP


def side_by_side(ref, start):
    return jnp.concatenate([ref[start + at] for at in range(STEP)], 1)


def blocks(first, step):
    start = first + step * STEP
    return start, pl.ds(pl.multiple_of(start * TOK, TOK), STEP * TOK)


def attend_body(
    own, near, asked, far_own, far_other,
    mixed_ref, keep_asked_ref, give_asked_ref, keep_ref, give_ref, keep_far_ref, give_far_ref,
    key_n, key_t, value_n, value_t, query_t, query_n, grad_t, grad_n, held, mixed_t, dq, dk, dv,
    clips, first_ref, count_ref,
):
    side = core()
    for at, key, value in window(side, own, near, far_own, far_other):
        lay_out_keys(at, key, key_n, key_t, clips)
        value = filled(value[0:HEAD_DIM], [jnp.ones((8, TOK), F32)])
        value_n[token_rows(at), :] = value.T.astype(BF)
        value_t[at] = value[0:80].astype(BF)
    value_n[SPAN * TOK :, :] = jnp.zeros(((ROOM - SPAN) * TOK, TOK), BF)
    for block in range(SPAN, ROOM):
        value_t[block] = jnp.zeros((80, TOK), BF)
    key_padding(key_n, key_t)
    for block in range(SIDE):
        tile, cols = block // PART, slice((block % PART) * TOK, (block % PART + 1) * TOK)
        query, grad = natural(side, own[SIDE * side + block, FULL:], asked[block])
        query = filled(query[0:HEAD_DIM], [same_clip(clips[EDGE + block][0:1], 1.0, 0.0)])
        query_t[tile, :, cols] = query.astype(BF)
        query_n[tile, cols, :] = query.T.astype(BF)
        grad = filled(grad, [])
        grad_t[tile, :, cols] = grad.astype(BF)
        grad_n[tile, cols, :] = grad.T.astype(BF)
    key_ranges(clips, first_ref, count_ref)
    dk[...] = jnp.zeros_like(dk)
    dv[...] = jnp.zeros_like(dv)

    def query_step(tile, carry):
        first, count = first_ref[tile], count_ref[tile]

        def score_step(step, top):
            scores = mm(key_n[blocks(first, step)[1], :], query_t[tile])
            held[step] = scores
            return jnp.maximum(top, jnp.max(scores, axis=0, keepdims=True))

        top = lax.fori_loop(0, count, score_step, jnp.full((1, TILE), 2.0 * FAR, F32))

        def value_step(step, total):
            weights = jnp.exp2((held[step] - top) * SCALE2)
            held[step] = weights
            return total + mm(side_by_side(value_t, blocks(first, step)[0]), weights.astype(BF))

        total = lax.fori_loop(0, count, value_step, jnp.zeros((80, TILE), F32))
        inverse = 1.0 / total[HEAD_DIM : HEAD_DIM + 1]
        mixed = jnp.concatenate([total[0:HEAD_DIM] * inverse, jnp.zeros((8, TILE), F32)], 0).astype(BF)
        grad = grad_t[tile]
        delta = jnp.sum(mixed.astype(F32) * grad[0:FULL].astype(F32), axis=0, keepdims=True)
        mixed_t[tile] = mixed

        def grad_step(step, total):
            start, rows = blocks(first, step)
            prob = held[step] * inverse
            pull = mm(value_n[rows, :], grad)
            dv[rows, :] += mm(prob.astype(BF), grad_n[tile])
            score_grad = (prob * (pull - delta)).astype(BF)
            dk[rows, :] += mm(score_grad, query_n[tile])
            return total + mm(side_by_side(key_t, start), score_grad)

        dq[tile] = lax.fori_loop(0, count, grad_step, jnp.zeros((80, TILE), F32)) * SCALE
        return carry

    lax.fori_loop(0, TILES, query_step, 0)

    def halves(wholes):
        low = jnp.concatenate([whole[0:HALF] for whole in wholes], 0)
        high = jnp.concatenate([whole[HALF:] for whole in wholes], 0)
        return pick(side, low, high).astype(BF), pick(side, high, low).astype(BF)

    def key_grads(at):
        rows = token_rows(at)
        return [dk[rows, :].T[0:FULL] * SCALE, dv[rows, :].T[0:FULL]]

    for block in range(SIDE):
        tile, cols = block // PART, slice((block % PART) * TOK, (block % PART + 1) * TOK)
        mixed = mixed_t[tile, :, cols]
        mixed_ref[block] = mixed
        keep_asked_ref[block], give_asked_ref[block] = halves([mixed.astype(F32), dq[tile, :, cols]])
        keep_ref[block], give_ref[block] = halves(key_grads(EDGE + block))
    for block in range(EDGE):
        keep_ref[SIDE + block], give_ref[SIDE + block] = halves(key_grads(block + NEAR * (1 - side)))
        keep_far_ref[block], give_far_ref[block] = halves(key_grads(block + NEAR * side))


def attend(own, near, asked, far_own, far_other):
    whole = jax.ShapeDtypeStruct((SIDE, FULL, TOK), BF)
    keys = jax.ShapeDtypeStruct((NEAR, FULL, TOK), BF)
    edge = jax.ShapeDtypeStruct((EDGE, FULL, TOK), BF)
    row_form = pltpu.VMEM((ROOM * TOK, TOK), BF)
    column_form = pltpu.VMEM((ROOM, 80, TOK), BF)
    return pl.pallas_call(
        attend_body,
        out_shape=(whole, whole, whole, keys, keys, edge, edge),
        in_specs=[WHOLE] * 5,
        out_specs=(WHOLE,) * 7,
        cost_estimate=cost(20),
        scratch_shapes=[
            row_form, column_form, row_form, column_form,
            pltpu.VMEM((TILES, TOK, TILE), BF), pltpu.VMEM((TILES, TILE, TOK), BF),
            pltpu.VMEM((TILES, TOK, TILE), BF), pltpu.VMEM((TILES, TILE, TOK), BF),
            pltpu.VMEM((CHUNKS, STEP * TOK, TILE), F32),
            pltpu.VMEM((TILES, FULL, TILE), BF),
            pltpu.VMEM((TILES, FULL, TILE), F32),
            pltpu.VMEM((ROOM * TOK, TOK), F32),
            pltpu.VMEM((ROOM * TOK, TOK), F32),
            pltpu.VMEM((SPAN, 8, TOK), F32),
            pltpu.SMEM((TILES,), jnp.int32),
            pltpu.SMEM((TILES,), jnp.int32),
        ],
        compiler_params=params(24),
        name="attend",
    )(own, near, asked, far_own, far_other)


def weight_term_body(mixed, other, branch, *refs):
    out_refs, total = refs[:PLANES], refs[PLANES]
    step = pl.program_id(0)
    side = core()
    left, right = [], []
    for chip in range(CHIPS):
        for at in range(2):
            block = 2 * (CHIPS * step + chip) + (side if at == 0 else 1 - side)
            place = lax.rem(block, SIDE)
            foreign = jnp.where(block // SIDE == side, 0, 1)
            right.append(pick(foreign, mixed[place].astype(F32), other[place].astype(F32)))
            left.append(branch[chip, at])
    term = lax.dot_general(
        jnp.concatenate(left, 1), jnp.concatenate(right, 1).astype(BF), (((1,), (1,)), ((), ())),
        preferred_element_type=F32,
    )

    @pl.when(step == 0)
    def _():
        total[:, 0:FULL] = term
        total[:, FULL:] = jnp.zeros((WIDTH // 2, TOK - FULL), F32)

    @pl.when(step > 0)
    def _():
        total[:, 0:FULL] += term

    @pl.when(step == HEADS // CHIPS - 1)
    def _():
        plane = lax.axis_index("dp") // PLANE
        for away in range(PLANES):
            start = pl.multiple_of(lax.rem(plane + away, PLANES) * SHARE, 8)
            out_refs[away][...] = total[pl.ds(start, SHARE), :].astype(BF)


def weight_term(mixed, other, branch):
    share = pl.BlockSpec((SHARE, TOK), lambda i: (0, 0))
    held = pl.BlockSpec((SIDE, FULL, TOK), lambda i: (0, 0, 0))
    return pl.pallas_call(
        weight_term_body,
        grid=(HEADS // CHIPS,),
        out_shape=(jax.ShapeDtypeStruct((SHARE, TOK), BF),) * PLANES,
        in_specs=[held, held, pl.BlockSpec((CHIPS, 2, WIDTH // 2, TOK), lambda i: (i, 0, 0, 0))],
        out_specs=(share,) * PLANES,
        scratch_shapes=[pltpu.VMEM((WIDTH // 2, TOK), F32)],
        compiler_params=params(16),
        cost_estimate=cost(4),
        name="weight_term",
    )(mixed, other, branch)


def join_asked_body(keep, got, out_ref):
    side = core()
    for block in range(SIDE):
        out_ref[SIDE * side + block] = keep[block]
        out_ref[SIDE * (1 - side) + block] = got[block]


def join_asked(keep, got):
    return pl.pallas_call(
        join_asked_body,
        out_shape=jax.ShapeDtypeStruct((PLANE, FULL, TOK), BF),
        in_specs=[WHOLE] * 2,
        out_specs=WHOLE,
        compiler_params=params(8),
        cost_estimate=cost(1),
        name="join_asked",
    )(keep, got)


def join_body(keep, got, got_same, got_cross, term, term1, term2, term3, out_ref, total, pairs):
    side = core()
    total[0:SHARE] = sum(one[...].astype(F32) for one in (term, term1, term2, term3))
    total[SHARE:] = jnp.zeros((8, TOK), F32)
    mine, others = SIDE * side, SIDE * (1 - side)
    for block in range(SIDE):
        pairs[mine + block] = keep[block].astype(F32)
        pairs[others + block] = got[block].astype(F32)
    late, early = (SIDE - EDGE) * side, (SIDE - EDGE) * (1 - side)
    for block in range(EDGE):
        pairs[others + late + block] += keep[SIDE + block].astype(F32)
        pairs[mine + early + block] += got[SIDE + block].astype(F32)
    for block in range(EDGE):
        pairs[others + early + block] += got_same[block].astype(F32)
        pairs[mine + late + block] += got_cross[block].astype(F32)
    for block in range(PLANE):
        start = (block % SIDE) * FINAL
        out_ref[block] = jnp.concatenate([pairs[block], total[start : start + 16, :]], 0).astype(BF)


def join(*values):
    return pl.pallas_call(
        join_body,
        out_shape=jax.ShapeDtypeStruct((PLANE, FULL + 16, TOK), BF),
        in_specs=[WHOLE] * 8,
        out_specs=WHOLE,
        scratch_shapes=[pltpu.VMEM((SHARE + 8, TOK), F32), pltpu.VMEM((PLANE, FULL, TOK), F32)],
        compiler_params=params(12),
        cost_estimate=cost(1),
        name="join",
    )(*values)


def all_heads(packed, at):
    low = slice(at * HALF, (at + 1) * HALF)
    high = slice(at * HALF, at * HALF + HEAD_DIM - HALF)
    parts = []
    for head in range(HEADS):
        parts += [packed[2 * head].astype(F32)[low], packed[2 * head + 1].astype(F32)[high]]
    return jnp.concatenate(parts, 0).T.astype(BF)


def finish_asked_body(packed, residual, tags, gate, weight, bias, out_ref, dq_ref):
    gate_rows = lax.dot_general(
        clip_onehot(tags), gate[...], (((0,), (0,)), ((), ())),
        precision=lax.Precision.HIGHEST, preferred_element_type=F32,
    )
    projected = mm(all_heads(packed, 0), weight[...]) + bias[...].reshape(1, WIDTH)
    out_ref[...] = (residual[...].astype(F32) + gate_rows * projected).astype(BF)
    dq_ref[...] = all_heads(packed, 1)


def finish_asked(packed, residual, tags, gate, weight, bias):
    return pl.pallas_call(
        finish_asked_body,
        out_shape=(jax.ShapeDtypeStruct((TOK, WIDTH), BF),) * 2,
        in_specs=[WHOLE] * 6,
        out_specs=(WHOLE,) * 2,
        compiler_params=params(16),
        cost_estimate=cost(2),
        name="finish_asked",
    )(packed, residual, tags, gate, weight, bias)


def finish_body(packed, dk_ref, dv_ref, dw_ref):
    dk_ref[...] = all_heads(packed, 0)
    dv_ref[...] = all_heads(packed, 1)
    source = lax.rem(lax.axis_index("dp"), PLANE) // SIDE
    tails = [packed[2 * head + source, FULL:].astype(F32)[:, 0:HEAD_DIM] for head in range(HEADS)]
    dw_ref[...] = jnp.concatenate(tails, 1)[0:FINAL]


def finish(packed):
    return pl.pallas_call(
        finish_body,
        out_shape=(jax.ShapeDtypeStruct((TOK, WIDTH), BF),) * 2 + (jax.ShapeDtypeStruct((FINAL, WIDTH), F32),),
        in_specs=[WHOLE],
        out_specs=(WHOLE,) * 3,
        compiler_params=params(16),
        cost_estimate=cost(1),
        name="finish",
    )(packed)


def sent(values, target):
    pairs = [(i, target(i)) for i in range(DEVICES)]
    return lax.ppermute(values, "dp", [(i, j) for i, j in pairs if 0 <= j < DEVICES])


def other_core(device):
    return device ^ 1


def same_out(device):
    return device + PLANE if device % 2 == 0 else device - PLANE


def same_back(device):
    return device - PLANE if device % 2 == 0 else device + PLANE


def cross(device):
    return device - PLANE + 1 if device % 2 == 0 else device + PLANE - 1


def planes_on(count):
    return lambda device: (device + count * PLANE) % DEVICES


def traded(values):
    groups = [[plane * PLANE + i for i in range(PLANE)] for plane in range(PLANES)]
    return lax.all_to_all(values, "dp", 0, 0, axis_index_groups=groups, tiled=True)


def some_blocks(values, start, rows, count):
    return lax.dynamic_slice(values, (start, rows, 0), (count, FULL, TOK))


def shards(query, key, value, residual, tags, gate, weight, bias, out_grad):
    me = lax.axis_index("dp")
    side = me % 2
    whole_branch, branch, branch_away = branch_columns(out_grad, tags, gate)
    chunk = pack(query, key, value, tags, whole_branch, weight)
    branch_got, chunk = lax.optimization_barrier((sent(branch_away, other_core), chunk))
    branch = fill(branch, branch_got)
    cores = [[plane * PLANE + 2 * chip + at for chip in range(HEADS)] for plane in range(PLANES) for at in range(2)]
    gathered = lax.all_gather(branch, "dp", axis=0, axis_index_groups=cores, tiled=False)
    own = traded(chunk)
    near = sent(some_blocks(own, (SIDE - EDGE) * (1 - side), 0, NEAR), other_core)
    asked = sent(some_blocks(own, SIDE * (1 - side), FULL, SIDE), other_core)
    last = PLANE - EDGE
    far_own = sent(some_blocks(own, last * (1 - side), 0, EDGE), same_out)
    far_other = sent(some_blocks(own, last * side, 0, EDGE), cross)
    mixed, keep_asked, give_asked, keep, give, keep_far, give_far = attend(own, near, asked, far_own, far_other)
    joined = join_asked(keep_asked, sent(give_asked, other_core))
    joined, mixed, give, keep_far, give_far = lax.optimization_barrier((joined, mixed, give, keep_far, give_far))
    asked_back = traded(joined)
    mixed_other = sent(mixed, other_core)
    got = sent(give, other_core)
    got_same = sent(keep_far, same_back)
    got_cross = sent(give_far, cross)
    term, *terms = weight_term(mixed, mixed_other, gathered)
    terms = [sent(one, planes_on(away + 1)) for away, one in enumerate(terms)]
    keys_back = traded(join(keep, got, got_same, got_cross, term, *terms))
    block_out, dq = finish_asked(asked_back, residual, tags, gate, weight, bias)
    dk, dv, dw = finish(keys_back)
    return block_out, dq, dk, dv, dw.T


def solution(mesh):
    rows = P("dp", None)
    in_specs = (rows, rows, rows, rows, P("dp"), P(), P(), P(), rows)
    out_specs = (rows,) * 4 + (P(None, "dp"),)
    return jax.shard_map(shards, mesh=mesh, in_specs=in_specs, out_specs=out_specs, check_vma=False)
```

```python
import math

import jax
import jax.numpy as jnp
from jax import lax
from jax.experimental import pallas as pl
from jax.experimental.pallas import tpu as pltpu
from jax.sharding import PartitionSpec as P

HEADS = 16
HEAD_DIM = 72
WIDTH = HEADS * HEAD_DIM
TOK = 128
DEVICES = 128
PLANES = 4
PLANE = 32
SIDE = 16
EDGE = 7
SPAN = SIDE + 2 * EDGE
NEAR = SIDE + EDGE
TILE = 256
TILES = SIDE * TOK // TILE
PART = TILE // TOK
STEP = 4
ROOM = SPAN + STEP - 1
CHUNKS = 4
HALF = 40
FULL = 2 * HALF
FINAL = WIDTH // DEVICES
CHIPS = 4
SHARE = WIDTH // PLANES // 2
CLIPS = 32
SCALE = 1.0 / math.sqrt(HEAD_DIM)
SCALE2 = SCALE / math.log(2.0)
FAR = -1e30
BF = jnp.bfloat16
F32 = jnp.float32

WHOLE = pl.BlockSpec(memory_space=pltpu.VMEM)
FAR_AWAY = pl.BlockSpec(memory_space=pltpu.HBM)


def params(mebibytes):
    return pltpu.CompilerParams(vmem_limit_bytes=mebibytes * 1024 * 1024)


def cost(micros):
    return pl.CostEstimate(flops=int(micros * 4e8), bytes_accessed=int(micros * 2e6), transcendentals=0)


def mm(left, right):
    return jnp.dot(left, right, preferred_element_type=F32)


def clip_onehot(tags):
    ids = lax.broadcasted_iota(jnp.int32, (CLIPS, TOK), 0)
    return (ids == tags[...].reshape(1, TOK)).astype(F32)


def core():
    return lax.axis_index("dp") % 2


def pick(flag, first, second):
    return jnp.where(jnp.full(first.shape, flag, jnp.int32) == 0, first, second)


def branch_body(out_grad, tags, gate, branch_ref, mine_ref, theirs_ref):
    gate_t = lax.dot_general(
        gate[...], clip_onehot(tags), (((0,), (0,)), ((), ())),
        precision=lax.Precision.HIGHEST, preferred_element_type=F32,
    )
    branch_t = (out_grad[...].astype(F32).T * gate_t).astype(BF)
    branch_ref[...] = branch_t
    wide = branch_t.astype(F32)
    halves = []
    for side in range(2):
        starts = [(2 * plane + side) * SHARE for plane in range(PLANES)]
        halves.append(jnp.concatenate([wide[start : start + SHARE] for start in starts], 0))
    side = core()
    mine_ref[0] = pick(side, halves[0], halves[1]).astype(BF)
    mine_ref[1] = jnp.zeros((WIDTH // 2, TOK), BF)
    theirs_ref[...] = pick(side, halves[1], halves[0]).astype(BF)


def branch_columns(out_grad, tags, gate):
    return pl.pallas_call(
        branch_body,
        out_shape=(
            jax.ShapeDtypeStruct((WIDTH, TOK), BF),
            jax.ShapeDtypeStruct((2, WIDTH // 2, TOK), BF),
            jax.ShapeDtypeStruct((WIDTH // 2, TOK), BF),
        ),
        in_specs=[WHOLE] * 3,
        out_specs=(WHOLE,) * 3,
        compiler_params=params(56),
        cost_estimate=cost(2),
        name="branch_columns",
    )(out_grad, tags, gate)


def fill_body(_, got, out_ref, sem):
    load = pltpu.make_async_copy(got, out_ref.at[1], sem)
    load.start()
    load.wait()


def fill(branch, got):
    return pl.pallas_call(
        fill_body,
        out_shape=jax.ShapeDtypeStruct(branch.shape, BF),
        in_specs=[FAR_AWAY] * 2,
        out_specs=FAR_AWAY,
        input_output_aliases={0: 0},
        scratch_shapes=[pltpu.SemaphoreType.DMA],
        compiler_params=params(16),
        cost_estimate=cost(1),
        name="fill",
    )(branch, got)


def pack_body(query, key, value, tags, branch, weight, chunk_ref, weight_here, weight_sem):
    load = pltpu.make_async_copy(weight, weight_here, weight_sem)
    load.start()
    key_t = key[...].astype(F32).T
    value_t = value[...].astype(F32).T
    query_t = query[...].astype(F32).T
    tag_rows = jnp.broadcast_to(tags[...].reshape(1, TOK).astype(F32) + 1.0, (8, TOK))
    blank = jnp.zeros((8, TOK), F32)
    load.wait()
    grad_t = mm(weight_here[...], branch[...])
    for head in range(HEADS):
        start = head * HEAD_DIM
        low, high = slice(start, start + HALF), slice(start + HALF, start + HEAD_DIM)
        whole = [key_t[low], value_t[low], query_t[low], grad_t[low]]
        chunk_ref[2 * head] = jnp.concatenate(whole, 0).astype(BF)
        whole = [key_t[high], tag_rows, value_t[high], blank, query_t[high], blank, grad_t[high], blank]
        chunk_ref[2 * head + 1] = jnp.concatenate(whole, 0).astype(BF)


def pack(query, key, value, tags, branch, weight):
    return pl.pallas_call(
        pack_body,
        out_shape=jax.ShapeDtypeStruct((PLANE, 2 * FULL, TOK), BF),
        in_specs=[WHOLE] * 5 + [FAR_AWAY],
        out_specs=WHOLE,
        scratch_shapes=[pltpu.VMEM((WIDTH, WIDTH), BF), pltpu.SemaphoreType.DMA],
        compiler_params=params(61),
        cost_estimate=cost(4),
        name="pack",
    )(query, key, value, tags, branch, weight)


def filled(piece, extra):
    rows = [piece] + extra
    have = sum(part.shape[0] for part in rows)
    if have < TOK:
        rows.append(jnp.zeros((TOK - have, TOK), F32))
    return jnp.concatenate(rows, 0)


def natural(side, own, other):
    own, other = own.astype(F32), other.astype(F32)
    low, high = pick(side, own, other), pick(side, other, own)
    return [jnp.concatenate([low[rows], high[rows]], 0) for rows in (slice(0, HALF), slice(HALF, FULL))]


def halves(side, wholes):
    low = jnp.concatenate([whole[0:HALF] for whole in wholes], 0)
    high = jnp.concatenate([whole[HALF:] for whole in wholes], 0)
    return pick(side, low, high), pick(side, high, low)


def window(side, own, near, far_own, far_other):
    for block in range(NEAR):
        at = block + EDGE * (1 - side)
        yield (at,) + tuple(natural(side, own[block + (SIDE - EDGE) * side, 0:FULL], near[block]))
    for block in range(EDGE):
        yield (block + NEAR * side,) + tuple(natural(side, far_own[block], far_other[block]))


def token_rows(block):
    return pl.ds(pl.multiple_of(block * TOK, TOK), TOK)


def same_clip(clip, same, other):
    ids = lax.broadcasted_iota(jnp.int32, (CLIPS, TOK), 0).astype(F32) + 1.0
    return jnp.where(ids == clip, same, other)


def lay_out_keys(block, key, key_n, key_t, clips):
    clip = key[HEAD_DIM : HEAD_DIM + 1]
    clips[block] = key[HEAD_DIM:]
    held = filled(key[0:HEAD_DIM], [same_clip(clip, 0.0, FAR)])
    key_n[token_rows(block), :] = held.T.astype(BF)
    if key_t is not None:
        key_t[block] = jnp.concatenate([key[0:HEAD_DIM], jnp.zeros((8, TOK), F32)], 0).astype(BF)


def key_padding(key_n, key_t):
    rows = slice(SPAN * TOK, ROOM * TOK)
    lane = lax.broadcasted_iota(jnp.int32, ((ROOM - SPAN) * TOK, TOK), 1)
    key_n[rows, :] = jnp.where((lane >= HEAD_DIM) & (lane < HEAD_DIM + CLIPS), FAR, 0.0).astype(BF)
    if key_t is not None:
        for block in range(SPAN, ROOM):
            key_t[block] = jnp.zeros((80, TOK), BF)


def key_ranges(clips, first_ref, count_ref):
    rows = [clips[block][0:1] for block in range(SPAN)]
    rows = [jnp.where(row == 0.0, 100.0, row) if at >= NEAR else row for at, row in enumerate(rows)]
    rows = jnp.concatenate(rows + [jnp.full((32 - SPAN, TOK), 100.0, F32)], 0)
    least = jnp.min(rows, axis=1, keepdims=True)
    most = jnp.max(rows, axis=1, keepdims=True)
    for tile in range(TILES):
        start = EDGE + tile * PART
        low, high = least[start : start + 1], most[start + PART - 1 : start + PART]
        first = jnp.sum(jnp.where(most < low, 1.0, 0.0)).astype(jnp.int32)
        end = jnp.sum(jnp.where(least <= high, 1.0, 0.0)).astype(jnp.int32)
        first_ref[tile] = first
        count_ref[tile] = (end - first + STEP - 1) // STEP


def side_by_side(ref, start):
    return jnp.concatenate([ref[start + at] for at in range(STEP)], 1)


def blocks(first, step):
    start = first + step * STEP
    return start, pl.ds(pl.multiple_of(start * TOK, TOK), STEP * TOK)


def attend_body(
    own, near, asked, far_own, far_other,
    mixed_ref, keep_asked_ref, give_asked_ref, keep_ref, give_ref, far_ref,
    key_n, key_t, value_n, value_t, query_t, query_n, grad_t, grad_n, held, pulls, mixed_t, dq, dk, dv,
    clips, first_ref, count_ref,
):
    side = core()
    for at, key, value in window(side, own, near, far_own, far_other):
        lay_out_keys(at, key, key_n, key_t, clips)
        value = filled(value[0:HEAD_DIM], [jnp.ones((8, TOK), F32)])
        value_n[token_rows(at), :] = value.T.astype(BF)
        value_t[at] = value[0:80].astype(BF)
    value_n[SPAN * TOK :, :] = jnp.zeros(((ROOM - SPAN) * TOK, TOK), BF)
    for block in range(SPAN, ROOM):
        value_t[block] = jnp.zeros((80, TOK), BF)
    key_padding(key_n, key_t)
    for block in range(SIDE):
        tile, cols = block // PART, slice((block % PART) * TOK, (block % PART + 1) * TOK)
        query, grad = natural(side, own[SIDE * side + block, FULL:], asked[block])
        query = filled(query[0:HEAD_DIM], [same_clip(clips[EDGE + block][0:1], 1.0, 0.0)])
        query_t[tile, :, cols] = query.astype(BF)
        query_n[tile, cols, :] = query.T.astype(BF)
        grad = filled(grad, [])
        grad_t[tile, :, cols] = grad.astype(BF)
        grad_n[tile, cols, :] = grad.T.astype(BF)
    key_ranges(clips, first_ref, count_ref)
    dk[...] = jnp.zeros_like(dk)
    dv[...] = jnp.zeros_like(dv)

    def whole_tile(tile, first, count):
        tops = []
        grad = grad_t[tile]
        for step in range(count):
            scores = mm(key_n[blocks(first, step)[1], :], query_t[tile])
            held[step] = scores
            tops.append(jnp.max(scores, axis=0, keepdims=True))
            pulls[step] = mm(value_n[blocks(first, step)[1], :], grad)
        top = tops[0]
        for other in tops[1:]:
            top = jnp.maximum(top, other)
        total = None
        for step in range(count):
            weights = jnp.exp2((held[step] - top) * SCALE2)
            held[step] = weights
            term = mm(side_by_side(value_t, blocks(first, step)[0]), weights.astype(BF))
            total = term if total is None else total + term
        inverse = 1.0 / total[HEAD_DIM : HEAD_DIM + 1]
        mixed = jnp.concatenate([total[0:HEAD_DIM] * inverse, jnp.zeros((8, TILE), F32)], 0).astype(BF)
        delta = jnp.sum(mixed.astype(F32) * grad[0:FULL].astype(F32), axis=0, keepdims=True)
        mixed_t[tile] = mixed
        total = None
        for step in range(count):
            start, rows = blocks(first, step)
            prob = held[step] * inverse
            pull = pulls[step]
            dv[rows, :] += mm(prob.astype(BF), grad_n[tile])
            score_grad = (prob * (pull - delta)).astype(BF)
            dk[rows, :] += mm(score_grad, query_n[tile])
            term = mm(side_by_side(key_t, start), score_grad)
            total = term if total is None else total + term
        dq[tile] = total * SCALE

    def query_step(tile, carry):
        first, count = first_ref[tile], count_ref[tile]
        for steps in range(1, CHUNKS + 1):
            pl.when(count == steps)(lambda steps=steps: whole_tile(tile, first, steps))
        return carry

    lax.fori_loop(0, TILES, query_step, 0)

    def key_grads(at):
        rows = token_rows(at)
        return [dk[rows, :].T[0:FULL] * SCALE, dv[rows, :].T[0:FULL]]

    def hand_out(keep, give, block, wholes):
        first, second = halves(side, wholes)
        keep[block], give[block] = first.astype(BF), second.astype(BF)

    for block in range(SIDE):
        tile, cols = block // PART, slice((block % PART) * TOK, (block % PART + 1) * TOK)
        mixed = mixed_t[tile, :, cols]
        mixed_ref[block] = mixed
        hand_out(keep_asked_ref, give_asked_ref, block, [mixed.astype(F32), dq[tile, :, cols]])
        hand_out(keep_ref, give_ref, block, key_grads(EDGE + block))
    for block in range(EDGE):
        hand_out(keep_ref, give_ref, SIDE + block, key_grads(block + NEAR * (1 - side)))
        far_ref[block] = jnp.concatenate(key_grads(block + NEAR * side), 0).astype(BF)


def attend(own, near, asked, far_own, far_other):
    whole = jax.ShapeDtypeStruct((SIDE, FULL, TOK), BF)
    keys = jax.ShapeDtypeStruct((NEAR, FULL, TOK), BF)
    edge = jax.ShapeDtypeStruct((EDGE, 2 * FULL, TOK), BF)
    row_form = pltpu.VMEM((ROOM * TOK, TOK), BF)
    column_form = pltpu.VMEM((ROOM, 80, TOK), BF)
    return pl.pallas_call(
        attend_body,
        out_shape=(whole, whole, whole, keys, keys, edge),
        in_specs=[WHOLE] * 5,
        out_specs=(WHOLE,) * 6,
        cost_estimate=cost(20),
        scratch_shapes=[
            row_form, column_form, row_form, column_form,
            pltpu.VMEM((TILES, TOK, TILE), BF), pltpu.VMEM((TILES, TILE, TOK), BF),
            pltpu.VMEM((TILES, TOK, TILE), BF), pltpu.VMEM((TILES, TILE, TOK), BF),
            pltpu.VMEM((CHUNKS, STEP * TOK, TILE), F32),
            pltpu.VMEM((CHUNKS, STEP * TOK, TILE), F32),
            pltpu.VMEM((TILES, FULL, TILE), BF),
            pltpu.VMEM((TILES, FULL, TILE), F32),
            pltpu.VMEM((ROOM * TOK, TOK), F32),
            pltpu.VMEM((ROOM * TOK, TOK), F32),
            pltpu.VMEM((SPAN, 8, TOK), F32),
            pltpu.SMEM((TILES,), jnp.int32),
            pltpu.SMEM((TILES,), jnp.int32),
        ],
        compiler_params=params(24),
        name="attend",
    )(own, near, asked, far_own, far_other)


def weight_term_body(mixed, other, branch, *refs):
    out_refs, total = refs[:PLANES], refs[PLANES]
    step = pl.program_id(0)
    side = core()
    left, right = [], []
    for chip in range(CHIPS):
        for at in range(2):
            block = 2 * (CHIPS * step + chip) + (side if at == 0 else 1 - side)
            place = lax.rem(block, SIDE)
            foreign = jnp.where(block // SIDE == side, 0, 1)
            right.append(pick(foreign, mixed[place].astype(F32), other[place].astype(F32)))
            left.append(branch[chip, at])
    term = lax.dot_general(
        jnp.concatenate(left, 1), jnp.concatenate(right, 1).astype(BF), (((1,), (1,)), ((), ())),
        preferred_element_type=F32,
    )

    @pl.when(step == 0)
    def _():
        total[:, 0:FULL] = term
        total[:, FULL:] = jnp.zeros((WIDTH // 2, TOK - FULL), F32)

    @pl.when(step > 0)
    def _():
        total[:, 0:FULL] += term

    @pl.when(step == HEADS // CHIPS - 1)
    def _():
        plane = lax.axis_index("dp") // PLANE
        for away in range(PLANES):
            start = pl.multiple_of(lax.rem(plane + away, PLANES) * SHARE, 8)
            out_refs[away][...] = total[pl.ds(start, SHARE), :].astype(BF)


def weight_term(mixed, other, branch):
    share = pl.BlockSpec((SHARE, TOK), lambda i: (0, 0))
    held = pl.BlockSpec((SIDE, FULL, TOK), lambda i: (0, 0, 0))
    return pl.pallas_call(
        weight_term_body,
        grid=(HEADS // CHIPS,),
        out_shape=(jax.ShapeDtypeStruct((SHARE, TOK), BF),) * PLANES,
        in_specs=[held, held, pl.BlockSpec((CHIPS, 2, WIDTH // 2, TOK), lambda i: (i, 0, 0, 0))],
        out_specs=(share,) * PLANES,
        scratch_shapes=[pltpu.VMEM((WIDTH // 2, TOK), F32)],
        compiler_params=params(16),
        cost_estimate=cost(4),
        name="weight_term",
    )(mixed, other, branch)


def fold_body(keep, give, far, keep_ref, give_ref):
    side = core()
    keep_ref[...] = keep[...]
    give_ref[...] = give[...]
    for block in range(EDGE):
        place = block + (SIDE - EDGE) * side
        whole = far[block].astype(F32)
        first, second = halves(side, [whole[0:FULL], whole[FULL:]])
        keep_ref[place] = (keep[place].astype(F32) + first).astype(BF)
        give_ref[place] = (give[place].astype(F32) + second).astype(BF)


def fold(keep, give, far):
    keys = jax.ShapeDtypeStruct((NEAR, FULL, TOK), BF)
    return pl.pallas_call(
        fold_body,
        out_shape=(keys, keys),
        in_specs=[WHOLE] * 3,
        out_specs=(WHOLE,) * 2,
        compiler_params=params(8),
        cost_estimate=cost(1),
        name="fold",
    )(keep, give, far)


def join_body(keep_asked, got_asked, keep, got, term, term1, term2, term3, out_ref, total, pairs):
    side = core()
    total[0:SHARE] = sum(one[...].astype(F32) for one in (term, term1, term2, term3))
    total[SHARE:] = jnp.zeros((8, TOK), F32)
    mine, others = SIDE * side, SIDE * (1 - side)
    for block in range(SIDE):
        pairs[mine + block] = keep[block].astype(F32)
        pairs[others + block] = got[block].astype(F32)
    for block in range(EDGE):
        pairs[others + (SIDE - EDGE) * side + block] += keep[SIDE + block].astype(F32)
        pairs[mine + (SIDE - EDGE) * (1 - side) + block] += got[SIDE + block].astype(F32)
    for block in range(SIDE):
        tail = total[block * FINAL : block * FINAL + 16, :]
        for start, asked in ((mine, keep_asked), (others, got_asked)):
            whole = [asked[block].astype(F32), pairs[start + block], tail]
            out_ref[start + block] = jnp.concatenate(whole, 0).astype(BF)


def join(*values):
    return pl.pallas_call(
        join_body,
        out_shape=jax.ShapeDtypeStruct((PLANE, 2 * FULL + 16, TOK), BF),
        in_specs=[WHOLE] * 8,
        out_specs=WHOLE,
        scratch_shapes=[pltpu.VMEM((SHARE + 8, TOK), F32), pltpu.VMEM((PLANE, FULL, TOK), F32)],
        compiler_params=params(12),
        cost_estimate=cost(1),
        name="join",
    )(*values)


def finish_body(packed, residual, tags, gate, weight, bias, out_ref, dq_ref, dk_ref, dv_ref, dw_ref):
    def rows(at):
        low = slice(at * HALF, (at + 1) * HALF)
        high = slice(at * HALF, at * HALF + HEAD_DIM - HALF)
        parts = []
        for head in range(HEADS):
            parts += [packed[2 * head].astype(F32)[low], packed[2 * head + 1].astype(F32)[high]]
        return jnp.concatenate(parts, 0).T.astype(BF)

    gate_rows = lax.dot_general(
        clip_onehot(tags), gate[...], (((0,), (0,)), ((), ())),
        precision=lax.Precision.HIGHEST, preferred_element_type=F32,
    )
    projected = mm(rows(0), weight[...]) + bias[...].reshape(1, WIDTH)
    out_ref[...] = (residual[...].astype(F32) + gate_rows * projected).astype(BF)
    dq_ref[...] = rows(1)
    dk_ref[...] = rows(2)
    dv_ref[...] = rows(3)
    source = lax.rem(lax.axis_index("dp"), PLANE) // SIDE
    tails = [packed[2 * head + source, 2 * FULL :].astype(F32)[:, 0:HEAD_DIM] for head in range(HEADS)]
    dw_ref[...] = jnp.concatenate(tails, 1)[0:FINAL]


def finish(packed, residual, tags, gate, weight, bias):
    return pl.pallas_call(
        finish_body,
        out_shape=(jax.ShapeDtypeStruct((TOK, WIDTH), BF),) * 4 + (jax.ShapeDtypeStruct((FINAL, WIDTH), F32),),
        in_specs=[WHOLE] * 6,
        out_specs=(WHOLE,) * 5,
        compiler_params=params(16),
        cost_estimate=cost(3),
        name="finish",
    )(packed, residual, tags, gate, weight, bias)


def sent(values, target):
    pairs = [(i, target(i)) for i in range(DEVICES)]
    return lax.ppermute(values, "dp", [(i, j) for i, j in pairs if 0 <= j < DEVICES])


def other_core(device):
    return device ^ 1


def cross(device):
    return device - PLANE + 1 if device % 2 == 0 else device + PLANE - 1


def planes_on(count):
    return lambda device: (device + count * PLANE) % DEVICES


def traded(values):
    groups = [[plane * PLANE + i for i in range(PLANE)] for plane in range(PLANES)]
    return lax.all_to_all(values, "dp", 0, 0, axis_index_groups=groups, tiled=True)


def some_blocks(values, start, rows, count):
    return lax.dynamic_slice(values, (start, rows, 0), (count, FULL, TOK))


def shards(query, key, value, residual, tags, gate, weight, bias, out_grad):
    me = lax.axis_index("dp")
    side = me % 2
    whole_branch, branch, branch_away = branch_columns(out_grad, tags, gate)
    chunk = pack(query, key, value, tags, whole_branch, weight)
    branch_got, chunk = lax.optimization_barrier((sent(branch_away, other_core), chunk))
    branch = fill(branch, branch_got)
    cores = [[plane * PLANE + 2 * chip + at for chip in range(HEADS)] for plane in range(PLANES) for at in range(2)]
    gathered = lax.all_gather(branch, "dp", axis=0, axis_index_groups=cores, tiled=False)
    own = traded(chunk)
    near = sent(some_blocks(own, (SIDE - EDGE) * (1 - side), 0, NEAR), other_core)
    asked = sent(some_blocks(own, SIDE * (1 - side), FULL, SIDE), other_core)
    far_other = sent(some_blocks(own, (PLANE - EDGE) * side, 0, EDGE), cross)
    far_own = sent(some_blocks(near, SIDE * side, 0, EDGE), cross)
    mixed, keep_asked, give_asked, keep, give, far = attend(own, near, asked, far_own, far_other)
    far = sent(far, cross)
    mixed_other = sent(mixed, other_core)
    got_asked = sent(give_asked, other_core)
    term, *terms = weight_term(mixed, mixed_other, gathered)
    terms = [sent(one, planes_on(away + 1)) for away, one in enumerate(terms)]
    keep, give = fold(keep, give, far)
    got = sent(give, other_core)
    packed = traded(join(keep_asked, got_asked, keep, got, term, *terms))
    block_out, dq, dk, dv, dw = finish(packed, residual, tags, gate, weight, bias)
    return block_out, dq, dk, dv, dw.T


def solution(mesh):
    rows = P("dp", None)
    in_specs = (rows, rows, rows, rows, P("dp"), P(), P(), P(), rows)
    out_specs = (rows,) * 4 + (P(None, "dp"),)
    return jax.shard_map(shards, mesh=mesh, in_specs=in_specs, out_specs=out_specs, check_vma=False)
```

```python
import math

import jax
import jax.numpy as jnp
from jax import lax
from jax.experimental import pallas as pl
from jax.experimental.pallas import tpu as pltpu
from jax.sharding import PartitionSpec as P

HEADS = 16
HEAD_DIM = 72
WIDTH = HEADS * HEAD_DIM
TOK = 128
DEVICES = 128
PLANES = 4
PLANE = 32
SIDE = 16
EDGE = 7
SPAN = SIDE + 2 * EDGE
NEAR = SIDE + EDGE
TILE = 256
TILES = SIDE * TOK // TILE
PART = TILE // TOK
STEP = 4
ROOM = SPAN + STEP - 1
CHUNKS = 4
HALF = 40
FULL = 2 * HALF
FINAL = WIDTH // DEVICES
CHIPS = 4
SHARE = WIDTH // PLANES // 2
CLIPS = 32
SCALE = 1.0 / math.sqrt(HEAD_DIM)
SCALE2 = SCALE / math.log(2.0)
FAR = -1e30
BF = jnp.bfloat16
F32 = jnp.float32

WHOLE = pl.BlockSpec(memory_space=pltpu.VMEM)
FAR_AWAY = pl.BlockSpec(memory_space=pltpu.HBM)


def params(mebibytes):
    return pltpu.CompilerParams(vmem_limit_bytes=mebibytes * 1024 * 1024)


def cost(micros):
    return pl.CostEstimate(flops=int(micros * 4e8), bytes_accessed=int(micros * 2e6), transcendentals=0)


def mm(left, right):
    return jnp.dot(left, right, preferred_element_type=F32)


def clip_onehot(tags):
    ids = lax.broadcasted_iota(jnp.int32, (CLIPS, TOK), 0)
    return (ids == tags[...].reshape(1, TOK)).astype(F32)


def core():
    return lax.axis_index("dp") % 2


def pick(flag, first, second):
    return jnp.where(jnp.full(first.shape, flag, jnp.int32) == 0, first, second)


def branch_body(out_grad, tags, gate, branch_ref, mine_ref, theirs_ref):
    gate_t = lax.dot_general(
        gate[...], clip_onehot(tags), (((0,), (0,)), ((), ())),
        precision=lax.Precision.HIGHEST, preferred_element_type=F32,
    )
    branch_t = (out_grad[...].astype(F32).T * gate_t).astype(BF)
    branch_ref[...] = branch_t
    wide = branch_t.astype(F32)
    halves = []
    for side in range(2):
        starts = [(2 * plane + side) * SHARE for plane in range(PLANES)]
        halves.append(jnp.concatenate([wide[start : start + SHARE] for start in starts], 0))
    side = core()
    mine_ref[0] = pick(side, halves[0], halves[1]).astype(BF)
    mine_ref[1] = jnp.zeros((WIDTH // 2, TOK), BF)
    theirs_ref[...] = pick(side, halves[1], halves[0]).astype(BF)


def branch_columns(out_grad, tags, gate):
    return pl.pallas_call(
        branch_body,
        out_shape=(
            jax.ShapeDtypeStruct((WIDTH, TOK), BF),
            jax.ShapeDtypeStruct((2, WIDTH // 2, TOK), BF),
            jax.ShapeDtypeStruct((WIDTH // 2, TOK), BF),
        ),
        in_specs=[WHOLE] * 3,
        out_specs=(WHOLE,) * 3,
        compiler_params=params(56),
        cost_estimate=cost(2),
        name="branch_columns",
    )(out_grad, tags, gate)


def fill_body(_, got, out_ref, sem):
    load = pltpu.make_async_copy(got, out_ref.at[1], sem)
    load.start()
    load.wait()


def fill(branch, got):
    return pl.pallas_call(
        fill_body,
        out_shape=jax.ShapeDtypeStruct(branch.shape, BF),
        in_specs=[FAR_AWAY] * 2,
        out_specs=FAR_AWAY,
        input_output_aliases={0: 0},
        scratch_shapes=[pltpu.SemaphoreType.DMA],
        compiler_params=params(16),
        cost_estimate=cost(1),
        name="fill",
    )(branch, got)


def pack_body(query, key, value, weight, tags, branch, chunk_ref, query_here, key_here, value_here, weight_here, sems):
    loads = []
    for at, (source, here) in enumerate(
        ((key, key_here), (value, value_here), (query, query_here), (weight, weight_here))
    ):
        loads.append(pltpu.make_async_copy(source, here, sems.at[at]))
        loads[-1].start()
    tag_rows = jnp.broadcast_to(tags[...].reshape(1, TOK).astype(F32) + 1.0, (8, TOK))
    blank = jnp.zeros((8, TOK), F32)
    loads[0].wait()
    key_t = key_here[...].astype(F32).T
    loads[1].wait()
    value_t = value_here[...].astype(F32).T
    loads[2].wait()
    query_t = query_here[...].astype(F32).T
    loads[3].wait()
    grad_t = mm(weight_here[...], branch[...])
    for head in range(HEADS):
        start = head * HEAD_DIM
        low, high = slice(start, start + HALF), slice(start + HALF, start + HEAD_DIM)
        whole = [key_t[low], value_t[low], query_t[low], grad_t[low]]
        chunk_ref[2 * head] = jnp.concatenate(whole, 0).astype(BF)
        whole = [key_t[high], tag_rows, value_t[high], blank, query_t[high], blank, grad_t[high], blank]
        chunk_ref[2 * head + 1] = jnp.concatenate(whole, 0).astype(BF)


def pack(query, key, value, tags, branch, weight):
    rows = pltpu.VMEM((TOK, WIDTH), BF)
    return pl.pallas_call(
        pack_body,
        out_shape=jax.ShapeDtypeStruct((PLANE, 2 * FULL, TOK), BF),
        in_specs=[FAR_AWAY] * 4 + [WHOLE] * 2,
        out_specs=WHOLE,
        scratch_shapes=[rows, rows, rows, pltpu.VMEM((WIDTH, WIDTH), BF), pltpu.SemaphoreType.DMA((4,))],
        compiler_params=params(61),
        cost_estimate=cost(4),
        name="pack",
    )(query, key, value, weight, tags, branch)


def filled(piece, extra):
    rows = [piece] + extra
    have = sum(part.shape[0] for part in rows)
    if have < TOK:
        rows.append(jnp.zeros((TOK - have, TOK), F32))
    return jnp.concatenate(rows, 0)


def natural(side, own, other):
    own, other = own.astype(F32), other.astype(F32)
    low, high = pick(side, own, other), pick(side, other, own)
    return [jnp.concatenate([low[rows], high[rows]], 0) for rows in (slice(0, HALF), slice(HALF, FULL))]


def halves(side, wholes):
    low = jnp.concatenate([whole[0:HALF] for whole in wholes], 0)
    high = jnp.concatenate([whole[HALF:] for whole in wholes], 0)
    return pick(side, low, high), pick(side, high, low)


def window(side, own, near, far_own, far_other):
    for block in range(NEAR):
        at = block + EDGE * (1 - side)
        yield (at,) + tuple(natural(side, own[block + (SIDE - EDGE) * side, 0:FULL], near[block]))
    for block in range(EDGE):
        yield (block + NEAR * side,) + tuple(natural(side, far_own[block], far_other[block]))


def token_rows(block):
    return pl.ds(pl.multiple_of(block * TOK, TOK), TOK)


def same_clip(clip, same, other):
    ids = lax.broadcasted_iota(jnp.int32, (CLIPS, TOK), 0).astype(F32) + 1.0
    return jnp.where(ids == clip, same, other)


def lay_out_keys(block, key, key_n, key_t, clips):
    clip = key[HEAD_DIM : HEAD_DIM + 1]
    clips[block] = key[HEAD_DIM:]
    held = filled(key[0:HEAD_DIM], [same_clip(clip, 0.0, FAR)])
    key_n[token_rows(block), :] = held.T.astype(BF)
    if key_t is not None:
        key_t[block] = jnp.concatenate([key[0:HEAD_DIM], jnp.zeros((8, TOK), F32)], 0).astype(BF)


def key_padding(key_n, key_t):
    rows = slice(SPAN * TOK, ROOM * TOK)
    lane = lax.broadcasted_iota(jnp.int32, ((ROOM - SPAN) * TOK, TOK), 1)
    key_n[rows, :] = jnp.where((lane >= HEAD_DIM) & (lane < HEAD_DIM + CLIPS), FAR, 0.0).astype(BF)
    if key_t is not None:
        for block in range(SPAN, ROOM):
            key_t[block] = jnp.zeros((80, TOK), BF)


def key_ranges(clips, first_ref, count_ref):
    rows = [clips[block][0:1] for block in range(SPAN)]
    rows = [jnp.where(row == 0.0, 100.0, row) if at >= NEAR else row for at, row in enumerate(rows)]
    rows = jnp.concatenate(rows + [jnp.full((32 - SPAN, TOK), 100.0, F32)], 0)
    least = jnp.min(rows, axis=1, keepdims=True)
    most = jnp.max(rows, axis=1, keepdims=True)
    for tile in range(TILES):
        start = EDGE + tile * PART
        low, high = least[start : start + 1], most[start + PART - 1 : start + PART]
        first = jnp.sum(jnp.where(most < low, 1.0, 0.0)).astype(jnp.int32)
        end = jnp.sum(jnp.where(least <= high, 1.0, 0.0)).astype(jnp.int32)
        first_ref[tile] = first
        count_ref[tile] = (end - first + STEP - 1) // STEP


def side_by_side(ref, start):
    return jnp.concatenate([ref[start + at] for at in range(STEP)], 1)


def blocks(first, step):
    start = first + step * STEP
    return start, pl.ds(pl.multiple_of(start * TOK, TOK), STEP * TOK)


def attend_body(
    own, near, asked, far_own, far_other,
    mixed_ref, keep_asked_ref, give_asked_ref, keep_ref, give_ref, far_ref,
    key_n, key_t, value_n, value_t, query_t, query_n, grad_t, grad_n, held, pulls, mixed_t, dq, dk, dv,
    clips, first_ref, count_ref,
):
    side = core()
    for at, key, value in window(side, own, near, far_own, far_other):
        lay_out_keys(at, key, key_n, key_t, clips)
        value = filled(value[0:HEAD_DIM], [jnp.ones((8, TOK), F32)])
        value_n[token_rows(at), :] = value.T.astype(BF)
        value_t[at] = value[0:80].astype(BF)
    value_n[SPAN * TOK :, :] = jnp.zeros(((ROOM - SPAN) * TOK, TOK), BF)
    for block in range(SPAN, ROOM):
        value_t[block] = jnp.zeros((80, TOK), BF)
    key_padding(key_n, key_t)
    for block in range(SIDE):
        tile, cols = block // PART, slice((block % PART) * TOK, (block % PART + 1) * TOK)
        query, grad = natural(side, own[SIDE * side + block, FULL:], asked[block])
        query = filled(query[0:HEAD_DIM], [same_clip(clips[EDGE + block][0:1], 1.0, 0.0)])
        query_t[tile, :, cols] = query.astype(BF)
        query_n[tile, cols, :] = query.T.astype(BF)
        grad = filled(grad, [])
        grad_t[tile, :, cols] = grad.astype(BF)
        grad_n[tile, cols, :] = grad.T.astype(BF)
    key_ranges(clips, first_ref, count_ref)
    dk[...] = jnp.zeros_like(dk)
    dv[...] = jnp.zeros_like(dv)

    def whole_tile(tile, first, count):
        tops = []
        grad = grad_t[tile]
        for step in range(count):
            scores = mm(key_n[blocks(first, step)[1], :], query_t[tile])
            held[step] = scores
            tops.append(jnp.max(scores, axis=0, keepdims=True))
            pulls[step] = mm(value_n[blocks(first, step)[1], :], grad)
        top = tops[0]
        for other in tops[1:]:
            top = jnp.maximum(top, other)
        total = None
        for step in range(count):
            weights = jnp.exp2((held[step] - top) * SCALE2)
            held[step] = weights
            term = mm(side_by_side(value_t, blocks(first, step)[0]), weights.astype(BF))
            total = term if total is None else total + term
        inverse = 1.0 / total[HEAD_DIM : HEAD_DIM + 1]
        mixed = jnp.concatenate([total[0:HEAD_DIM] * inverse, jnp.zeros((8, TILE), F32)], 0).astype(BF)
        delta = jnp.sum(mixed.astype(F32) * grad[0:FULL].astype(F32), axis=0, keepdims=True)
        mixed_t[tile] = mixed
        total = None
        for step in range(count):
            start, rows = blocks(first, step)
            prob = held[step] * inverse
            pull = pulls[step]
            dv[rows, :] += mm(prob.astype(BF), grad_n[tile])
            score_grad = (prob * (pull - delta)).astype(BF)
            dk[rows, :] += mm(score_grad, query_n[tile])
            term = mm(side_by_side(key_t, start), score_grad)
            total = term if total is None else total + term
        dq[tile] = total * SCALE

    def query_step(tile, carry):
        first, count = first_ref[tile], count_ref[tile]
        for steps in range(1, CHUNKS + 1):
            pl.when(count == steps)(lambda steps=steps: whole_tile(tile, first, steps))
        return carry

    lax.fori_loop(0, TILES, query_step, 0)

    def key_grads(at):
        rows = token_rows(at)
        return [dk[rows, :].T[0:FULL] * SCALE, dv[rows, :].T[0:FULL]]

    def hand_out(keep, give, block, wholes):
        first, second = halves(side, wholes)
        keep[block], give[block] = first.astype(BF), second.astype(BF)

    for block in range(SIDE):
        tile, cols = block // PART, slice((block % PART) * TOK, (block % PART + 1) * TOK)
        mixed = mixed_t[tile, :, cols]
        mixed_ref[block] = mixed
        hand_out(keep_asked_ref, give_asked_ref, block, [mixed.astype(F32), dq[tile, :, cols]])
        hand_out(keep_ref, give_ref, block, key_grads(EDGE + block))
    for block in range(EDGE):
        hand_out(keep_ref, give_ref, SIDE + block, key_grads(block + NEAR * (1 - side)))
        far_ref[block] = jnp.concatenate(key_grads(block + NEAR * side), 0).astype(BF)


def attend(own, near, asked, far_own, far_other):
    whole = jax.ShapeDtypeStruct((SIDE, FULL, TOK), BF)
    keys = jax.ShapeDtypeStruct((NEAR, FULL, TOK), BF)
    edge = jax.ShapeDtypeStruct((EDGE, 2 * FULL, TOK), BF)
    row_form = pltpu.VMEM((ROOM * TOK, TOK), BF)
    column_form = pltpu.VMEM((ROOM, 80, TOK), BF)
    return pl.pallas_call(
        attend_body,
        out_shape=(whole, whole, whole, keys, keys, edge),
        in_specs=[WHOLE] * 5,
        out_specs=(WHOLE,) * 6,
        cost_estimate=cost(20),
        scratch_shapes=[
            row_form, column_form, row_form, column_form,
            pltpu.VMEM((TILES, TOK, TILE), BF), pltpu.VMEM((TILES, TILE, TOK), BF),
            pltpu.VMEM((TILES, TOK, TILE), BF), pltpu.VMEM((TILES, TILE, TOK), BF),
            pltpu.VMEM((CHUNKS, STEP * TOK, TILE), F32),
            pltpu.VMEM((CHUNKS, STEP * TOK, TILE), F32),
            pltpu.VMEM((TILES, FULL, TILE), BF),
            pltpu.VMEM((TILES, FULL, TILE), F32),
            pltpu.VMEM((ROOM * TOK, TOK), F32),
            pltpu.VMEM((ROOM * TOK, TOK), F32),
            pltpu.VMEM((SPAN, 8, TOK), F32),
            pltpu.SMEM((TILES,), jnp.int32),
            pltpu.SMEM((TILES,), jnp.int32),
        ],
        compiler_params=params(24),
        name="attend",
    )(own, near, asked, far_own, far_other)


def weight_term_body(mixed, other, branch, *refs):
    out_refs, total = refs[:PLANES], refs[PLANES]
    step = pl.program_id(0)
    side = core()
    left, right = [], []
    for chip in range(CHIPS):
        for at in range(2):
            block = 2 * (CHIPS * step + chip) + (side if at == 0 else 1 - side)
            place = lax.rem(block, SIDE)
            foreign = jnp.where(block // SIDE == side, 0, 1)
            right.append(pick(foreign, mixed[place].astype(F32), other[place].astype(F32)))
            left.append(branch[chip, at])
    term = lax.dot_general(
        jnp.concatenate(left, 1), jnp.concatenate(right, 1).astype(BF), (((1,), (1,)), ((), ())),
        preferred_element_type=F32,
    )

    @pl.when(step == 0)
    def _():
        total[:, 0:FULL] = term
        total[:, FULL:] = jnp.zeros((WIDTH // 2, TOK - FULL), F32)

    @pl.when(step > 0)
    def _():
        total[:, 0:FULL] += term

    @pl.when(step == HEADS // CHIPS - 1)
    def _():
        plane = lax.axis_index("dp") // PLANE
        for away in range(PLANES):
            start = pl.multiple_of(lax.rem(plane + away, PLANES) * SHARE, 8)
            out_refs[away][...] = total[pl.ds(start, SHARE), :].astype(BF)


def weight_term(mixed, other, branch):
    share = pl.BlockSpec((SHARE, TOK), lambda i: (0, 0))
    held = pl.BlockSpec((SIDE, FULL, TOK), lambda i: (0, 0, 0))
    return pl.pallas_call(
        weight_term_body,
        grid=(HEADS // CHIPS,),
        out_shape=(jax.ShapeDtypeStruct((SHARE, TOK), BF),) * PLANES,
        in_specs=[held, held, pl.BlockSpec((CHIPS, 2, WIDTH // 2, TOK), lambda i: (i, 0, 0, 0))],
        out_specs=(share,) * PLANES,
        scratch_shapes=[pltpu.VMEM((WIDTH // 2, TOK), F32)],
        compiler_params=params(16),
        cost_estimate=cost(4),
        name="weight_term",
    )(mixed, other, branch)


def fold_body(keep, give, far, keep_ref, give_ref):
    side = core()
    keep_ref[...] = keep[...]
    give_ref[...] = give[...]
    for block in range(EDGE):
        place = block + (SIDE - EDGE) * side
        whole = far[block].astype(F32)
        first, second = halves(side, [whole[0:FULL], whole[FULL:]])
        keep_ref[place] = (keep[place].astype(F32) + first).astype(BF)
        give_ref[place] = (give[place].astype(F32) + second).astype(BF)


def fold(keep, give, far):
    keys = jax.ShapeDtypeStruct((NEAR, FULL, TOK), BF)
    return pl.pallas_call(
        fold_body,
        out_shape=(keys, keys),
        in_specs=[WHOLE] * 3,
        out_specs=(WHOLE,) * 2,
        compiler_params=params(8),
        cost_estimate=cost(1),
        name="fold",
    )(keep, give, far)


def join_body(keep_asked, got_asked, keep, got, term, term1, term2, term3, out_ref, total, pairs):
    side = core()
    total[0:SHARE] = sum(one[...].astype(F32) for one in (term, term1, term2, term3))
    total[SHARE:] = jnp.zeros((8, TOK), F32)
    mine, others = SIDE * side, SIDE * (1 - side)
    for block in range(SIDE):
        pairs[mine + block] = keep[block].astype(F32)
        pairs[others + block] = got[block].astype(F32)
    for block in range(EDGE):
        pairs[others + (SIDE - EDGE) * side + block] += keep[SIDE + block].astype(F32)
        pairs[mine + (SIDE - EDGE) * (1 - side) + block] += got[SIDE + block].astype(F32)
    for block in range(SIDE):
        tail = total[block * FINAL : block * FINAL + 16, :]
        for start, asked in ((mine, keep_asked), (others, got_asked)):
            whole = [asked[block].astype(F32), pairs[start + block], tail]
            out_ref[start + block] = jnp.concatenate(whole, 0).astype(BF)


def join(*values):
    return pl.pallas_call(
        join_body,
        out_shape=jax.ShapeDtypeStruct((PLANE, 2 * FULL + 16, TOK), BF),
        in_specs=[WHOLE] * 8,
        out_specs=WHOLE,
        scratch_shapes=[pltpu.VMEM((SHARE + 8, TOK), F32), pltpu.VMEM((PLANE, FULL, TOK), F32)],
        compiler_params=params(12),
        cost_estimate=cost(1),
        name="join",
    )(*values)


def finish_body(packed, residual, tags, gate, weight, bias, out_ref, dq_ref, dk_ref, dv_ref, dw_ref):
    def rows(at):
        low = slice(at * HALF, (at + 1) * HALF)
        high = slice(at * HALF, at * HALF + HEAD_DIM - HALF)
        parts = []
        for head in range(HEADS):
            parts += [packed[2 * head].astype(F32)[low], packed[2 * head + 1].astype(F32)[high]]
        return jnp.concatenate(parts, 0).T.astype(BF)

    gate_rows = lax.dot_general(
        clip_onehot(tags), gate[...], (((0,), (0,)), ((), ())),
        precision=lax.Precision.HIGHEST, preferred_element_type=F32,
    )
    projected = mm(rows(0), weight[...]) + bias[...].reshape(1, WIDTH)
    out_ref[...] = (residual[...].astype(F32) + gate_rows * projected).astype(BF)
    dq_ref[...] = rows(1)
    dk_ref[...] = rows(2)
    dv_ref[...] = rows(3)
    source = lax.rem(lax.axis_index("dp"), PLANE) // SIDE
    tails = [packed[2 * head + source, 2 * FULL :].astype(F32)[:, 0:HEAD_DIM] for head in range(HEADS)]
    dw_ref[...] = jnp.concatenate(tails, 1)[0:FINAL]


def finish(packed, residual, tags, gate, weight, bias):
    return pl.pallas_call(
        finish_body,
        out_shape=(jax.ShapeDtypeStruct((TOK, WIDTH), BF),) * 4 + (jax.ShapeDtypeStruct((FINAL, WIDTH), F32),),
        in_specs=[WHOLE] * 6,
        out_specs=(WHOLE,) * 5,
        compiler_params=params(16),
        cost_estimate=cost(3),
        name="finish",
    )(packed, residual, tags, gate, weight, bias)


def sent(values, target):
    pairs = [(i, target(i)) for i in range(DEVICES)]
    return lax.ppermute(values, "dp", [(i, j) for i, j in pairs if 0 <= j < DEVICES])


def other_core(device):
    return device ^ 1


def cross(device):
    return device - PLANE + 1 if device % 2 == 0 else device + PLANE - 1


def planes_on(count):
    return lambda device: (device + count * PLANE) % DEVICES


def traded(values):
    groups = [[plane * PLANE + i for i in range(PLANE)] for plane in range(PLANES)]
    return lax.all_to_all(values, "dp", 0, 0, axis_index_groups=groups, tiled=True)


def some_blocks(values, start, rows, count):
    return lax.dynamic_slice(values, (start, rows, 0), (count, FULL, TOK))


def shards(query, key, value, residual, tags, gate, weight, bias, out_grad):
    me = lax.axis_index("dp")
    side = me % 2
    whole_branch, branch, branch_away = branch_columns(out_grad, tags, gate)
    chunk = pack(query, key, value, tags, whole_branch, weight)
    branch_got, chunk = lax.optimization_barrier((sent(branch_away, other_core), chunk))
    branch = fill(branch, branch_got)
    cores = [[plane * PLANE + 2 * chip + at for chip in range(HEADS)] for plane in range(PLANES) for at in range(2)]
    gathered = lax.all_gather(branch, "dp", axis=0, axis_index_groups=cores, tiled=False)
    own = traded(chunk)
    near = sent(some_blocks(own, (SIDE - EDGE) * (1 - side), 0, NEAR), other_core)
    asked = sent(some_blocks(own, SIDE * (1 - side), FULL, SIDE), other_core)
    far_other = sent(some_blocks(own, (PLANE - EDGE) * side, 0, EDGE), cross)
    far_own = sent(some_blocks(near, SIDE * side, 0, EDGE), cross)
    mixed, keep_asked, give_asked, keep, give, far = attend(own, near, asked, far_own, far_other)
    far = sent(far, cross)
    mixed_other = sent(mixed, other_core)
    got_asked = sent(give_asked, other_core)
    term, *terms = weight_term(mixed, mixed_other, gathered)
    terms = [sent(one, planes_on(away + 1)) for away, one in enumerate(terms)]
    far, _ = lax.optimization_barrier((far, term))
    keep, give = fold(keep, give, far)
    got = sent(give, other_core)
    packed = traded(join(keep_asked, got_asked, keep, got, term, *terms))
    block_out, dq, dk, dv, dw = finish(packed, residual, tags, gate, weight, bias)
    return block_out, dq, dk, dv, dw.T


def solution(mesh):
    rows = P("dp", None)
    in_specs = (rows, rows, rows, rows, P("dp"), P(), P(), P(), rows)
    out_specs = (rows,) * 4 + (P(None, "dp"),)
    return jax.shard_map(shards, mesh=mesh, in_specs=in_specs, out_specs=out_specs, check_vma=False)
```

```python
import math

import jax
import jax.numpy as jnp
from jax import lax
from jax.experimental import pallas as pl
from jax.experimental.pallas import tpu as pltpu
from jax.sharding import PartitionSpec as P

HEADS = 16
HEAD_DIM = 72
WIDTH = HEADS * HEAD_DIM
TOK = 128
DEVICES = 128
PLANES = 4
PLANE = 32
SIDE = 16
EDGE = 7
SPAN = SIDE + 2 * EDGE
NEAR = SIDE + EDGE
TILE = 256
TILES = SIDE * TOK // TILE
PART = TILE // TOK
STEP = 4
ROOM = SPAN + STEP - 1
CHUNKS = 4
HALF = 40
FULL = 2 * HALF
FINAL = WIDTH // DEVICES
CHIPS = 4
SHARE = WIDTH // PLANES // 2
CLIPS = 32
SCALE = 1.0 / math.sqrt(HEAD_DIM)
SCALE2 = SCALE / math.log(2.0)
FAR = -1e30
BF = jnp.bfloat16
F32 = jnp.float32

WHOLE = pl.BlockSpec(memory_space=pltpu.VMEM)
FAR_AWAY = pl.BlockSpec(memory_space=pltpu.HBM)


def params(mebibytes):
    return pltpu.CompilerParams(vmem_limit_bytes=mebibytes * 1024 * 1024)


def cost(micros):
    return pl.CostEstimate(flops=int(micros * 4e8), bytes_accessed=int(micros * 2e6), transcendentals=0)


def mm(left, right):
    return jnp.dot(left, right, preferred_element_type=F32)


def clip_onehot(tags):
    ids = lax.broadcasted_iota(jnp.int32, (CLIPS, TOK), 0)
    return (ids == tags[...].reshape(1, TOK)).astype(F32)


def core():
    return lax.axis_index("dp") % 2


def pick(flag, first, second):
    return jnp.where(jnp.full(first.shape, flag, jnp.int32) == 0, first, second)


def branch_body(out_grad, tags, gate, branch_ref, mine_ref, theirs_ref):
    gate_t = lax.dot_general(
        gate[...], clip_onehot(tags), (((0,), (0,)), ((), ())),
        precision=lax.Precision.HIGHEST, preferred_element_type=F32,
    )
    branch_t = (out_grad[...].astype(F32).T * gate_t).astype(BF)
    branch_ref[...] = branch_t
    wide = branch_t.astype(F32)
    halves = []
    for side in range(2):
        starts = [(2 * plane + side) * SHARE for plane in range(PLANES)]
        halves.append(jnp.concatenate([wide[start : start + SHARE] for start in starts], 0))
    side = core()
    mine_ref[0] = pick(side, halves[0], halves[1]).astype(BF)
    mine_ref[1] = jnp.zeros((WIDTH // 2, TOK), BF)
    theirs_ref[...] = pick(side, halves[1], halves[0]).astype(BF)


def branch_columns(out_grad, tags, gate):
    return pl.pallas_call(
        branch_body,
        out_shape=(
            jax.ShapeDtypeStruct((WIDTH, TOK), BF),
            jax.ShapeDtypeStruct((2, WIDTH // 2, TOK), BF),
            jax.ShapeDtypeStruct((WIDTH // 2, TOK), BF),
        ),
        in_specs=[WHOLE] * 3,
        out_specs=(WHOLE,) * 3,
        compiler_params=params(56),
        cost_estimate=cost(2),
        name="branch_columns",
    )(out_grad, tags, gate)


def fill_body(_, got, out_ref, sem):
    load = pltpu.make_async_copy(got, out_ref.at[1], sem)
    load.start()
    load.wait()


def fill(branch, got):
    return pl.pallas_call(
        fill_body,
        out_shape=jax.ShapeDtypeStruct(branch.shape, BF),
        in_specs=[FAR_AWAY] * 2,
        out_specs=FAR_AWAY,
        input_output_aliases={0: 0},
        scratch_shapes=[pltpu.SemaphoreType.DMA],
        compiler_params=params(16),
        cost_estimate=cost(1),
        name="fill",
    )(branch, got)


def pack_body(query, key, value, weight, tags, branch, chunk_ref, query_here, key_here, value_here, weight_here, sems):
    loads = []
    for at, (source, here) in enumerate(
        ((key, key_here), (value, value_here), (query, query_here), (weight, weight_here))
    ):
        loads.append(pltpu.make_async_copy(source, here, sems.at[at]))
        loads[-1].start()
    tag_rows = jnp.broadcast_to(tags[...].reshape(1, TOK).astype(F32) + 1.0, (8, TOK))
    blank = jnp.zeros((8, TOK), F32)
    loads[0].wait()
    key_t = key_here[...].astype(F32).T
    loads[1].wait()
    value_t = value_here[...].astype(F32).T
    loads[2].wait()
    query_t = query_here[...].astype(F32).T
    loads[3].wait()
    grad_t = mm(weight_here[...], branch[...])
    for head in range(HEADS):
        start = head * HEAD_DIM
        low, high = slice(start, start + HALF), slice(start + HALF, start + HEAD_DIM)
        whole = [key_t[low], value_t[low], query_t[low], grad_t[low]]
        chunk_ref[2 * head] = jnp.concatenate(whole, 0).astype(BF)
        whole = [key_t[high], tag_rows, value_t[high], blank, query_t[high], blank, grad_t[high], blank]
        chunk_ref[2 * head + 1] = jnp.concatenate(whole, 0).astype(BF)


def pack(query, key, value, tags, branch, weight):
    rows = pltpu.VMEM((TOK, WIDTH), BF)
    return pl.pallas_call(
        pack_body,
        out_shape=jax.ShapeDtypeStruct((PLANE, 2 * FULL, TOK), BF),
        in_specs=[FAR_AWAY] * 4 + [WHOLE] * 2,
        out_specs=WHOLE,
        scratch_shapes=[rows, rows, rows, pltpu.VMEM((WIDTH, WIDTH), BF), pltpu.SemaphoreType.DMA((4,))],
        compiler_params=params(61),
        cost_estimate=cost(4),
        name="pack",
    )(query, key, value, weight, tags, branch)


def filled(piece, extra):
    rows = [piece] + extra
    have = sum(part.shape[0] for part in rows)
    if have < TOK:
        rows.append(jnp.zeros((TOK - have, TOK), F32))
    return jnp.concatenate(rows, 0)


def natural(side, own, other):
    own, other = own.astype(F32), other.astype(F32)
    low, high = pick(side, own, other), pick(side, other, own)
    return [jnp.concatenate([low[rows], high[rows]], 0) for rows in (slice(0, HALF), slice(HALF, FULL))]


def halves(side, wholes):
    low = jnp.concatenate([whole[0:HALF] for whole in wholes], 0)
    high = jnp.concatenate([whole[HALF:] for whole in wholes], 0)
    return pick(side, low, high), pick(side, high, low)


def window(side, own, near, far_own, far_other):
    for block in range(NEAR):
        at = block + EDGE * (1 - side)
        yield (at,) + tuple(natural(side, own[block + (SIDE - EDGE) * side, 0:FULL], near[block]))
    for block in range(EDGE):
        yield (block + NEAR * side,) + tuple(natural(side, far_own[block], far_other[block]))


def token_rows(block):
    return pl.ds(pl.multiple_of(block * TOK, TOK), TOK)


def same_clip(clip, same, other):
    ids = lax.broadcasted_iota(jnp.int32, (CLIPS, TOK), 0).astype(F32) + 1.0
    return jnp.where(ids == clip, same, other)


def lay_out_keys(block, key, key_n, key_t, clips):
    clip = key[HEAD_DIM : HEAD_DIM + 1]
    clips[block] = key[HEAD_DIM:]
    held = filled(key[0:HEAD_DIM], [same_clip(clip, 0.0, FAR)])
    key_n[token_rows(block), :] = held.T.astype(BF)
    if key_t is not None:
        key_t[block] = jnp.concatenate([key[0:HEAD_DIM], jnp.zeros((8, TOK), F32)], 0).astype(BF)


def key_padding(key_n, key_t):
    rows = slice(SPAN * TOK, ROOM * TOK)
    lane = lax.broadcasted_iota(jnp.int32, ((ROOM - SPAN) * TOK, TOK), 1)
    key_n[rows, :] = jnp.where((lane >= HEAD_DIM) & (lane < HEAD_DIM + CLIPS), FAR, 0.0).astype(BF)
    if key_t is not None:
        for block in range(SPAN, ROOM):
            key_t[block] = jnp.zeros((80, TOK), BF)


def key_ranges(clips, first_ref, count_ref):
    rows = [clips[block][0:1] for block in range(SPAN)]
    rows = [jnp.where(row == 0.0, 100.0, row) if at >= NEAR else row for at, row in enumerate(rows)]
    rows = jnp.concatenate(rows + [jnp.full((32 - SPAN, TOK), 100.0, F32)], 0)
    least = jnp.min(rows, axis=1, keepdims=True)
    most = jnp.max(rows, axis=1, keepdims=True)
    for tile in range(TILES):
        start = EDGE + tile * PART
        low, high = least[start : start + 1], most[start + PART - 1 : start + PART]
        first = jnp.sum(jnp.where(most < low, 1.0, 0.0)).astype(jnp.int32)
        end = jnp.sum(jnp.where(least <= high, 1.0, 0.0)).astype(jnp.int32)
        first_ref[tile] = first
        count_ref[tile] = (end - first + STEP - 1) // STEP


def side_by_side(ref, start):
    return jnp.concatenate([ref[start + at] for at in range(STEP)], 1)


def blocks(first, step):
    start = first + step * STEP
    return start, pl.ds(pl.multiple_of(start * TOK, TOK), STEP * TOK)


def attend_body(
    own, near, asked, far_own, far_other,
    mixed_ref, keep_asked_ref, give_asked_ref, both_ref, far_ref,
    key_n, key_t, value_n, value_t, query_t, query_n, grad_t, grad_n, held, pulls, mixed_t, dq, dk, dv,
    clips, first_ref, count_ref,
):
    side = core()
    for at, key, value in window(side, own, near, far_own, far_other):
        lay_out_keys(at, key, key_n, key_t, clips)
        value = filled(value[0:HEAD_DIM], [jnp.ones((8, TOK), F32)])
        value_n[token_rows(at), :] = value.T.astype(BF)
        value_t[at] = value[0:80].astype(BF)
    value_n[SPAN * TOK :, :] = jnp.zeros(((ROOM - SPAN) * TOK, TOK), BF)
    for block in range(SPAN, ROOM):
        value_t[block] = jnp.zeros((80, TOK), BF)
    key_padding(key_n, key_t)
    for block in range(SIDE):
        tile, cols = block // PART, slice((block % PART) * TOK, (block % PART + 1) * TOK)
        query, grad = natural(side, own[SIDE * side + block, FULL:], asked[block])
        query = filled(query[0:HEAD_DIM], [same_clip(clips[EDGE + block][0:1], 1.0, 0.0)])
        query_t[tile, :, cols] = query.astype(BF)
        query_n[tile, cols, :] = query.T.astype(BF)
        grad = filled(grad, [])
        grad_t[tile, :, cols] = grad.astype(BF)
        grad_n[tile, cols, :] = grad.T.astype(BF)
    key_ranges(clips, first_ref, count_ref)
    dk[...] = jnp.zeros_like(dk)
    dv[...] = jnp.zeros_like(dv)

    def whole_tile(tile, first, count):
        tops = []
        grad = grad_t[tile]
        for step in range(count):
            scores = mm(key_n[blocks(first, step)[1], :], query_t[tile])
            held[step] = scores
            tops.append(jnp.max(scores, axis=0, keepdims=True))
            pulls[step] = mm(value_n[blocks(first, step)[1], :], grad)
        top = tops[0]
        for other in tops[1:]:
            top = jnp.maximum(top, other)
        total = None
        for step in range(count):
            weights = jnp.exp2((held[step] - top) * SCALE2)
            held[step] = weights
            term = mm(side_by_side(value_t, blocks(first, step)[0]), weights.astype(BF))
            total = term if total is None else total + term
        inverse = 1.0 / total[HEAD_DIM : HEAD_DIM + 1]
        mixed = jnp.concatenate([total[0:HEAD_DIM] * inverse, jnp.zeros((8, TILE), F32)], 0).astype(BF)
        delta = jnp.sum(mixed.astype(F32) * grad[0:FULL].astype(F32), axis=0, keepdims=True)
        mixed_t[tile] = mixed
        total = None
        for step in range(count):
            start, rows = blocks(first, step)
            prob = held[step] * inverse
            pull = pulls[step]
            dv[rows, :] += mm(prob.astype(BF), grad_n[tile])
            score_grad = (prob * (pull - delta)).astype(BF)
            dk[rows, :] += mm(score_grad, query_n[tile])
            term = mm(side_by_side(key_t, start), score_grad)
            total = term if total is None else total + term
        dq[tile] = total * SCALE

    def query_step(tile, carry):
        first, count = first_ref[tile], count_ref[tile]
        for steps in range(1, CHUNKS + 1):
            pl.when(count == steps)(lambda steps=steps: whole_tile(tile, first, steps))
        return carry

    lax.fori_loop(0, TILES, query_step, 0)

    def key_grads(at):
        rows = token_rows(at)
        return [dk[rows, :].T[0:FULL] * SCALE, dv[rows, :].T[0:FULL]]

    keep_ref, give_ref = both_ref.at[0:NEAR], both_ref.at[NEAR : 2 * NEAR]

    def hand_out(keep, give, block, wholes):
        first, second = halves(side, wholes)
        keep[block], give[block] = first.astype(BF), second.astype(BF)

    for block in range(SIDE):
        tile, cols = block // PART, slice((block % PART) * TOK, (block % PART + 1) * TOK)
        mixed = mixed_t[tile, :, cols]
        mixed_ref[block] = mixed
        hand_out(keep_asked_ref, give_asked_ref, block, [mixed.astype(F32), dq[tile, :, cols]])
        hand_out(keep_ref, give_ref, block, key_grads(EDGE + block))
    for block in range(EDGE):
        hand_out(keep_ref, give_ref, SIDE + block, key_grads(block + NEAR * (1 - side)))
        far_ref[block] = jnp.concatenate(key_grads(block + NEAR * side), 0).astype(BF)


def attend(own, near, asked, far_own, far_other):
    whole = jax.ShapeDtypeStruct((SIDE, FULL, TOK), BF)
    both = jax.ShapeDtypeStruct((2 * NEAR, FULL, TOK), BF)
    edge = jax.ShapeDtypeStruct((EDGE, 2 * FULL, TOK), BF)
    row_form = pltpu.VMEM((ROOM * TOK, TOK), BF)
    column_form = pltpu.VMEM((ROOM, 80, TOK), BF)
    return pl.pallas_call(
        attend_body,
        out_shape=(whole, whole, whole, both, edge),
        in_specs=[WHOLE] * 5,
        out_specs=(WHOLE,) * 5,
        cost_estimate=cost(20),
        scratch_shapes=[
            row_form, column_form, row_form, column_form,
            pltpu.VMEM((TILES, TOK, TILE), BF), pltpu.VMEM((TILES, TILE, TOK), BF),
            pltpu.VMEM((TILES, TOK, TILE), BF), pltpu.VMEM((TILES, TILE, TOK), BF),
            pltpu.VMEM((CHUNKS, STEP * TOK, TILE), F32),
            pltpu.VMEM((CHUNKS, STEP * TOK, TILE), F32),
            pltpu.VMEM((TILES, FULL, TILE), BF),
            pltpu.VMEM((TILES, FULL, TILE), F32),
            pltpu.VMEM((ROOM * TOK, TOK), F32),
            pltpu.VMEM((ROOM * TOK, TOK), F32),
            pltpu.VMEM((SPAN, 8, TOK), F32),
            pltpu.SMEM((TILES,), jnp.int32),
            pltpu.SMEM((TILES,), jnp.int32),
        ],
        compiler_params=params(24),
        name="attend",
    )(own, near, asked, far_own, far_other)


def weight_term_body(mixed, other, branch, *refs):
    out_refs, total = refs[:PLANES], refs[PLANES]
    step = pl.program_id(0)
    side = core()
    left, right = [], []
    for chip in range(CHIPS):
        for at in range(2):
            block = 2 * (CHIPS * step + chip) + (side if at == 0 else 1 - side)
            place = lax.rem(block, SIDE)
            foreign = jnp.where(block // SIDE == side, 0, 1)
            right.append(pick(foreign, mixed[place].astype(F32), other[place].astype(F32)))
            left.append(branch[chip, at])
    term = lax.dot_general(
        jnp.concatenate(left, 1), jnp.concatenate(right, 1).astype(BF), (((1,), (1,)), ((), ())),
        preferred_element_type=F32,
    )

    @pl.when(step == 0)
    def _():
        total[:, 0:FULL] = term
        total[:, FULL:] = jnp.zeros((WIDTH // 2, TOK - FULL), F32)

    @pl.when(step > 0)
    def _():
        total[:, 0:FULL] += term

    @pl.when(step == HEADS // CHIPS - 1)
    def _():
        plane = lax.axis_index("dp") // PLANE
        for away in range(PLANES):
            start = pl.multiple_of(lax.rem(plane + away, PLANES) * SHARE, 8)
            out_refs[away][...] = total[pl.ds(start, SHARE), :].astype(BF)


def weight_term(mixed, other, branch):
    share = pl.BlockSpec((SHARE, TOK), lambda i: (0, 0))
    held = pl.BlockSpec((SIDE, FULL, TOK), lambda i: (0, 0, 0))
    return pl.pallas_call(
        weight_term_body,
        grid=(HEADS // CHIPS,),
        out_shape=(jax.ShapeDtypeStruct((SHARE, TOK), BF),) * PLANES,
        in_specs=[held, held, pl.BlockSpec((CHIPS, 2, WIDTH // 2, TOK), lambda i: (i, 0, 0, 0))],
        out_specs=(share,) * PLANES,
        scratch_shapes=[pltpu.VMEM((WIDTH // 2, TOK), F32)],
        compiler_params=params(16),
        cost_estimate=cost(4),
        name="weight_term",
    )(mixed, other, branch)


def fold_body(both, far, keep_ref, give_ref):
    side = core()
    keep, give = both.at[0:NEAR], both.at[NEAR : 2 * NEAR]
    keep_ref[...] = keep[...]
    give_ref[...] = give[...]
    for block in range(EDGE):
        place = block + (SIDE - EDGE) * side
        whole = far[block].astype(F32)
        first, second = halves(side, [whole[0:FULL], whole[FULL:]])
        keep_ref[place] = (keep[place].astype(F32) + first).astype(BF)
        give_ref[place] = (give[place].astype(F32) + second).astype(BF)


def fold(both, far):
    keys = jax.ShapeDtypeStruct((NEAR, FULL, TOK), BF)
    return pl.pallas_call(
        fold_body,
        out_shape=(keys, keys),
        in_specs=[WHOLE] * 2,
        out_specs=(WHOLE,) * 2,
        compiler_params=params(8),
        cost_estimate=cost(1),
        name="fold",
    )(both, far)


def join_asked_body(keep, got, out_ref):
    side = core()
    for block in range(SIDE):
        out_ref[SIDE * side + block] = keep[block]
        out_ref[SIDE * (1 - side) + block] = got[block]


def join_asked(keep, got):
    return pl.pallas_call(
        join_asked_body,
        out_shape=jax.ShapeDtypeStruct((PLANE, FULL, TOK), BF),
        in_specs=[WHOLE] * 2,
        out_specs=WHOLE,
        compiler_params=params(8),
        cost_estimate=cost(1),
        name="join_asked",
    )(keep, got)


def join_body(keep, got, term, term1, term2, term3, out_ref, total, pairs):
    side = core()
    total[0:SHARE] = sum(one[...].astype(F32) for one in (term, term1, term2, term3))
    total[SHARE:] = jnp.zeros((8, TOK), F32)
    mine, others = SIDE * side, SIDE * (1 - side)
    for block in range(SIDE):
        pairs[mine + block] = keep[block].astype(F32)
        pairs[others + block] = got[block].astype(F32)
    for block in range(EDGE):
        pairs[others + (SIDE - EDGE) * side + block] += keep[SIDE + block].astype(F32)
        pairs[mine + (SIDE - EDGE) * (1 - side) + block] += got[SIDE + block].astype(F32)
    for block in range(PLANE):
        start = (block % SIDE) * FINAL
        out_ref[block] = jnp.concatenate([pairs[block], total[start : start + 16, :]], 0).astype(BF)


def join(*values):
    return pl.pallas_call(
        join_body,
        out_shape=jax.ShapeDtypeStruct((PLANE, FULL + 16, TOK), BF),
        in_specs=[WHOLE] * 6,
        out_specs=WHOLE,
        scratch_shapes=[pltpu.VMEM((SHARE + 8, TOK), F32), pltpu.VMEM((PLANE, FULL, TOK), F32)],
        compiler_params=params(12),
        cost_estimate=cost(1),
        name="join",
    )(*values)


def all_heads(packed, at):
    low = slice(at * HALF, (at + 1) * HALF)
    high = slice(at * HALF, at * HALF + HEAD_DIM - HALF)
    parts = []
    for head in range(HEADS):
        parts += [packed[2 * head].astype(F32)[low], packed[2 * head + 1].astype(F32)[high]]
    return jnp.concatenate(parts, 0).T.astype(BF)


def finish_asked_body(packed, residual, tags, gate, weight, bias, out_ref, dq_ref):
    gate_rows = lax.dot_general(
        clip_onehot(tags), gate[...], (((0,), (0,)), ((), ())),
        precision=lax.Precision.HIGHEST, preferred_element_type=F32,
    )
    projected = mm(all_heads(packed, 0), weight[...]) + bias[...].reshape(1, WIDTH)
    out_ref[...] = (residual[...].astype(F32) + gate_rows * projected).astype(BF)
    dq_ref[...] = all_heads(packed, 1)


def finish_asked(packed, residual, tags, gate, weight, bias):
    return pl.pallas_call(
        finish_asked_body,
        out_shape=(jax.ShapeDtypeStruct((TOK, WIDTH), BF),) * 2,
        in_specs=[WHOLE] * 6,
        out_specs=(WHOLE,) * 2,
        compiler_params=params(16),
        cost_estimate=cost(2),
        name="finish_asked",
    )(packed, residual, tags, gate, weight, bias)


def finish_body(packed, dk_ref, dv_ref, dw_ref):
    dk_ref[...] = all_heads(packed, 0)
    dv_ref[...] = all_heads(packed, 1)
    source = lax.rem(lax.axis_index("dp"), PLANE) // SIDE
    tails = [packed[2 * head + source, FULL:].astype(F32)[:, 0:HEAD_DIM] for head in range(HEADS)]
    dw_ref[...] = jnp.concatenate(tails, 1)[0:FINAL]


def finish(packed):
    return pl.pallas_call(
        finish_body,
        out_shape=(jax.ShapeDtypeStruct((TOK, WIDTH), BF),) * 2 + (jax.ShapeDtypeStruct((FINAL, WIDTH), F32),),
        in_specs=[WHOLE],
        out_specs=(WHOLE,) * 3,
        compiler_params=params(16),
        cost_estimate=cost(1),
        name="finish",
    )(packed)


def sent(values, target):
    pairs = [(i, target(i)) for i in range(DEVICES)]
    return lax.ppermute(values, "dp", [(i, j) for i, j in pairs if 0 <= j < DEVICES])


def other_core(device):
    return device ^ 1


def cross(device):
    return device - PLANE + 1 if device % 2 == 0 else device + PLANE - 1


def planes_on(count):
    return lambda device: (device + count * PLANE) % DEVICES


def traded(values):
    groups = [[plane * PLANE + i for i in range(PLANE)] for plane in range(PLANES)]
    return lax.all_to_all(values, "dp", 0, 0, axis_index_groups=groups, tiled=True)


def some_blocks(values, start, rows, count):
    return lax.dynamic_slice(values, (start, rows, 0), (count, FULL, TOK))


def shards(query, key, value, residual, tags, gate, weight, bias, out_grad):
    me = lax.axis_index("dp")
    side = me % 2
    whole_branch, branch, branch_away = branch_columns(out_grad, tags, gate)
    chunk = pack(query, key, value, tags, whole_branch, weight)
    branch_got, chunk = lax.optimization_barrier((sent(branch_away, other_core), chunk))
    branch = fill(branch, branch_got)
    cores = [[plane * PLANE + 2 * chip + at for chip in range(HEADS)] for plane in range(PLANES) for at in range(2)]
    gathered = lax.all_gather(branch, "dp", axis=0, axis_index_groups=cores, tiled=False)
    own = traded(chunk)
    near = sent(some_blocks(own, (SIDE - EDGE) * (1 - side), 0, NEAR), other_core)
    asked = sent(some_blocks(own, SIDE * (1 - side), FULL, SIDE), other_core)
    far_other = sent(some_blocks(own, (PLANE - EDGE) * side, 0, EDGE), cross)
    far_own = sent(some_blocks(near, SIDE * side, 0, EDGE), cross)
    mixed, keep_asked, give_asked, both, far = attend(own, near, asked, far_own, far_other)
    joined = join_asked(keep_asked, sent(give_asked, other_core))
    asked_back = traded(joined)
    far = sent(far, cross)
    mixed_other, _ = lax.optimization_barrier((sent(mixed, other_core), joined))
    term, *terms = weight_term(mixed, mixed_other, gathered)
    terms = [sent(one, planes_on(away + 1)) for away, one in enumerate(terms)]
    far, _ = lax.optimization_barrier((far, term))
    keep, give = fold(both, far)
    got = sent(give, other_core)
    keys_back = traded(join(keep, got, term, *terms))
    block_out, dq = finish_asked(asked_back, residual, tags, gate, weight, bias)
    dk, dv, dw = finish(keys_back)
    return block_out, dq, dk, dv, dw.T


def solution(mesh):
    rows = P("dp", None)
    in_specs = (rows, rows, rows, rows, P("dp"), P(), P(), P(), rows)
    out_specs = (rows,) * 4 + (P(None, "dp"),)
    return jax.shard_map(shards, mesh=mesh, in_specs=in_specs, out_specs=out_specs, check_vma=False)
```

```python
import math

import jax
import jax.numpy as jnp
from jax import lax
from jax.experimental import pallas as pl
from jax.experimental.pallas import tpu as pltpu
from jax.sharding import PartitionSpec as P

HEADS = 16
HEAD_DIM = 72
WIDTH = HEADS * HEAD_DIM
TOK = 128
DEVICES = 128
PLANES = 4
PLANE = 32
SIDE = 16
EDGE = 7
SPAN = SIDE + 2 * EDGE
NEAR = SIDE + EDGE
TILE = 256
TILES = SIDE * TOK // TILE
PART = TILE // TOK
STEP = 4
ROOM = SPAN + STEP - 1
CHUNKS = 4
HALF = 40
FULL = 2 * HALF
FINAL = WIDTH // DEVICES
CHIPS = 4
SHARE = WIDTH // PLANES
CLIPS = 32
SCALE = 1.0 / math.sqrt(HEAD_DIM)
SCALE2 = SCALE / math.log(2.0)
FAR = -1e30
BF = jnp.bfloat16
F32 = jnp.float32

WHOLE = pl.BlockSpec(memory_space=pltpu.VMEM)
FAR_AWAY = pl.BlockSpec(memory_space=pltpu.HBM)


def params(mebibytes):
    return pltpu.CompilerParams(vmem_limit_bytes=mebibytes * 1024 * 1024)


def cost(micros):
    return pl.CostEstimate(flops=int(micros * 4e8), bytes_accessed=int(micros * 2e6), transcendentals=0)


def mm(left, right):
    return jnp.dot(left, right, preferred_element_type=F32)


def clip_onehot(tags):
    ids = lax.broadcasted_iota(jnp.int32, (CLIPS, TOK), 0)
    return (ids == tags[...].reshape(1, TOK)).astype(F32)


def core():
    return lax.axis_index("dp") % 2


def pick(flag, first, second):
    return jnp.where(jnp.full(first.shape, flag, jnp.int32) == 0, first, second)


def pack_body(
    query, key, value, out_grad, gate, weight, tags, chunk_ref, branch_ref,
    query_here, key_here, value_here, out_grad_here, gate_here, weight_here, sems,
):
    loads = {}
    for at, (name, source, here) in enumerate((
        ("out_grad", out_grad, out_grad_here), ("gate", gate, gate_here), ("key", key, key_here),
        ("value", value, value_here), ("query", query, query_here), ("weight", weight, weight_here),
    )):
        loads[name] = pltpu.make_async_copy(source, here, sems.at[at])
        loads[name].start()
    tag_rows = jnp.broadcast_to(tags[...].reshape(1, TOK).astype(F32) + 1.0, (8, TOK))
    blank = jnp.zeros((8, TOK), F32)
    onehot = clip_onehot(tags)
    loads["out_grad"].wait()
    out_grad_t = out_grad_here[...].astype(F32).T
    loads["gate"].wait()
    gate_t = lax.dot_general(
        gate_here[...], onehot, (((0,), (0,)), ((), ())),
        precision=lax.Precision.HIGHEST, preferred_element_type=F32,
    )
    branch = (out_grad_t * gate_t).astype(BF)
    branch_ref[...] = branch
    loads["key"].wait()
    key_t = key_here[...].astype(F32).T
    loads["value"].wait()
    value_t = value_here[...].astype(F32).T
    loads["query"].wait()
    query_t = query_here[...].astype(F32).T
    loads["weight"].wait()
    grad_t = mm(weight_here[...], branch)
    for head in range(HEADS):
        start = head * HEAD_DIM
        low, high = slice(start, start + HALF), slice(start + HALF, start + HEAD_DIM)
        whole = [key_t[low], value_t[low], query_t[low], grad_t[low]]
        chunk_ref[2 * head] = jnp.concatenate(whole, 0).astype(BF)
        whole = [key_t[high], tag_rows, value_t[high], blank, query_t[high], blank, grad_t[high], blank]
        chunk_ref[2 * head + 1] = jnp.concatenate(whole, 0).astype(BF)


def pack(query, key, value, out_grad, gate, weight, tags):
    rows = pltpu.VMEM((TOK, WIDTH), BF)
    return pl.pallas_call(
        pack_body,
        out_shape=(
            jax.ShapeDtypeStruct((PLANE, 2 * FULL, TOK), BF),
            jax.ShapeDtypeStruct((WIDTH, TOK), BF),
        ),
        in_specs=[FAR_AWAY] * 6 + [WHOLE],
        out_specs=(WHOLE,) * 2,
        scratch_shapes=[
            rows, rows, rows, rows, pltpu.VMEM((CLIPS, WIDTH), F32), pltpu.VMEM((WIDTH, WIDTH), BF),
            pltpu.SemaphoreType.DMA((6,)),
        ],
        compiler_params=params(61),
        cost_estimate=cost(5),
        name="pack",
    )(query, key, value, out_grad, gate, weight, tags)


def filled(piece, extra):
    rows = [piece] + extra
    have = sum(part.shape[0] for part in rows)
    if have < TOK:
        rows.append(jnp.zeros((TOK - have, TOK), F32))
    return jnp.concatenate(rows, 0)


def natural(side, own, other):
    own, other = own.astype(F32), other.astype(F32)
    low, high = pick(side, own, other), pick(side, other, own)
    return [jnp.concatenate([low[rows], high[rows]], 0) for rows in (slice(0, HALF), slice(HALF, FULL))]


def halves(side, wholes):
    low = jnp.concatenate([whole[0:HALF] for whole in wholes], 0)
    high = jnp.concatenate([whole[HALF:] for whole in wholes], 0)
    return pick(side, low, high), pick(side, high, low)


def window(side, own, near, far_own, far_other):
    for block in range(NEAR):
        at = block + EDGE * (1 - side)
        yield (at,) + tuple(natural(side, own[block + (SIDE - EDGE) * side, 0:FULL], near[block]))
    for block in range(EDGE):
        yield (block + NEAR * side,) + tuple(natural(side, far_own[block], far_other[block]))


def token_rows(block):
    return pl.ds(pl.multiple_of(block * TOK, TOK), TOK)


def same_clip(clip, same, other):
    ids = lax.broadcasted_iota(jnp.int32, (CLIPS, TOK), 0).astype(F32) + 1.0
    return jnp.where(ids == clip, same, other)


def lay_out_keys(block, key, key_n, key_t, clips):
    clip = key[HEAD_DIM : HEAD_DIM + 1]
    clips[block] = key[HEAD_DIM:]
    held = filled(key[0:HEAD_DIM], [same_clip(clip, 0.0, FAR)])
    key_n[token_rows(block), :] = held.T.astype(BF)
    if key_t is not None:
        key_t[block] = jnp.concatenate([key[0:HEAD_DIM], jnp.zeros((8, TOK), F32)], 0).astype(BF)


def key_padding(key_n, key_t):
    rows = slice(SPAN * TOK, ROOM * TOK)
    lane = lax.broadcasted_iota(jnp.int32, ((ROOM - SPAN) * TOK, TOK), 1)
    key_n[rows, :] = jnp.where((lane >= HEAD_DIM) & (lane < HEAD_DIM + CLIPS), FAR, 0.0).astype(BF)
    if key_t is not None:
        for block in range(SPAN, ROOM):
            key_t[block] = jnp.zeros((80, TOK), BF)


def key_ranges(clips, first_ref, count_ref):
    rows = [clips[block][0:1] for block in range(SPAN)]
    rows = [jnp.where(row == 0.0, 100.0, row) if at >= NEAR else row for at, row in enumerate(rows)]
    rows = jnp.concatenate(rows + [jnp.full((32 - SPAN, TOK), 100.0, F32)], 0)
    least = jnp.min(rows, axis=1, keepdims=True)
    most = jnp.max(rows, axis=1, keepdims=True)
    for tile in range(TILES):
        start = EDGE + tile * PART
        low, high = least[start : start + 1], most[start + PART - 1 : start + PART]
        first = jnp.sum(jnp.where(most < low, 1.0, 0.0)).astype(jnp.int32)
        end = jnp.sum(jnp.where(least <= high, 1.0, 0.0)).astype(jnp.int32)
        first_ref[tile] = first
        count_ref[tile] = (end - first + STEP - 1) // STEP


def side_by_side(ref, start):
    return jnp.concatenate([ref[start + at] for at in range(STEP)], 1)


def blocks(first, step):
    start = first + step * STEP
    return start, pl.ds(pl.multiple_of(start * TOK, TOK), STEP * TOK)


def attend_body(
    own, near, asked, far_own, far_other,
    mixed_ref, keep_asked_ref, give_asked_ref, keep_ref, give_ref, far_ref,
    key_n, key_t, value_n, value_t, query_t, query_n, grad_t, grad_n, held, pulls, mixed_t, dq, dk, dv,
    clips, first_ref, count_ref,
):
    side = core()
    for at, key, value in window(side, own, near, far_own, far_other):
        lay_out_keys(at, key, key_n, key_t, clips)
        value = filled(value[0:HEAD_DIM], [jnp.ones((8, TOK), F32)])
        value_n[token_rows(at), :] = value.T.astype(BF)
        value_t[at] = value[0:80].astype(BF)
    value_n[SPAN * TOK :, :] = jnp.zeros(((ROOM - SPAN) * TOK, TOK), BF)
    for block in range(SPAN, ROOM):
        value_t[block] = jnp.zeros((80, TOK), BF)
    key_padding(key_n, key_t)
    for block in range(SIDE):
        tile, cols = block // PART, slice((block % PART) * TOK, (block % PART + 1) * TOK)
        query, grad = natural(side, own[SIDE * side + block, FULL:], asked[block])
        query = filled(query[0:HEAD_DIM], [same_clip(clips[EDGE + block][0:1], 1.0, 0.0)])
        query_t[tile, :, cols] = query.astype(BF)
        query_n[tile, cols, :] = query.T.astype(BF)
        grad = filled(grad, [])
        grad_t[tile, :, cols] = grad.astype(BF)
        grad_n[tile, cols, :] = grad.T.astype(BF)
    key_ranges(clips, first_ref, count_ref)
    dk[...] = jnp.zeros_like(dk)
    dv[...] = jnp.zeros_like(dv)

    def whole_tile(tile, first, count):
        tops = []
        grad = grad_t[tile]
        for step in range(count):
            scores = mm(key_n[blocks(first, step)[1], :], query_t[tile])
            held[step] = scores
            tops.append(jnp.max(scores, axis=0, keepdims=True))
            pulls[step] = mm(value_n[blocks(first, step)[1], :], grad)
        top = tops[0]
        for other in tops[1:]:
            top = jnp.maximum(top, other)
        total = None
        for step in range(count):
            weights = jnp.exp2((held[step] - top) * SCALE2)
            held[step] = weights
            term = mm(side_by_side(value_t, blocks(first, step)[0]), weights.astype(BF))
            total = term if total is None else total + term
        inverse = 1.0 / total[HEAD_DIM : HEAD_DIM + 1]
        mixed = jnp.concatenate([total[0:HEAD_DIM] * inverse, jnp.zeros((8, TILE), F32)], 0).astype(BF)
        delta = jnp.sum(mixed.astype(F32) * grad[0:FULL].astype(F32), axis=0, keepdims=True)
        mixed_t[tile] = mixed
        total = None
        for step in range(count):
            start, rows = blocks(first, step)
            prob = held[step] * inverse
            pull = pulls[step]
            dv[rows, :] += mm(prob.astype(BF), grad_n[tile])
            score_grad = (prob * (pull - delta)).astype(BF)
            dk[rows, :] += mm(score_grad, query_n[tile])
            term = mm(side_by_side(key_t, start), score_grad)
            total = term if total is None else total + term
        dq[tile] = total * SCALE

    def query_step(tile, carry):
        first, count = first_ref[tile], count_ref[tile]
        for steps in range(1, CHUNKS + 1):
            pl.when(count == steps)(lambda steps=steps: whole_tile(tile, first, steps))
        return carry

    lax.fori_loop(0, TILES, query_step, 0)

    def key_grads(at):
        rows = token_rows(at)
        return [dk[rows, :].T[0:FULL] * SCALE, dv[rows, :].T[0:FULL]]

    def hand_out(keep, give, block, wholes):
        first, second = halves(side, wholes)
        keep[block], give[block] = first.astype(BF), second.astype(BF)

    for block in range(SIDE):
        tile, cols = block // PART, slice((block % PART) * TOK, (block % PART + 1) * TOK)
        mixed = mixed_t[tile, :, cols]
        mixed_ref[block] = mixed
        hand_out(keep_asked_ref, give_asked_ref, block, [mixed.astype(F32), dq[tile, :, cols]])
        hand_out(keep_ref, give_ref, block, key_grads(EDGE + block))
    for block in range(EDGE):
        hand_out(keep_ref, give_ref, SIDE + block, key_grads(block + NEAR * (1 - side)))
        far_ref[block] = jnp.concatenate(key_grads(block + NEAR * side), 0).astype(BF)


def attend(own, near, asked, far_own, far_other):
    whole = jax.ShapeDtypeStruct((SIDE, FULL, TOK), BF)
    keys = jax.ShapeDtypeStruct((NEAR, FULL, TOK), BF)
    edge = jax.ShapeDtypeStruct((EDGE, 2 * FULL, TOK), BF)
    row_form = pltpu.VMEM((ROOM * TOK, TOK), BF)
    column_form = pltpu.VMEM((ROOM, 80, TOK), BF)
    return pl.pallas_call(
        attend_body,
        out_shape=(whole, whole, whole, keys, keys, edge),
        in_specs=[WHOLE] * 5,
        out_specs=(WHOLE,) * 6,
        cost_estimate=cost(20),
        scratch_shapes=[
            row_form, column_form, row_form, column_form,
            pltpu.VMEM((TILES, TOK, TILE), BF), pltpu.VMEM((TILES, TILE, TOK), BF),
            pltpu.VMEM((TILES, TOK, TILE), BF), pltpu.VMEM((TILES, TILE, TOK), BF),
            pltpu.VMEM((CHUNKS, STEP * TOK, TILE), F32),
            pltpu.VMEM((CHUNKS, STEP * TOK, TILE), F32),
            pltpu.VMEM((TILES, FULL, TILE), BF),
            pltpu.VMEM((TILES, FULL, TILE), F32),
            pltpu.VMEM((ROOM * TOK, TOK), F32),
            pltpu.VMEM((ROOM * TOK, TOK), F32),
            pltpu.VMEM((SPAN, 8, TOK), F32),
            pltpu.SMEM((TILES,), jnp.int32),
            pltpu.SMEM((TILES,), jnp.int32),
        ],
        compiler_params=params(24),
        name="attend",
    )(own, near, asked, far_own, far_other)


def weight_term_body(mixed, other, branch, *refs):
    out_refs, total = refs[:PLANES], refs[PLANES]
    step = pl.program_id(0)
    side = core()
    left, right = [], []
    for at in range(CHIPS):
        chip = CHIPS * step + at
        place = 2 * lax.rem(chip, HEADS // 2) + side
        foreign = jnp.where(chip // (HEADS // 2) == side, 0, 1)
        right.append(pick(foreign, mixed[place].astype(F32), other[place].astype(F32)))
        left.append(branch[at])
    term = lax.dot_general(
        jnp.concatenate(left, 1), jnp.concatenate(right, 1).astype(BF), (((1,), (1,)), ((), ())),
        preferred_element_type=F32,
    )

    @pl.when(step == 0)
    def _():
        total[:, 0:FULL] = term
        total[:, FULL:] = jnp.zeros((WIDTH, TOK - FULL), F32)

    @pl.when(step > 0)
    def _():
        total[:, 0:FULL] += term

    @pl.when(step == HEADS // CHIPS - 1)
    def _():
        plane = lax.axis_index("dp") // PLANE
        for away in range(PLANES):
            start = pl.multiple_of(lax.rem(plane + away, PLANES) * SHARE, 8)
            out_refs[away][...] = total[pl.ds(start, SHARE), :].astype(BF)


def weight_term(mixed, other, branch):
    share = pl.BlockSpec((SHARE, TOK), lambda i: (0, 0))
    held = pl.BlockSpec((SIDE, FULL, TOK), lambda i: (0, 0, 0))
    return pl.pallas_call(
        weight_term_body,
        grid=(HEADS // CHIPS,),
        out_shape=(jax.ShapeDtypeStruct((SHARE, TOK), BF),) * PLANES,
        in_specs=[held, held, pl.BlockSpec((CHIPS, WIDTH, TOK), lambda i: (i, 0, 0))],
        out_specs=(share,) * PLANES,
        scratch_shapes=[pltpu.VMEM((WIDTH, TOK), F32)],
        compiler_params=params(16),
        cost_estimate=cost(4),
        name="weight_term",
    )(mixed, other, branch)


def fold_body(keep, give, far, keep_ref, give_ref):
    side = core()
    keep_ref[...] = keep[...]
    give_ref[...] = give[...]
    for block in range(EDGE):
        place = block + (SIDE - EDGE) * side
        whole = far[block].astype(F32)
        first, second = halves(side, [whole[0:FULL], whole[FULL:]])
        keep_ref[place] = (keep[place].astype(F32) + first).astype(BF)
        give_ref[place] = (give[place].astype(F32) + second).astype(BF)


def fold(keep, give, far):
    keys = jax.ShapeDtypeStruct((NEAR, FULL, TOK), BF)
    return pl.pallas_call(
        fold_body,
        out_shape=(keys, keys),
        in_specs=[WHOLE] * 3,
        out_specs=(WHOLE,) * 2,
        compiler_params=params(8),
        cost_estimate=cost(1),
        name="fold",
    )(keep, give, far)


def join_body(keep_asked, got_asked, keep, got, term, term1, term2, term3, out_ref, total, pairs):
    side = core()
    total[0:SHARE] = sum(one[...].astype(F32) for one in (term, term1, term2, term3))
    total[SHARE:] = jnp.zeros((8, TOK), F32)
    mine, others = SIDE * side, SIDE * (1 - side)
    for block in range(SIDE):
        pairs[mine + block] = keep[block].astype(F32)
        pairs[others + block] = got[block].astype(F32)
    for block in range(EDGE):
        pairs[others + (SIDE - EDGE) * side + block] += keep[SIDE + block].astype(F32)
        pairs[mine + (SIDE - EDGE) * (1 - side) + block] += got[SIDE + block].astype(F32)
    for block in range(SIDE):
        for start, asked in ((mine, keep_asked), (others, got_asked)):
            at = start + block
            whole = [asked[block].astype(F32), pairs[at], total[pl.ds(at * FINAL, 16), :]]
            out_ref[at] = jnp.concatenate(whole, 0).astype(BF)


def join(*values):
    return pl.pallas_call(
        join_body,
        out_shape=jax.ShapeDtypeStruct((PLANE, 2 * FULL + 16, TOK), BF),
        in_specs=[WHOLE] * 8,
        out_specs=WHOLE,
        scratch_shapes=[pltpu.VMEM((SHARE + 8, TOK), F32), pltpu.VMEM((PLANE, FULL, TOK), F32)],
        compiler_params=params(12),
        cost_estimate=cost(1),
        name="join",
    )(*values)


def finish_body(packed, residual, tags, gate, weight, bias, out_ref, dq_ref, dk_ref, dv_ref, dw_ref):
    def rows(at):
        low = slice(at * HALF, (at + 1) * HALF)
        high = slice(at * HALF, at * HALF + HEAD_DIM - HALF)
        parts = []
        for head in range(HEADS):
            parts += [packed[2 * head].astype(F32)[low], packed[2 * head + 1].astype(F32)[high]]
        return jnp.concatenate(parts, 0).T.astype(BF)

    gate_rows = lax.dot_general(
        clip_onehot(tags), gate[...], (((0,), (0,)), ((), ())),
        precision=lax.Precision.HIGHEST, preferred_element_type=F32,
    )
    projected = mm(rows(0), weight[...]) + bias[...].reshape(1, WIDTH)
    out_ref[...] = (residual[...].astype(F32) + gate_rows * projected).astype(BF)
    dq_ref[...] = rows(1)
    dk_ref[...] = rows(2)
    dv_ref[...] = rows(3)
    tails = []
    for head in range(HEADS):
        first, second = [packed[2 * head + at, 2 * FULL :].astype(F32) for at in range(2)]
        tails.append((first + second)[:, 0:HEAD_DIM])
    dw_ref[...] = jnp.concatenate(tails, 1)[0:FINAL]


def finish(packed, residual, tags, gate, weight, bias):
    return pl.pallas_call(
        finish_body,
        out_shape=(jax.ShapeDtypeStruct((TOK, WIDTH), BF),) * 4 + (jax.ShapeDtypeStruct((FINAL, WIDTH), F32),),
        in_specs=[WHOLE] * 6,
        out_specs=(WHOLE,) * 5,
        compiler_params=params(16),
        cost_estimate=cost(3),
        name="finish",
    )(packed, residual, tags, gate, weight, bias)


def sent(values, target):
    pairs = [(i, target(i)) for i in range(DEVICES)]
    return lax.ppermute(values, "dp", [(i, j) for i, j in pairs if 0 <= j < DEVICES])


def other_core(device):
    return device ^ 1


def cross(device):
    return device - PLANE + 1 if device % 2 == 0 else device + PLANE - 1


def planes_on(count):
    return lambda device: (device + count * PLANE) % DEVICES


def traded(values):
    groups = [[plane * PLANE + i for i in range(PLANE)] for plane in range(PLANES)]
    return lax.all_to_all(values, "dp", 0, 0, axis_index_groups=groups, tiled=True)


def some_blocks(values, start, rows, count):
    return lax.dynamic_slice(values, (start, rows, 0), (count, FULL, TOK))


def shards(query, key, value, residual, tags, gate, weight, bias, out_grad):
    me = lax.axis_index("dp")
    side = me % 2
    chunk, branch = pack(query, key, value, out_grad, gate, weight, tags)
    cores = [[plane * PLANE + 2 * chip + at for chip in range(HEADS)] for plane in range(PLANES) for at in range(2)]
    gathered = lax.all_gather(branch, "dp", axis=0, axis_index_groups=cores, tiled=False)
    own = traded(chunk)
    near = sent(some_blocks(own, (SIDE - EDGE) * (1 - side), 0, NEAR), other_core)
    asked = sent(some_blocks(own, SIDE * (1 - side), FULL, SIDE), other_core)
    far_other = sent(some_blocks(own, (PLANE - EDGE) * side, 0, EDGE), cross)
    far_own = sent(some_blocks(near, SIDE * side, 0, EDGE), cross)
    mixed, keep_asked, give_asked, keep, give, far = attend(own, near, asked, far_own, far_other)
    far = sent(far, cross)
    mixed_other = sent(mixed, other_core)
    got_asked = sent(give_asked, other_core)
    term, *terms = weight_term(mixed, mixed_other, gathered)
    terms = [sent(one, planes_on(away + 1)) for away, one in enumerate(terms)]
    far, _ = lax.optimization_barrier((far, term))
    keep, give = fold(keep, give, far)
    got = sent(give, other_core)
    packed = traded(join(keep_asked, got_asked, keep, got, term, *terms))
    block_out, dq, dk, dv, dw = finish(packed, residual, tags, gate, weight, bias)
    return block_out, dq, dk, dv, dw.T


def solution(mesh):
    rows = P("dp", None)
    in_specs = (rows, rows, rows, rows, P("dp"), P(), P(), P(), rows)
    out_specs = (rows,) * 4 + (P(None, "dp"),)
    return jax.shard_map(shards, mesh=mesh, in_specs=in_specs, out_specs=out_specs, check_vma=False)
```

```python
import math

import jax
import jax.numpy as jnp
from jax import lax
from jax.experimental import pallas as pl
from jax.experimental.pallas import tpu as pltpu
from jax.sharding import PartitionSpec as P

HEADS = 16
HEAD_DIM = 72
WIDTH = HEADS * HEAD_DIM
TOK = 128
DEVICES = 128
PLANES = 4
PLANE = 32
SIDE = 16
EDGE = 7
SPAN = SIDE + 2 * EDGE
NEAR = SIDE + EDGE
TILE = 256
TILES = SIDE * TOK // TILE
PART = TILE // TOK
STEP = 4
ROOM = SPAN + STEP - 1
CHUNKS = 4
HALF = 40
FULL = 2 * HALF
FINAL = WIDTH // DEVICES
CHIPS = 4
SHARE = WIDTH // PLANES
CLIPS = 32
SCALE = 1.0 / math.sqrt(HEAD_DIM)
SCALE2 = SCALE / math.log(2.0)
FAR = -1e30
BF = jnp.bfloat16
F32 = jnp.float32

WHOLE = pl.BlockSpec(memory_space=pltpu.VMEM)
FAR_AWAY = pl.BlockSpec(memory_space=pltpu.HBM)


def params(mebibytes):
    return pltpu.CompilerParams(vmem_limit_bytes=mebibytes * 1024 * 1024)


def cost(micros):
    return pl.CostEstimate(flops=int(micros * 4e8), bytes_accessed=int(micros * 2e6), transcendentals=0)


def mm(left, right):
    return jnp.dot(left, right, preferred_element_type=F32)


def clip_onehot(tags):
    ids = lax.broadcasted_iota(jnp.int32, (CLIPS, TOK), 0)
    return (ids == tags[...].reshape(1, TOK)).astype(F32)


def core():
    return lax.axis_index("dp") % 2


def pick(flag, first, second):
    return jnp.where(jnp.full(first.shape, flag, jnp.int32) == 0, first, second)


def pack_body(
    query, key, value, out_grad, gate, weight, tags, chunk_ref, branch_ref,
    query_here, key_here, value_here, out_grad_here, gate_here, weight_here, sems,
):
    loads = {}
    for at, (name, source, here) in enumerate((
        ("out_grad", out_grad, out_grad_here), ("gate", gate, gate_here), ("key", key, key_here),
        ("value", value, value_here), ("query", query, query_here), ("weight", weight, weight_here),
    )):
        loads[name] = pltpu.make_async_copy(source, here, sems.at[at])
        loads[name].start()
    tag_rows = jnp.broadcast_to(tags[...].reshape(1, TOK).astype(F32) + 1.0, (8, TOK))
    blank = jnp.zeros((8, TOK), F32)
    onehot = clip_onehot(tags)
    loads["out_grad"].wait()
    out_grad_t = out_grad_here[...].astype(F32).T
    loads["gate"].wait()
    gate_t = lax.dot_general(
        gate_here[...], onehot, (((0,), (0,)), ((), ())),
        precision=lax.Precision.HIGHEST, preferred_element_type=F32,
    )
    branch = (out_grad_t * gate_t).astype(BF)
    branch_ref[...] = branch
    loads["key"].wait()
    key_t = key_here[...].astype(F32).T
    loads["value"].wait()
    value_t = value_here[...].astype(F32).T
    loads["query"].wait()
    query_t = query_here[...].astype(F32).T
    loads["weight"].wait()
    grad_t = mm(weight_here[...], branch)
    for head in range(HEADS):
        start = head * HEAD_DIM
        low, high = slice(start, start + HALF), slice(start + HALF, start + HEAD_DIM)
        whole = [key_t[low], value_t[low], query_t[low], grad_t[low]]
        chunk_ref[2 * head] = jnp.concatenate(whole, 0).astype(BF)
        whole = [key_t[high], tag_rows, value_t[high], blank, query_t[high], blank, grad_t[high], blank]
        chunk_ref[2 * head + 1] = jnp.concatenate(whole, 0).astype(BF)


def pack(query, key, value, out_grad, gate, weight, tags):
    rows = pltpu.VMEM((TOK, WIDTH), BF)
    return pl.pallas_call(
        pack_body,
        out_shape=(
            jax.ShapeDtypeStruct((PLANE, 2 * FULL, TOK), BF),
            jax.ShapeDtypeStruct((WIDTH, TOK), BF),
        ),
        in_specs=[FAR_AWAY] * 6 + [WHOLE],
        out_specs=(WHOLE,) * 2,
        scratch_shapes=[
            rows, rows, rows, rows, pltpu.VMEM((CLIPS, WIDTH), F32), pltpu.VMEM((WIDTH, WIDTH), BF),
            pltpu.SemaphoreType.DMA((6,)),
        ],
        compiler_params=params(61),
        cost_estimate=cost(5),
        name="pack",
    )(query, key, value, out_grad, gate, weight, tags)


def filled(piece, extra):
    rows = [piece] + extra
    have = sum(part.shape[0] for part in rows)
    if have < TOK:
        rows.append(jnp.zeros((TOK - have, TOK), F32))
    return jnp.concatenate(rows, 0)


def natural(side, own, other):
    own, other = own.astype(F32), other.astype(F32)
    low, high = pick(side, own, other), pick(side, other, own)
    return [jnp.concatenate([low[rows], high[rows]], 0) for rows in (slice(0, HALF), slice(HALF, FULL))]


def halves(side, wholes):
    low = jnp.concatenate([whole[0:HALF] for whole in wholes], 0)
    high = jnp.concatenate([whole[HALF:] for whole in wholes], 0)
    return pick(side, low, high), pick(side, high, low)


def window(side, own, near, far_own, far_other):
    for block in range(NEAR):
        at = block + EDGE * (1 - side)
        yield (at,) + tuple(natural(side, own[block + (SIDE - EDGE) * side, 0:FULL], near[block]))
    for block in range(EDGE):
        yield (block + NEAR * side,) + tuple(natural(side, far_own[block], far_other[block]))


def token_rows(block):
    return pl.ds(pl.multiple_of(block * TOK, TOK), TOK)


def same_clip(clip, same, other):
    ids = lax.broadcasted_iota(jnp.int32, (CLIPS, TOK), 0).astype(F32) + 1.0
    return jnp.where(ids == clip, same, other)


def lay_out_keys(block, key, key_n, key_t, clips):
    clip = key[HEAD_DIM : HEAD_DIM + 1]
    clips[block] = key[HEAD_DIM:]
    held = filled(key[0:HEAD_DIM], [same_clip(clip, 0.0, FAR)])
    key_n[token_rows(block), :] = held.T.astype(BF)
    if key_t is not None:
        key_t[block] = jnp.concatenate([key[0:HEAD_DIM], jnp.zeros((8, TOK), F32)], 0).astype(BF)


def key_padding(key_n, key_t):
    rows = slice(SPAN * TOK, ROOM * TOK)
    lane = lax.broadcasted_iota(jnp.int32, ((ROOM - SPAN) * TOK, TOK), 1)
    key_n[rows, :] = jnp.where((lane >= HEAD_DIM) & (lane < HEAD_DIM + CLIPS), FAR, 0.0).astype(BF)
    if key_t is not None:
        for block in range(SPAN, ROOM):
            key_t[block] = jnp.zeros((80, TOK), BF)


def key_ranges(clips, first_ref, count_ref):
    rows = [clips[block][0:1] for block in range(SPAN)]
    rows = [jnp.where(row == 0.0, 100.0, row) if at >= NEAR else row for at, row in enumerate(rows)]
    rows = jnp.concatenate(rows + [jnp.full((32 - SPAN, TOK), 100.0, F32)], 0)
    least = jnp.min(rows, axis=1, keepdims=True)
    most = jnp.max(rows, axis=1, keepdims=True)
    for tile in range(TILES):
        start = EDGE + tile * PART
        low, high = least[start : start + 1], most[start + PART - 1 : start + PART]
        first = jnp.sum(jnp.where(most < low, 1.0, 0.0)).astype(jnp.int32)
        end = jnp.sum(jnp.where(least <= high, 1.0, 0.0)).astype(jnp.int32)
        first_ref[tile] = first
        count_ref[tile] = (end - first + STEP - 1) // STEP


def side_by_side(ref, start):
    return jnp.concatenate([ref[start + at] for at in range(STEP)], 1)


def blocks(first, step):
    start = first + step * STEP
    return start, pl.ds(pl.multiple_of(start * TOK, TOK), STEP * TOK)


def attend_body(
    own, near, asked, far_own, far_other,
    mixed_ref, keep_asked_ref, give_asked_ref, keep_ref, give_ref, far_ref,
    key_n, key_t, value_n, value_t, query_t, query_n, grad_t, grad_n, held, pulls, mixed_t, dq, dk, dv,
    clips, first_ref, count_ref,
):
    side = core()
    for at, key, value in window(side, own, near, far_own, far_other):
        lay_out_keys(at, key, key_n, key_t, clips)
        value = filled(value[0:HEAD_DIM], [jnp.ones((8, TOK), F32)])
        value_n[token_rows(at), :] = value.T.astype(BF)
        value_t[at] = value[0:80].astype(BF)
    value_n[SPAN * TOK :, :] = jnp.zeros(((ROOM - SPAN) * TOK, TOK), BF)
    for block in range(SPAN, ROOM):
        value_t[block] = jnp.zeros((80, TOK), BF)
    key_padding(key_n, key_t)
    for block in range(SIDE):
        tile, cols = block // PART, slice((block % PART) * TOK, (block % PART + 1) * TOK)
        query, grad = natural(side, own[SIDE * side + block, FULL:], asked[block])
        query = filled(query[0:HEAD_DIM], [same_clip(clips[EDGE + block][0:1], 1.0, 0.0)])
        query_t[tile, :, cols] = query.astype(BF)
        query_n[tile, cols, :] = query.T.astype(BF)
        grad = filled(grad, [])
        grad_t[tile, :, cols] = grad.astype(BF)
        grad_n[tile, cols, :] = grad.T.astype(BF)
    key_ranges(clips, first_ref, count_ref)
    dk[...] = jnp.zeros_like(dk)
    dv[...] = jnp.zeros_like(dv)

    def whole_tile(tile, first, count):
        tops = []
        grad = grad_t[tile]
        for step in range(count):
            scores = mm(key_n[blocks(first, step)[1], :], query_t[tile])
            held[step] = scores
            tops.append(jnp.max(scores, axis=0, keepdims=True))
            pulls[step] = mm(value_n[blocks(first, step)[1], :], grad)
        top = tops[0]
        for other in tops[1:]:
            top = jnp.maximum(top, other)
        total = None
        for step in range(count):
            weights = jnp.exp2((held[step] - top) * SCALE2)
            held[step] = weights
            term = mm(side_by_side(value_t, blocks(first, step)[0]), weights.astype(BF))
            total = term if total is None else total + term
        inverse = 1.0 / total[HEAD_DIM : HEAD_DIM + 1]
        mixed = jnp.concatenate([total[0:HEAD_DIM] * inverse, jnp.zeros((8, TILE), F32)], 0).astype(BF)
        delta = jnp.sum(mixed.astype(F32) * grad[0:FULL].astype(F32), axis=0, keepdims=True)
        mixed_t[tile] = mixed
        total = None
        for step in range(count):
            start, rows = blocks(first, step)
            prob = held[step] * inverse
            pull = pulls[step]
            dv[rows, :] += mm(prob.astype(BF), grad_n[tile])
            score_grad = (prob * (pull - delta)).astype(BF)
            dk[rows, :] += mm(score_grad, query_n[tile])
            term = mm(side_by_side(key_t, start), score_grad)
            total = term if total is None else total + term
        dq[tile] = total * SCALE

    def query_step(tile, carry):
        first, count = first_ref[tile], count_ref[tile]
        for steps in range(1, CHUNKS + 1):
            pl.when(count == steps)(lambda steps=steps: whole_tile(tile, first, steps))
        return carry

    lax.fori_loop(0, TILES, query_step, 0)

    def key_grads(at):
        rows = token_rows(at)
        return [dk[rows, :].T[0:FULL] * SCALE, dv[rows, :].T[0:FULL]]

    def hand_out(keep, give, block, wholes):
        first, second = halves(side, wholes)
        keep[block], give[block] = first.astype(BF), second.astype(BF)

    for block in range(SIDE):
        tile, cols = block // PART, slice((block % PART) * TOK, (block % PART + 1) * TOK)
        mixed = mixed_t[tile, :, cols]
        mixed_ref[block] = mixed
        hand_out(keep_asked_ref, give_asked_ref, block, [mixed.astype(F32), dq[tile, :, cols]])
        hand_out(keep_ref, give_ref, block, key_grads(EDGE + block))
    for block in range(EDGE):
        hand_out(keep_ref, give_ref, SIDE + block, key_grads(block + NEAR * (1 - side)))
        far_ref[block] = jnp.concatenate(key_grads(block + NEAR * side), 0).astype(BF)


def attend(own, near, asked, far_own, far_other):
    whole = jax.ShapeDtypeStruct((SIDE, FULL, TOK), BF)
    keys = jax.ShapeDtypeStruct((NEAR, FULL, TOK), BF)
    edge = jax.ShapeDtypeStruct((EDGE, 2 * FULL, TOK), BF)
    row_form = pltpu.VMEM((ROOM * TOK, TOK), BF)
    column_form = pltpu.VMEM((ROOM, 80, TOK), BF)
    return pl.pallas_call(
        attend_body,
        out_shape=(whole, whole, whole, keys, keys, edge),
        in_specs=[WHOLE] * 5,
        out_specs=(WHOLE,) * 6,
        cost_estimate=cost(20),
        scratch_shapes=[
            row_form, column_form, row_form, column_form,
            pltpu.VMEM((TILES, TOK, TILE), BF), pltpu.VMEM((TILES, TILE, TOK), BF),
            pltpu.VMEM((TILES, TOK, TILE), BF), pltpu.VMEM((TILES, TILE, TOK), BF),
            pltpu.VMEM((CHUNKS, STEP * TOK, TILE), F32),
            pltpu.VMEM((CHUNKS, STEP * TOK, TILE), F32),
            pltpu.VMEM((TILES, FULL, TILE), BF),
            pltpu.VMEM((TILES, FULL, TILE), F32),
            pltpu.VMEM((ROOM * TOK, TOK), F32),
            pltpu.VMEM((ROOM * TOK, TOK), F32),
            pltpu.VMEM((SPAN, 8, TOK), F32),
            pltpu.SMEM((TILES,), jnp.int32),
            pltpu.SMEM((TILES,), jnp.int32),
        ],
        compiler_params=params(24),
        name="attend",
    )(own, near, asked, far_own, far_other)


def weight_term_body(mixed, other, branch, *refs):
    out_refs, total = refs[:PLANES], refs[PLANES]
    step = pl.program_id(0)
    side = core()
    left, right = [], []
    for at in range(CHIPS):
        chip = CHIPS * step + at
        place = 2 * lax.rem(chip, HEADS // 2) + side
        foreign = jnp.where(chip // (HEADS // 2) == side, 0, 1)
        right.append(pick(foreign, mixed[place].astype(F32), other[place].astype(F32)))
        left.append(branch[at])
    term = lax.dot_general(
        jnp.concatenate(left, 1), jnp.concatenate(right, 1).astype(BF), (((1,), (1,)), ((), ())),
        preferred_element_type=F32,
    )

    @pl.when(step == 0)
    def _():
        total[:, 0:FULL] = term
        total[:, FULL:] = jnp.zeros((WIDTH, TOK - FULL), F32)

    @pl.when(step > 0)
    def _():
        total[:, 0:FULL] += term

    @pl.when(step == HEADS // CHIPS - 1)
    def _():
        plane = lax.axis_index("dp") // PLANE
        for away in range(PLANES):
            start = pl.multiple_of((plane ^ away) * SHARE, 8)
            out_refs[away][...] = total[pl.ds(start, SHARE), :].astype(BF)


def weight_term(mixed, other, branch):
    share = pl.BlockSpec((SHARE, TOK), lambda i: (0, 0))
    held = pl.BlockSpec((SIDE, FULL, TOK), lambda i: (0, 0, 0))
    return pl.pallas_call(
        weight_term_body,
        grid=(HEADS // CHIPS,),
        out_shape=(jax.ShapeDtypeStruct((SHARE, TOK), BF),) * PLANES,
        in_specs=[held, held, pl.BlockSpec((CHIPS, WIDTH, TOK), lambda i: (i, 0, 0))],
        out_specs=(share,) * PLANES,
        scratch_shapes=[pltpu.VMEM((WIDTH, TOK), F32)],
        compiler_params=params(16),
        cost_estimate=cost(4),
        name="weight_term",
    )(mixed, other, branch)


def fold_body(keep, give, far, keep_ref, give_ref):
    side = core()
    keep_ref[...] = keep[...]
    give_ref[...] = give[...]
    for block in range(EDGE):
        place = block + (SIDE - EDGE) * side
        whole = far[block].astype(F32)
        first, second = halves(side, [whole[0:FULL], whole[FULL:]])
        keep_ref[place] = (keep[place].astype(F32) + first).astype(BF)
        give_ref[place] = (give[place].astype(F32) + second).astype(BF)


def fold(keep, give, far):
    keys = jax.ShapeDtypeStruct((NEAR, FULL, TOK), BF)
    return pl.pallas_call(
        fold_body,
        out_shape=(keys, keys),
        in_specs=[WHOLE] * 3,
        out_specs=(WHOLE,) * 2,
        compiler_params=params(8),
        cost_estimate=cost(1),
        name="fold",
    )(keep, give, far)


def join_body(keep_asked, got_asked, keep, got, term, term1, term2, term3, out_ref, total, pairs):
    side = core()
    total[0:SHARE] = sum(one[...].astype(F32) for one in (term, term1, term2, term3))
    total[SHARE:] = jnp.zeros((8, TOK), F32)
    mine, others = SIDE * side, SIDE * (1 - side)
    for block in range(SIDE):
        pairs[mine + block] = keep[block].astype(F32)
        pairs[others + block] = got[block].astype(F32)
    for block in range(EDGE):
        pairs[others + (SIDE - EDGE) * side + block] += keep[SIDE + block].astype(F32)
        pairs[mine + (SIDE - EDGE) * (1 - side) + block] += got[SIDE + block].astype(F32)
    for block in range(SIDE):
        for start, asked in ((mine, keep_asked), (others, got_asked)):
            at = start + block
            whole = [asked[block].astype(F32), pairs[at], total[pl.ds(at * FINAL, 16), :]]
            out_ref[at] = jnp.concatenate(whole, 0).astype(BF)


def join(*values):
    return pl.pallas_call(
        join_body,
        out_shape=jax.ShapeDtypeStruct((PLANE, 2 * FULL + 16, TOK), BF),
        in_specs=[WHOLE] * 8,
        out_specs=WHOLE,
        scratch_shapes=[pltpu.VMEM((SHARE + 8, TOK), F32), pltpu.VMEM((PLANE, FULL, TOK), F32)],
        compiler_params=params(12),
        cost_estimate=cost(1),
        name="join",
    )(*values)


def finish_body(packed, residual, tags, gate, weight, bias, out_ref, dq_ref, dk_ref, dv_ref, dw_ref):
    def rows(at):
        low = slice(at * HALF, (at + 1) * HALF)
        high = slice(at * HALF, at * HALF + HEAD_DIM - HALF)
        parts = []
        for head in range(HEADS):
            parts += [packed[2 * head].astype(F32)[low], packed[2 * head + 1].astype(F32)[high]]
        return jnp.concatenate(parts, 0).T.astype(BF)

    gate_rows = lax.dot_general(
        clip_onehot(tags), gate[...], (((0,), (0,)), ((), ())),
        precision=lax.Precision.HIGHEST, preferred_element_type=F32,
    )
    projected = mm(rows(0), weight[...]) + bias[...].reshape(1, WIDTH)
    out_ref[...] = (residual[...].astype(F32) + gate_rows * projected).astype(BF)
    dq_ref[...] = rows(1)
    dk_ref[...] = rows(2)
    dv_ref[...] = rows(3)
    tails = []
    for head in range(HEADS):
        first, second = [packed[2 * head + at, 2 * FULL :].astype(F32) for at in range(2)]
        tails.append((first + second)[:, 0:HEAD_DIM])
    dw_ref[...] = jnp.concatenate(tails, 1)[0:FINAL]


def finish(packed, residual, tags, gate, weight, bias):
    return pl.pallas_call(
        finish_body,
        out_shape=(jax.ShapeDtypeStruct((TOK, WIDTH), BF),) * 4 + (jax.ShapeDtypeStruct((FINAL, WIDTH), F32),),
        in_specs=[WHOLE] * 6,
        out_specs=(WHOLE,) * 5,
        compiler_params=params(16),
        cost_estimate=cost(3),
        name="finish",
    )(packed, residual, tags, gate, weight, bias)


def sent(values, target):
    pairs = [(i, target(i)) for i in range(DEVICES)]
    return lax.ppermute(values, "dp", [(i, j) for i, j in pairs if 0 <= j < DEVICES])


def other_core(device):
    return device ^ 1


def cross(device):
    return device - PLANE + 1 if device % 2 == 0 else device + PLANE - 1


def plane_pair(bits):
    return lambda device: device ^ (bits * PLANE)


def traded(values):
    groups = [[plane * PLANE + i for i in range(PLANE)] for plane in range(PLANES)]
    return lax.all_to_all(values, "dp", 0, 0, axis_index_groups=groups, tiled=True)


def some_blocks(values, start, rows, count):
    return lax.dynamic_slice(values, (start, rows, 0), (count, FULL, TOK))


def shards(query, key, value, residual, tags, gate, weight, bias, out_grad):
    me = lax.axis_index("dp")
    side = me % 2
    chunk, branch = pack(query, key, value, out_grad, gate, weight, tags)
    cores = [[plane * PLANE + 2 * chip + at for chip in range(HEADS)] for plane in range(PLANES) for at in range(2)]
    gathered = lax.all_gather(branch, "dp", axis=0, axis_index_groups=cores, tiled=False)
    own = traded(chunk)
    near = sent(some_blocks(own, (SIDE - EDGE) * (1 - side), 0, NEAR), other_core)
    asked = sent(some_blocks(own, SIDE * (1 - side), FULL, SIDE), other_core)
    far_other = sent(some_blocks(own, (PLANE - EDGE) * side, 0, EDGE), cross)
    far_own = sent(some_blocks(near, SIDE * side, 0, EDGE), cross)
    mixed, keep_asked, give_asked, keep, give, far = attend(own, near, asked, far_own, far_other)
    far = sent(far, cross)
    mixed_other = sent(mixed, other_core)
    got_asked = sent(give_asked, other_core)
    term, *terms = weight_term(mixed, mixed_other, gathered)
    terms = [sent(one, plane_pair(away + 1)) for away, one in enumerate(terms)]
    far, _ = lax.optimization_barrier((far, term))
    keep, give = fold(keep, give, far)
    got = sent(give, other_core)
    packed = traded(join(keep_asked, got_asked, keep, got, term, *terms))
    block_out, dq, dk, dv, dw = finish(packed, residual, tags, gate, weight, bias)
    return block_out, dq, dk, dv, dw.T


def solution(mesh):
    rows = P("dp", None)
    in_specs = (rows, rows, rows, rows, P("dp"), P(), P(), P(), rows)
    out_specs = (rows,) * 4 + (P(None, "dp"),)
    return jax.shard_map(shards, mesh=mesh, in_specs=in_specs, out_specs=out_specs, check_vma=False)
```

```python
import math

import jax
import jax.numpy as jnp
from jax import lax
from jax.experimental import pallas as pl
from jax.experimental.pallas import tpu as pltpu
from jax.sharding import PartitionSpec as P

HEADS = 16
HEAD_DIM = 72
WIDTH = HEADS * HEAD_DIM
TOK = 128
DEVICES = 128
PLANES = 4
PLANE = 32
SIDE = 16
EDGE = 7
SPAN = SIDE + 2 * EDGE
NEAR = SIDE + EDGE
TILE = 256
TILES = SIDE * TOK // TILE
PART = TILE // TOK
STEP = 4
ROOM = SPAN + STEP - 1
CHUNKS = 4
HALF = 40
FULL = 2 * HALF
FINAL = WIDTH // DEVICES
CHIPS = 4
SHARE = WIDTH // PLANES
CLIPS = 32
SCALE = 1.0 / math.sqrt(HEAD_DIM)
SCALE2 = SCALE / math.log(2.0)
FAR = -1e30
BF = jnp.bfloat16
F32 = jnp.float32

WHOLE = pl.BlockSpec(memory_space=pltpu.VMEM)
FAR_AWAY = pl.BlockSpec(memory_space=pltpu.HBM)


def params(mebibytes):
    return pltpu.CompilerParams(vmem_limit_bytes=mebibytes * 1024 * 1024)


def cost(micros):
    return pl.CostEstimate(flops=int(micros * 4e8), bytes_accessed=int(micros * 2e6), transcendentals=0)


def mm(left, right):
    return jnp.dot(left, right, preferred_element_type=F32)


def clip_onehot(tags):
    ids = lax.broadcasted_iota(jnp.int32, (CLIPS, TOK), 0)
    return (ids == tags[...].reshape(1, TOK)).astype(F32)


def core():
    return lax.axis_index("dp") % 2


def pick(flag, first, second):
    return jnp.where(jnp.full(first.shape, flag, jnp.int32) == 0, first, second)


def pack_body(
    query, key, value, out_grad, gate, weight, tags, chunk_ref, branch_ref,
    query_here, key_here, value_here, out_grad_here, gate_here, weight_here, sems,
):
    loads = {}
    for at, (name, source, here) in enumerate((
        ("out_grad", out_grad, out_grad_here), ("gate", gate, gate_here), ("key", key, key_here),
        ("value", value, value_here), ("query", query, query_here), ("weight", weight, weight_here),
    )):
        loads[name] = pltpu.make_async_copy(source, here, sems.at[at])
        loads[name].start()
    tag_rows = jnp.broadcast_to(tags[...].reshape(1, TOK).astype(F32) + 1.0, (8, TOK))
    blank = jnp.zeros((8, TOK), F32)
    onehot = clip_onehot(tags)
    loads["out_grad"].wait()
    out_grad_t = out_grad_here[...].astype(F32).T
    loads["gate"].wait()
    gate_t = lax.dot_general(
        gate_here[...], onehot, (((0,), (0,)), ((), ())),
        precision=lax.Precision.HIGHEST, preferred_element_type=F32,
    )
    branch = (out_grad_t * gate_t).astype(BF)
    branch_ref[...] = branch
    loads["key"].wait()
    key_t = key_here[...].astype(F32).T
    loads["value"].wait()
    value_t = value_here[...].astype(F32).T
    halves_of = [
        (slice(head * HEAD_DIM, head * HEAD_DIM + HALF), slice(head * HEAD_DIM + HALF, (head + 1) * HEAD_DIM))
        for head in range(HEADS)
    ]
    for head, (low, high) in enumerate(halves_of):
        chunk_ref[2 * head, 0:FULL] = jnp.concatenate([key_t[low], value_t[low]], 0).astype(BF)
        whole = [key_t[high], tag_rows, value_t[high], blank]
        chunk_ref[2 * head + 1, 0:FULL] = jnp.concatenate(whole, 0).astype(BF)
    loads["query"].wait()
    query_t = query_here[...].astype(F32).T
    loads["weight"].wait()
    grad_t = mm(weight_here[...], branch)
    for head, (low, high) in enumerate(halves_of):
        chunk_ref[2 * head, FULL:] = jnp.concatenate([query_t[low], grad_t[low]], 0).astype(BF)
        whole = [query_t[high], blank, grad_t[high], blank]
        chunk_ref[2 * head + 1, FULL:] = jnp.concatenate(whole, 0).astype(BF)


def pack(query, key, value, out_grad, gate, weight, tags):
    rows = pltpu.VMEM((TOK, WIDTH), BF)
    return pl.pallas_call(
        pack_body,
        out_shape=(
            jax.ShapeDtypeStruct((PLANE, 2 * FULL, TOK), BF),
            jax.ShapeDtypeStruct((WIDTH, TOK), BF),
        ),
        in_specs=[FAR_AWAY] * 6 + [WHOLE],
        out_specs=(WHOLE,) * 2,
        scratch_shapes=[
            rows, rows, rows, rows, pltpu.VMEM((CLIPS, WIDTH), F32), pltpu.VMEM((WIDTH, WIDTH), BF),
            pltpu.SemaphoreType.DMA((6,)),
        ],
        compiler_params=params(61),
        cost_estimate=cost(5),
        name="pack",
    )(query, key, value, out_grad, gate, weight, tags)


def filled(piece, extra):
    rows = [piece] + extra
    have = sum(part.shape[0] for part in rows)
    if have < TOK:
        rows.append(jnp.zeros((TOK - have, TOK), F32))
    return jnp.concatenate(rows, 0)


def natural(side, own, other):
    own, other = own.astype(F32), other.astype(F32)
    low, high = pick(side, own, other), pick(side, other, own)
    return [jnp.concatenate([low[rows], high[rows]], 0) for rows in (slice(0, HALF), slice(HALF, FULL))]


def halves(side, wholes):
    low = jnp.concatenate([whole[0:HALF] for whole in wholes], 0)
    high = jnp.concatenate([whole[HALF:] for whole in wholes], 0)
    return pick(side, low, high), pick(side, high, low)


def window(side, own, near, far_own, far_other):
    for block in range(NEAR):
        at = block + EDGE * (1 - side)
        yield (at,) + tuple(natural(side, own[block + (SIDE - EDGE) * side, 0:FULL], near[block]))
    for block in range(EDGE):
        yield (block + NEAR * side,) + tuple(natural(side, far_own[block], far_other[block]))


def token_rows(block):
    return pl.ds(pl.multiple_of(block * TOK, TOK), TOK)


def same_clip(clip, same, other):
    ids = lax.broadcasted_iota(jnp.int32, (CLIPS, TOK), 0).astype(F32) + 1.0
    return jnp.where(ids == clip, same, other)


def lay_out_keys(block, key, key_n, key_t, clips):
    clip = key[HEAD_DIM : HEAD_DIM + 1]
    clips[block] = key[HEAD_DIM:]
    held = filled(key[0:HEAD_DIM], [same_clip(clip, 0.0, FAR)])
    key_n[token_rows(block), :] = held.T.astype(BF)
    if key_t is not None:
        key_t[block] = jnp.concatenate([key[0:HEAD_DIM], jnp.zeros((8, TOK), F32)], 0).astype(BF)


def key_padding(key_n, key_t):
    rows = slice(SPAN * TOK, ROOM * TOK)
    lane = lax.broadcasted_iota(jnp.int32, ((ROOM - SPAN) * TOK, TOK), 1)
    key_n[rows, :] = jnp.where((lane >= HEAD_DIM) & (lane < HEAD_DIM + CLIPS), FAR, 0.0).astype(BF)
    if key_t is not None:
        for block in range(SPAN, ROOM):
            key_t[block] = jnp.zeros((80, TOK), BF)


def key_ranges(clips, first_ref, count_ref):
    rows = [clips[block][0:1] for block in range(SPAN)]
    rows = [jnp.where(row == 0.0, 100.0, row) if at >= NEAR else row for at, row in enumerate(rows)]
    rows = jnp.concatenate(rows + [jnp.full((32 - SPAN, TOK), 100.0, F32)], 0)
    least = jnp.min(rows, axis=1, keepdims=True)
    most = jnp.max(rows, axis=1, keepdims=True)
    for tile in range(TILES):
        start = EDGE + tile * PART
        low, high = least[start : start + 1], most[start + PART - 1 : start + PART]
        first = jnp.sum(jnp.where(most < low, 1.0, 0.0)).astype(jnp.int32)
        end = jnp.sum(jnp.where(least <= high, 1.0, 0.0)).astype(jnp.int32)
        first_ref[tile] = first
        count_ref[tile] = (end - first + STEP - 1) // STEP


def side_by_side(ref, start):
    return jnp.concatenate([ref[start + at] for at in range(STEP)], 1)


def blocks(first, step):
    start = first + step * STEP
    return start, pl.ds(pl.multiple_of(start * TOK, TOK), STEP * TOK)


def attend_body(
    own, near, asked, far_own, far_other,
    mixed_ref, keep_asked_ref, give_asked_ref, keep_ref, give_ref, far_ref,
    key_n, key_t, value_n, value_t, query_t, query_n, grad_t, grad_n, held, pulls, mixed_t, dq, dk, dv,
    clips, first_ref, count_ref,
):
    side = core()
    for at, key, value in window(side, own, near, far_own, far_other):
        lay_out_keys(at, key, key_n, key_t, clips)
        value = filled(value[0:HEAD_DIM], [jnp.ones((8, TOK), F32)])
        value_n[token_rows(at), :] = value.T.astype(BF)
        value_t[at] = value[0:80].astype(BF)
    value_n[SPAN * TOK :, :] = jnp.zeros(((ROOM - SPAN) * TOK, TOK), BF)
    for block in range(SPAN, ROOM):
        value_t[block] = jnp.zeros((80, TOK), BF)
    key_padding(key_n, key_t)
    for block in range(SIDE):
        tile, cols = block // PART, slice((block % PART) * TOK, (block % PART + 1) * TOK)
        query, grad = natural(side, own[SIDE * side + block, FULL:], asked[block])
        query = filled(query[0:HEAD_DIM], [same_clip(clips[EDGE + block][0:1], 1.0, 0.0)])
        query_t[tile, :, cols] = query.astype(BF)
        query_n[tile, cols, :] = query.T.astype(BF)
        grad = filled(grad, [])
        grad_t[tile, :, cols] = grad.astype(BF)
        grad_n[tile, cols, :] = grad.T.astype(BF)
    key_ranges(clips, first_ref, count_ref)
    dk[...] = jnp.zeros_like(dk)
    dv[...] = jnp.zeros_like(dv)

    def whole_tile(tile, first, count):
        tops = []
        grad = grad_t[tile]
        for step in range(count):
            scores = mm(key_n[blocks(first, step)[1], :], query_t[tile])
            held[step] = scores
            tops.append(jnp.max(scores, axis=0, keepdims=True))
            pulls[step] = mm(value_n[blocks(first, step)[1], :], grad)
        top = tops[0]
        for other in tops[1:]:
            top = jnp.maximum(top, other)
        total = None
        for step in range(count):
            weights = jnp.exp2((held[step] - top) * SCALE2)
            held[step] = weights
            term = mm(side_by_side(value_t, blocks(first, step)[0]), weights.astype(BF))
            total = term if total is None else total + term
        inverse = 1.0 / total[HEAD_DIM : HEAD_DIM + 1]
        mixed = jnp.concatenate([total[0:HEAD_DIM] * inverse, jnp.zeros((8, TILE), F32)], 0).astype(BF)
        delta = jnp.sum(mixed.astype(F32) * grad[0:FULL].astype(F32), axis=0, keepdims=True)
        mixed_t[tile] = mixed
        total = None
        for step in range(count):
            start, rows = blocks(first, step)
            prob = held[step] * inverse
            pull = pulls[step]
            dv[rows, :] += mm(prob.astype(BF), grad_n[tile])
            score_grad = (prob * (pull - delta)).astype(BF)
            dk[rows, :] += mm(score_grad, query_n[tile])
            term = mm(side_by_side(key_t, start), score_grad)
            total = term if total is None else total + term
        dq[tile] = total * SCALE

    def query_step(tile, carry):
        first, count = first_ref[tile], count_ref[tile]
        for steps in range(1, CHUNKS + 1):
            pl.when(count == steps)(lambda steps=steps: whole_tile(tile, first, steps))
        return carry

    lax.fori_loop(0, TILES, query_step, 0)

    def key_grads(at):
        rows = token_rows(at)
        return [dk[rows, :].T[0:FULL] * SCALE, dv[rows, :].T[0:FULL]]

    def hand_out(keep, give, block, wholes):
        first, second = halves(side, wholes)
        keep[block], give[block] = first.astype(BF), second.astype(BF)

    for block in range(SIDE):
        tile, cols = block // PART, slice((block % PART) * TOK, (block % PART + 1) * TOK)
        mixed = mixed_t[tile, :, cols]
        mixed_ref[block] = mixed
        hand_out(keep_asked_ref, give_asked_ref, block, [mixed.astype(F32), dq[tile, :, cols]])
        hand_out(keep_ref, give_ref, block, key_grads(EDGE + block))
    for block in range(EDGE):
        hand_out(keep_ref, give_ref, SIDE + block, key_grads(block + NEAR * (1 - side)))
        far_ref[block] = jnp.concatenate(key_grads(block + NEAR * side), 0).astype(BF)


def attend(own, near, asked, far_own, far_other):
    whole = jax.ShapeDtypeStruct((SIDE, FULL, TOK), BF)
    keys = jax.ShapeDtypeStruct((NEAR, FULL, TOK), BF)
    edge = jax.ShapeDtypeStruct((EDGE, 2 * FULL, TOK), BF)
    row_form = pltpu.VMEM((ROOM * TOK, TOK), BF)
    column_form = pltpu.VMEM((ROOM, 80, TOK), BF)
    return pl.pallas_call(
        attend_body,
        out_shape=(whole, whole, whole, keys, keys, edge),
        in_specs=[WHOLE] * 5,
        out_specs=(WHOLE,) * 6,
        cost_estimate=cost(20),
        scratch_shapes=[
            row_form, column_form, row_form, column_form,
            pltpu.VMEM((TILES, TOK, TILE), BF), pltpu.VMEM((TILES, TILE, TOK), BF),
            pltpu.VMEM((TILES, TOK, TILE), BF), pltpu.VMEM((TILES, TILE, TOK), BF),
            pltpu.VMEM((CHUNKS, STEP * TOK, TILE), F32),
            pltpu.VMEM((CHUNKS, STEP * TOK, TILE), F32),
            pltpu.VMEM((TILES, FULL, TILE), BF),
            pltpu.VMEM((TILES, FULL, TILE), F32),
            pltpu.VMEM((ROOM * TOK, TOK), F32),
            pltpu.VMEM((ROOM * TOK, TOK), F32),
            pltpu.VMEM((SPAN, 8, TOK), F32),
            pltpu.SMEM((TILES,), jnp.int32),
            pltpu.SMEM((TILES,), jnp.int32),
        ],
        compiler_params=params(24),
        name="attend",
    )(own, near, asked, far_own, far_other)


def weight_term_body(mixed, other, branch, *refs):
    out_refs, total = refs[:PLANES], refs[PLANES]
    step = pl.program_id(0)
    side = core()
    left, right = [], []
    for at in range(CHIPS):
        chip = CHIPS * step + at
        place = 2 * lax.rem(chip, HEADS // 2) + side
        foreign = jnp.where(chip // (HEADS // 2) == side, 0, 1)
        right.append(pick(foreign, mixed[place].astype(F32), other[place].astype(F32)))
        left.append(branch[at])
    term = lax.dot_general(
        jnp.concatenate(left, 1), jnp.concatenate(right, 1).astype(BF), (((1,), (1,)), ((), ())),
        preferred_element_type=F32,
    )

    @pl.when(step == 0)
    def _():
        total[:, 0:FULL] = term
        total[:, FULL:] = jnp.zeros((WIDTH, TOK - FULL), F32)

    @pl.when(step > 0)
    def _():
        total[:, 0:FULL] += term

    @pl.when(step == HEADS // CHIPS - 1)
    def _():
        plane = lax.axis_index("dp") // PLANE
        for away in range(PLANES):
            start = pl.multiple_of(lax.rem(plane + away, PLANES) * SHARE, 8)
            out_refs[away][...] = total[pl.ds(start, SHARE), :].astype(BF)


def weight_term(mixed, other, branch):
    share = pl.BlockSpec((SHARE, TOK), lambda i: (0, 0))
    held = pl.BlockSpec((SIDE, FULL, TOK), lambda i: (0, 0, 0))
    return pl.pallas_call(
        weight_term_body,
        grid=(HEADS // CHIPS,),
        out_shape=(jax.ShapeDtypeStruct((SHARE, TOK), BF),) * PLANES,
        in_specs=[held, held, pl.BlockSpec((CHIPS, WIDTH, TOK), lambda i: (i, 0, 0))],
        out_specs=(share,) * PLANES,
        scratch_shapes=[pltpu.VMEM((WIDTH, TOK), F32)],
        compiler_params=params(16),
        cost_estimate=cost(4),
        name="weight_term",
    )(mixed, other, branch)


def fold_body(keep, give, far, keep_ref, give_ref):
    side = core()
    keep_ref[...] = keep[...]
    give_ref[...] = give[...]
    for block in range(EDGE):
        place = block + (SIDE - EDGE) * side
        whole = far[block].astype(F32)
        first, second = halves(side, [whole[0:FULL], whole[FULL:]])
        keep_ref[place] = (keep[place].astype(F32) + first).astype(BF)
        give_ref[place] = (give[place].astype(F32) + second).astype(BF)


def fold(keep, give, far):
    keys = jax.ShapeDtypeStruct((NEAR, FULL, TOK), BF)
    return pl.pallas_call(
        fold_body,
        out_shape=(keys, keys),
        in_specs=[WHOLE] * 3,
        out_specs=(WHOLE,) * 2,
        compiler_params=params(8),
        cost_estimate=cost(1),
        name="fold",
    )(keep, give, far)


def join_body(keep_asked, got_asked, keep, got, term, term1, term2, term3, out_ref, total, pairs):
    side = core()
    total[0:SHARE] = sum(one[...].astype(F32) for one in (term, term1, term2, term3))
    total[SHARE:] = jnp.zeros((8, TOK), F32)
    mine, others = SIDE * side, SIDE * (1 - side)
    for block in range(SIDE):
        pairs[mine + block] = keep[block].astype(F32)
        pairs[others + block] = got[block].astype(F32)
    for block in range(EDGE):
        pairs[others + (SIDE - EDGE) * side + block] += keep[SIDE + block].astype(F32)
        pairs[mine + (SIDE - EDGE) * (1 - side) + block] += got[SIDE + block].astype(F32)
    for block in range(SIDE):
        for start, asked in ((mine, keep_asked), (others, got_asked)):
            at = start + block
            whole = [asked[block].astype(F32), pairs[at], total[pl.ds(at * FINAL, 16), :]]
            out_ref[at] = jnp.concatenate(whole, 0).astype(BF)


def join(*values):
    return pl.pallas_call(
        join_body,
        out_shape=jax.ShapeDtypeStruct((PLANE, 2 * FULL + 16, TOK), BF),
        in_specs=[WHOLE] * 8,
        out_specs=WHOLE,
        scratch_shapes=[pltpu.VMEM((SHARE + 8, TOK), F32), pltpu.VMEM((PLANE, FULL, TOK), F32)],
        compiler_params=params(12),
        cost_estimate=cost(1),
        name="join",
    )(*values)


def finish_body(packed, residual, tags, gate, weight, bias, out_ref, dq_ref, dk_ref, dv_ref, dw_ref):
    def rows(at):
        low = slice(at * HALF, (at + 1) * HALF)
        high = slice(at * HALF, at * HALF + HEAD_DIM - HALF)
        parts = []
        for head in range(HEADS):
            parts += [packed[2 * head].astype(F32)[low], packed[2 * head + 1].astype(F32)[high]]
        return jnp.concatenate(parts, 0).T.astype(BF)

    gate_rows = lax.dot_general(
        clip_onehot(tags), gate[...], (((0,), (0,)), ((), ())),
        precision=lax.Precision.HIGHEST, preferred_element_type=F32,
    )
    projected = mm(rows(0), weight[...]) + bias[...].reshape(1, WIDTH)
    out_ref[...] = (residual[...].astype(F32) + gate_rows * projected).astype(BF)
    dq_ref[...] = rows(1)
    dk_ref[...] = rows(2)
    dv_ref[...] = rows(3)
    tails = []
    for head in range(HEADS):
        first, second = [packed[2 * head + at, 2 * FULL :].astype(F32) for at in range(2)]
        tails.append((first + second)[:, 0:HEAD_DIM])
    dw_ref[...] = jnp.concatenate(tails, 1)[0:FINAL]


def finish(packed, residual, tags, gate, weight, bias):
    return pl.pallas_call(
        finish_body,
        out_shape=(jax.ShapeDtypeStruct((TOK, WIDTH), BF),) * 4 + (jax.ShapeDtypeStruct((FINAL, WIDTH), F32),),
        in_specs=[WHOLE] * 6,
        out_specs=(WHOLE,) * 5,
        compiler_params=params(16),
        cost_estimate=cost(3),
        name="finish",
    )(packed, residual, tags, gate, weight, bias)


def sent(values, target):
    pairs = [(i, target(i)) for i in range(DEVICES)]
    return lax.ppermute(values, "dp", [(i, j) for i, j in pairs if 0 <= j < DEVICES])


def other_core(device):
    return device ^ 1


def cross(device):
    return device - PLANE + 1 if device % 2 == 0 else device + PLANE - 1


def planes_on(count):
    return lambda device: (device + count * PLANE) % DEVICES


def traded(values):
    groups = [[plane * PLANE + i for i in range(PLANE)] for plane in range(PLANES)]
    return lax.all_to_all(values, "dp", 0, 0, axis_index_groups=groups, tiled=True)


def some_blocks(values, start, rows, count):
    return lax.dynamic_slice(values, (start, rows, 0), (count, FULL, TOK))


def shards(query, key, value, residual, tags, gate, weight, bias, out_grad):
    me = lax.axis_index("dp")
    side = me % 2
    chunk, branch = pack(query, key, value, out_grad, gate, weight, tags)
    cores = [[plane * PLANE + 2 * chip + at for chip in range(HEADS)] for plane in range(PLANES) for at in range(2)]
    gathered = lax.all_gather(branch, "dp", axis=0, axis_index_groups=cores, tiled=False)
    own = traded(chunk)
    near = sent(some_blocks(own, (SIDE - EDGE) * (1 - side), 0, NEAR), other_core)
    asked = sent(some_blocks(own, SIDE * (1 - side), FULL, SIDE), other_core)
    far_other = sent(some_blocks(own, (PLANE - EDGE) * side, 0, EDGE), cross)
    far_own = sent(some_blocks(near, SIDE * side, 0, EDGE), cross)
    mixed, keep_asked, give_asked, keep, give, far = attend(own, near, asked, far_own, far_other)
    far = sent(far, cross)
    mixed_other = sent(mixed, other_core)
    got_asked = sent(give_asked, other_core)
    term, *terms = weight_term(mixed, mixed_other, gathered)
    terms = [sent(one, planes_on(away + 1)) for away, one in enumerate(terms)]
    far, _ = lax.optimization_barrier((far, term))
    keep, give = fold(keep, give, far)
    got = sent(give, other_core)
    packed = traded(join(keep_asked, got_asked, keep, got, term, *terms))
    block_out, dq, dk, dv, dw = finish(packed, residual, tags, gate, weight, bias)
    return block_out, dq, dk, dv, dw.T


def solution(mesh):
    rows = P("dp", None)
    in_specs = (rows, rows, rows, rows, P("dp"), P(), P(), P(), rows)
    out_specs = (rows,) * 4 + (P(None, "dp"),)
    return jax.shard_map(shards, mesh=mesh, in_specs=in_specs, out_specs=out_specs, check_vma=False)
```
